256 devices in a mesh: section: 2 (over y_hi), ctx: 128 (over x, y_lo, z, core).
Axes of the slice: x: 4, y: 4 (y_hi: 2, y_lo: 2; y = y_hi * 2 + y_lo), z: 8, core: 2. Of those that a mesh axis runs over, the one named last changes fastest.
Arguments:
- queries: bfloat16 [32768, 2048], P(('section', 'ctx')), parts along dimension 0, may hold values from -300 to 300
- key_rows_slotted: bfloat16 [32768, 512], P(('section', 'ctx')), parts along dimension 0, may hold values from -12 to 12
- value_rows_slotted: bfloat16 [32768, 512], P(('section', 'ctx')), parts along dimension 0, may hold values from -5 to 5
- output_gradient: bfloat16 [32768, 2048], P(('section', 'ctx')), parts along dimension 0, may hold values from -5 to 5
- slot_to_block: int32 [512], P('section'), parts along dimension 0, may hold values from 0 to 255, as said below
- doc_starts: int32 [684], P('section'), parts along dimension 0, may hold values from 0 to 16384, as said below
- block_live: int32 [512, 4], P('section'), parts along dimension 0, may hold values from 0 to 1, as said below
Outputs:
- query_grad: bfloat16 [32768, 2048], P(('section', 'ctx')), parts along dimension 0
- key_gradient: bfloat16 [32768, 512], P(('section', 'ctx')), parts along dimension 0
- value_gradient: bfloat16 [32768, 512], P(('section', 'ctx')), parts along dimension 0
The draws below stay inside these ranges and needn't reach their ends.
There are 2 independent parts, one for each index of `section`. The reference program is written for one: setup_inputs(seed, part) draws one part's arguments, and reference() takes and returns one part's arrays. A program takes and returns all parts, laid end to end along the dimension named above; each array names one. Nothing has to cross between parts.
Inputs may be any that keep to these rules, and one draw needn't show every extreme that they name: `slot_to_block`: index i of ctx holds slots 2i and 2i + 1; slot 2i holds block m and slot 2i + 1 holds block 255 - m, where m = (i - r) mod (128) for one r of each draw. `doc_starts`: Ascending, the first entry 0; every document holds at most 192 tokens; entries equal to 16384 start no document. `block_live`: entry [b, d] is 1 where block b and block b - d of the sequence hold tokens of one document, always 1 at d = 0, else 0.
All inputs are finite; a program needn't handle non-finite values.
Results may differ from the reference program's by a relative error of at most 0.005.
Values may be sent and summed in bfloat16 or wider, within the bound.
No kernel may reach another device: no remote copies, remote signals or barrier semaphores. Data moves between devices by JAX's collectives and lax.ppermute only.
A program may use at most 128 MiB of HBM per device.

```python
import math
import jax
import jax.numpy as jnp
from jax import lax

BLOCK_TOKENS = 64
QUERY_HEADS = 16
KEY_VALUE_HEADS = 4
HEAD_WIDTH = 128
MAX_BLOCK_SPAN = 3
SEQUENCE_TOKENS = 16384
BLOCK_COUNT = 256
DOCMAX = 192
NDOC = 342
N_CTX = 128


def document_starts(key):
    lengths = jax.random.randint(jax.random.fold_in(key, 201), (NDOC,), DOCMAX // 4 + 1, DOCMAX + 1)
    lengths = lengths.at[0].set(DOCMAX)
    starts = jnp.cumsum(lengths) - lengths
    return jnp.minimum(starts, SEQUENCE_TOKENS).astype(jnp.int32)


def draw_queries(key, part):
    key = jax.random.fold_in(key, 2)
    row_indices = jnp.clip(jax.random.normal(key, (SEQUENCE_TOKENS, QUERY_HEADS * HEAD_WIDTH), jnp.float32), -4.0, 4.0)
    return row_indices.astype(jnp.bfloat16)


def draw_key_rows_slotted(key, part):
    key = jax.random.fold_in(key, 1)
    row_indices = jnp.clip(jax.random.normal(key, (SEQUENCE_TOKENS, KEY_VALUE_HEADS * HEAD_WIDTH), jnp.float32), -4.0, 4.0)
    return row_indices.astype(jnp.bfloat16)


def draw_slot_to_block(key, part):
    key = jax.random.fold_in(key, 3)
    turn = jax.random.randint(key, (), 0, N_CTX)
    slots = jnp.arange(BLOCK_COUNT, dtype=jnp.int32)
    first_block = (slots // 2 - turn) % N_CTX
    return jnp.where(slots % 2 == 0, first_block, BLOCK_COUNT - 1 - first_block).astype(jnp.int32)


def draw_doc_starts(key, part):
    starts = document_starts(key)
    return starts


def draw_block_live(key, part):
    starts = document_starts(key)
    positions = jnp.arange(SEQUENCE_TOKENS, dtype=jnp.int32)
    docs = (jnp.searchsorted(starts, positions, side='right') - 1).astype(jnp.int32)
    first_doc = docs[::BLOCK_TOKENS]
    last_doc = docs[BLOCK_TOKENS - 1::BLOCK_TOKENS]
    block_ids = jnp.arange(BLOCK_COUNT, dtype=jnp.int32)[:, None]
    distance = jnp.arange(MAX_BLOCK_SPAN + 1, dtype=jnp.int32)[None, :]
    source = block_ids - distance
    shared = first_doc[block_ids] == last_doc[jnp.clip(source, 0, BLOCK_COUNT - 1)]
    live = (distance == 0) | (source >= 0) & shared
    return live.astype(jnp.int32)


def shard_levels(stream_key, extent, pieces, least, high):
    level = 1.0
    for position, blocks in pieces:
        draws = jax.random.uniform(jax.random.fold_in(jax.random.fold_in(stream_key, 6), position), (blocks,), jnp.float32, least / len(pieces), high / len(pieces))
        level = level * jnp.repeat(jnp.exp(draws), extent[position] // blocks).reshape((-1,) + (1,) * (len(extent) - 1 - position))
    return level


def bell_draw(key, shape, deviation, bound, cuts=(), kind=jnp.bfloat16):
    array = deviation * jax.random.normal(key, shape, jnp.float32)
    if cuts:
        array = array * shard_levels(key, shape, cuts, -0.22, 0.18)
    return jnp.clip(array, -bound, bound).astype(kind)


def setup_inputs(seed: int = 0, part: int = 0) -> dict:
    key_of = jax.random.split(jax.random.key(seed), 8)
    part_keys = jax.random.split(jax.random.fold_in(key_of[7], part), 8)
    return {
        "queries": draw_queries(jax.random.fold_in(jax.random.fold_in(key_of[7], part), 71), part),
        "key_rows_slotted": draw_key_rows_slotted(jax.random.fold_in(jax.random.fold_in(key_of[7], part), 71), part),
        "value_rows_slotted": bell_draw(part_keys[2], (SEQUENCE_TOKENS, KEY_VALUE_HEADS * HEAD_WIDTH), 1.0, 5.0, ((0, 128),)),
        "output_gradient": bell_draw(part_keys[3], (SEQUENCE_TOKENS, QUERY_HEADS * HEAD_WIDTH), 1.0, 5.0, ((0, 128),)),
        "slot_to_block": draw_slot_to_block(jax.random.fold_in(jax.random.fold_in(key_of[7], part), 71), part),
        "doc_starts": draw_doc_starts(jax.random.fold_in(jax.random.fold_in(key_of[7], part), 71), part),
        "block_live": draw_block_live(jax.random.fold_in(jax.random.fold_in(key_of[7], part), 71), part),
    }


LOWEST_VALUE = -1e+30

def doc_index(doc_starts, positions):
    return lax.optimization_barrier(jnp.sum((doc_starts[None, :] <= positions[:, None]).astype(jnp.int32), axis=1)).astype(jnp.int32) - 1

def reference(queries, key_rows_slotted, value_rows_slotted, output_gradient, slot_to_block, doc_starts, block_live):
    group_width = QUERY_HEADS // KEY_VALUE_HEADS
    score_scale = 1.0 / math.sqrt(HEAD_WIDTH)
    inverse_order = jnp.zeros((BLOCK_COUNT,), jnp.int32).at[slot_to_block].set(jnp.arange(BLOCK_COUNT, dtype=jnp.int32))
    blocks_of_queries = queries.reshape(BLOCK_COUNT, BLOCK_TOKENS, KEY_VALUE_HEADS, group_width, HEAD_WIDTH)[inverse_order]
    gradient_blocks = output_gradient.reshape(BLOCK_COUNT, BLOCK_TOKENS, KEY_VALUE_HEADS, group_width, HEAD_WIDTH)[inverse_order]
    padding_rows = jnp.zeros((MAX_BLOCK_SPAN, BLOCK_TOKENS, KEY_VALUE_HEADS, HEAD_WIDTH), key_rows_slotted.dtype)
    blocks_of_keys = jnp.concatenate([padding_rows, key_rows_slotted.reshape(BLOCK_COUNT, BLOCK_TOKENS, KEY_VALUE_HEADS, HEAD_WIDTH)[inverse_order]], axis=0)
    blocks_of_values = jnp.concatenate([padding_rows, value_rows_slotted.reshape(BLOCK_COUNT, BLOCK_TOKENS, KEY_VALUE_HEADS, HEAD_WIDTH)[inverse_order]], axis=0)
    span_rows = (MAX_BLOCK_SPAN + 1) * BLOCK_TOKENS
    zeroed_sums = jnp.zeros(((BLOCK_COUNT + MAX_BLOCK_SPAN) * BLOCK_TOKENS, KEY_VALUE_HEADS, HEAD_WIDTH), jnp.float32)

    def one_block(carried, block_number):
        key_accumulated, value_accumulated = carried
        query_block = lax.dynamic_index_in_dim(blocks_of_queries, block_number, 0, keepdims=False).astype(jnp.float32)
        grad_block = lax.dynamic_index_in_dim(gradient_blocks, block_number, 0, keepdims=False).astype(jnp.float32)
        key_span_rows = lax.dynamic_slice_in_dim(blocks_of_keys, block_number, MAX_BLOCK_SPAN + 1, 0).reshape(span_rows, KEY_VALUE_HEADS, HEAD_WIDTH).astype(jnp.float32)
        value_span_rows = lax.dynamic_slice_in_dim(blocks_of_values, block_number, MAX_BLOCK_SPAN + 1, 0).reshape(span_rows, KEY_VALUE_HEADS, HEAD_WIDTH).astype(jnp.float32)
        query_pos = block_number * BLOCK_TOKENS + jnp.arange(BLOCK_TOKENS, dtype=jnp.int32)
        key_pos = (block_number - MAX_BLOCK_SPAN) * BLOCK_TOKENS + jnp.arange(span_rows, dtype=jnp.int32)
        distance = MAX_BLOCK_SPAN - jnp.arange(span_rows, dtype=jnp.int32) // BLOCK_TOKENS
        live_row = lax.dynamic_index_in_dim(block_live, block_number, 0, keepdims=False)
        listed = live_row[distance]
        same_doc = doc_index(doc_starts, query_pos)[:, None] == doc_index(doc_starts, jnp.maximum(key_pos, 0))[None, :]
        allowed = (key_pos[None, :] <= query_pos[:, None]) & (key_pos[None, :] >= 0) & same_doc & (listed[None, :] == 1)
        scores = jnp.einsum('qgjd,kgd->gjqk', query_block, key_span_rows) * score_scale
        scores = jnp.where(allowed, scores, LOWEST_VALUE)
        top_score = lax.optimization_barrier(jnp.max(scores, axis=-1))
        weights = jnp.where(allowed, jnp.exp(scores - top_score[..., None]), 0.0)
        total = lax.optimization_barrier(jnp.sum(weights, axis=-1))
        log_total = top_score + jnp.log(total)
        grad_scores = jnp.einsum('qgjd,kgd->gjqk', grad_block, value_span_rows)
        probs = jnp.where(allowed, jnp.exp(scores - log_total[..., None]), 0.0)
        grad_offset = lax.optimization_barrier(jnp.sum(probs * grad_scores, axis=-1))
        probs_low = lax.optimization_barrier(probs.astype(jnp.bfloat16)).astype(jnp.float32)
        value_add = jnp.einsum('gjqk,qgjd->kgd', probs_low, grad_block)
        score_grads = probs * (grad_scores - grad_offset[..., None])
        score_low = lax.optimization_barrier(score_grads.astype(jnp.bfloat16)).astype(jnp.float32)
        query_grad = (jnp.einsum('gjqk,kgd->qgjd', score_low, key_span_rows) * score_scale).astype(jnp.bfloat16)
        key_add = jnp.einsum('gjqk,qgjd->kgd', score_low, query_block) * score_scale
        start = block_number * BLOCK_TOKENS
        key_accumulated = lax.dynamic_update_slice_in_dim(key_accumulated, lax.dynamic_slice_in_dim(key_accumulated, start, span_rows, 0) + key_add, start, 0)
        value_accumulated = lax.dynamic_update_slice_in_dim(value_accumulated, lax.dynamic_slice_in_dim(value_accumulated, start, span_rows, 0) + value_add, start, 0)
        return ((key_accumulated, value_accumulated), query_grad)
    (key_accumulated, value_accumulated), query_parts = lax.scan(one_block, (zeroed_sums, zeroed_sums), jnp.arange(BLOCK_COUNT, dtype=jnp.int32))
    key_gradient = key_accumulated[MAX_BLOCK_SPAN * BLOCK_TOKENS:].reshape(BLOCK_COUNT, BLOCK_TOKENS, KEY_VALUE_HEADS * HEAD_WIDTH)[slot_to_block].reshape(SEQUENCE_TOKENS, KEY_VALUE_HEADS * HEAD_WIDTH).astype(jnp.bfloat16)
    value_gradient = value_accumulated[MAX_BLOCK_SPAN * BLOCK_TOKENS:].reshape(BLOCK_COUNT, BLOCK_TOKENS, KEY_VALUE_HEADS * HEAD_WIDTH)[slot_to_block].reshape(SEQUENCE_TOKENS, KEY_VALUE_HEADS * HEAD_WIDTH).astype(jnp.bfloat16)
    query_grad = query_parts.reshape(BLOCK_COUNT, BLOCK_TOKENS, QUERY_HEADS * HEAD_WIDTH)[slot_to_block].reshape(SEQUENCE_TOKENS, QUERY_HEADS * HEAD_WIDTH)
    return (query_grad, key_gradient, value_gradient)
```

```python
import functools
import math

import jax
import jax.numpy as jnp
from jax import lax
from jax.experimental import pallas as pl
from jax.experimental.pallas import tpu as pltpu
from jax.sharding import PartitionSpec as P

QUERY_HEADS = 16
KEY_VALUE_HEADS = 4
GROUP = QUERY_HEADS // KEY_VALUE_HEADS
HEAD_WIDTH = 128
ROWS = 64
KV = KEY_VALUE_HEADS * HEAD_WIDTH
WIDE = QUERY_HEADS * HEAD_WIDTH
REACH = 3
SPAN = (REACH + 1) * ROWS
SCALE = 1.0 / math.sqrt(HEAD_WIDTH)
EXP2_SCALE = SCALE * math.log2(math.e)
MASKED = -1e30
FAR = 1 << 30
ENTRIES = 9
VMEM_LIMIT = 48 * 1024 * 1024

TABLE_A, TABLE_B, TABLE_C = 4, 6, 8


def send(array, even_by, odd_by):
    count = lax.axis_size("ctx")
    pairs = [(i, (i + (odd_by if i % 2 else even_by)) % count) for i in range(count)]
    return lax.ppermute(array, "ctx", pairs)


def fold_flags(chip_base, slots, live):
    half = slots.shape[0] // 2
    middle_even = slots[chip_base] == half - 1
    middle_odd = slots[chip_base + 2] == half - 1
    far_middle = jnp.logical_and(middle_odd, live[half * (REACH + 1) + REACH] == 1)
    return middle_even, far_middle


def attention_kernel(
    place,
    slots,
    live,
    row_start,
    q_own,
    q_sib,
    g_own,
    g_sib,
    kv_own,
    kv_sib,
    kv_a,
    kv_b,
    kv_c,
    dq_first,
    dq_rest,
    out_own,
    out_sib,
    out_a,
    out_b,
    out_c,
    table,
    total,
    q_work,
    g_work,
    dq,
    bias,
):
    me = place[0]
    count = slots.shape[0] // 2
    parity = lax.rem(me, 2)
    is_odd = parity == 1
    chip_base = 2 * (me - parity)
    middle_even, far_middle = fold_flags(chip_base, slots, live)

    own_at = pl.multiple_of(parity * 128, 128)
    sib_at = pl.multiple_of((1 - parity) * 128, 128)
    table[pl.ds(own_at, 128), :] = kv_own[...]
    table[pl.ds(sib_at, 128), :] = kv_sib[...]
    table[TABLE_A * ROWS : TABLE_B * ROWS, :] = kv_a[...]
    table[TABLE_B * ROWS : TABLE_C * ROWS, :] = kv_b[...]
    table[TABLE_C * ROWS :, :] = kv_c[...]
    total[...] = jnp.zeros_like(total)

    toward = jnp.where(is_odd, 1, -1)
    near_a = lax.rem(me + 2 * toward + count, count)
    near_b = lax.rem(me + toward + count, count)
    far = lax.rem(me + 3 * toward + count, count)
    entry_ids = [slots[chip_base + e] for e in range(4)]
    entry_ids += [slots[2 * near_a], slots[2 * near_a + 1]]
    entry_ids += [slots[2 * near_b], slots[2 * near_b + 1]]
    entry_ids += [slots[2 * far + parity]]

    own_row = pl.multiple_of(parity * ROWS, ROWS)
    other_row = pl.multiple_of((1 - parity) * ROWS, ROWS)
    q_work[0] = q_own[pl.ds(own_row, ROWS), :]
    g_work[0] = g_own[pl.ds(own_row, ROWS), :]

    @pl.when(middle_even)
    def _():
        q_work[1] = q_own[pl.ds(other_row, ROWS), :]
        g_work[1] = g_own[pl.ds(other_row, ROWS), :]

    @pl.when(jnp.logical_not(middle_even))
    def _():
        q_work[1] = q_sib[pl.ds(own_row, ROWS), :]
        g_work[1] = g_sib[pl.ds(own_row, ROWS), :]

    @pl.when(far_middle)
    def _():
        q_work[2] = q_sib[ROWS:, :]
        g_work[2] = g_sib[ROWS:, :]

    first = jnp.where(jnp.logical_and(far_middle, is_odd), 1, 0)
    last = jnp.where(jnp.logical_and(far_middle, jnp.logical_not(is_odd)), 3, 2)

    own_entry = 3 * parity
    other_entry = jnp.where(middle_even, 1 + parity, jnp.where(is_odd, 1, 2))

    def work_item(item, carry):
        entry = jnp.where(item == 0, own_entry, jnp.where(item == 1, other_entry, 3))
        query_id = slots[chip_base + entry]
        indices = []
        key_base = []
        for distance in range(REACH + 1):
            key_id = query_id - distance
            is_live = jnp.logical_and(
                key_id >= 0, live[query_id * (REACH + 1) + distance] == 1
            )
            index = jnp.int32(0)
            found = jnp.bool_(False)
            for e in range(ENTRIES):
                match = entry_ids[e] == key_id
                index = jnp.where(match, e, index)
                found = jnp.logical_or(found, match)
            ok = jnp.logical_and(is_live, found)
            indices.append(pl.multiple_of(jnp.where(ok, index, 0) * ROWS, ROWS))
            key_base.append(jnp.where(ok, key_id * ROWS, FAR))
        lane = lax.broadcasted_iota(jnp.int32, (1, GROUP * ROWS), 1)
        query_pos = query_id * ROWS + lax.rem(lane, ROWS)
        query_start = row_start[pl.ds(entry, 1), :]
        sub = lax.broadcasted_iota(jnp.int32, (ROWS, GROUP * ROWS), 0)
        for distance in range(REACH + 1):
            key_pos = sub + key_base[distance]
            allowed = jnp.logical_and(key_pos <= query_pos, key_pos >= query_start)
            bias[distance * ROWS : (distance + 1) * ROWS, :] = jnp.where(
                allowed, 0.0, MASKED
            )
        for g in range(KEY_VALUE_HEADS):
            kcols = slice(g * HEAD_WIDTH, (g + 1) * HEAD_WIDTH)
            vcols = slice(KV + g * HEAD_WIDTH, KV + (g + 1) * HEAD_WIDTH)
            heads = [
                slice((GROUP * g + j) * HEAD_WIDTH, (GROUP * g + j + 1) * HEAD_WIDTH)
                for j in range(GROUP)
            ]
            keys = jnp.concatenate([table[pl.ds(i, ROWS), kcols] for i in indices], 0)
            values = jnp.concatenate([table[pl.ds(i, ROWS), vcols] for i in indices], 0)
            q = jnp.concatenate([q_work[item, :, h] for h in heads], 0)
            grad = jnp.concatenate([g_work[item, :, h] for h in heads], 0)
            nt = (((1,), (1,)), ((), ()))
            raw = lax.dot_general(keys, q, nt, preferred_element_type=jnp.float32)
            raw = raw + bias[...]
            top = jnp.max(raw, axis=0, keepdims=True)
            weights = jnp.exp2((raw - top) * EXP2_SCALE)
            probs = weights * (1.0 / jnp.sum(weights, axis=0, keepdims=True))
            grad_scores = lax.dot_general(
                values, grad, nt, preferred_element_type=jnp.float32
            )
            offset = jnp.sum(probs * grad_scores, axis=0, keepdims=True)
            score_low = (probs * (grad_scores - offset)).astype(jnp.bfloat16)
            value_add = jnp.dot(
                probs.astype(jnp.bfloat16), grad, preferred_element_type=jnp.float32
            )
            key_add = jnp.dot(score_low, q, preferred_element_type=jnp.float32)
            query_add = lax.dot_general(
                score_low,
                keys,
                (((0,), (0,)), ((), ())),
                preferred_element_type=jnp.float32,
            )
            query_add = (query_add * SCALE).astype(jnp.bfloat16)
            for j, h in enumerate(heads):
                dq[item, :, h] = query_add[j * ROWS : (j + 1) * ROWS]
            for distance in range(REACH + 1):
                part = slice(distance * ROWS, (distance + 1) * ROWS)
                at = pl.ds(indices[distance], ROWS)
                total[at, kcols] += key_add[part] * SCALE
                total[at, vcols] += value_add[part]
        return carry

    lax.fori_loop(first, last, work_item, 0)

    dq_first[...] = dq[0]
    dq_rest[...] = dq[1:]
    out_own[...] = total[pl.ds(own_at, 128), :]
    out_sib[...] = total[pl.ds(sib_at, 128), :].astype(jnp.bfloat16)
    out_a[...] = total[TABLE_A * ROWS : TABLE_B * ROWS, :].astype(jnp.bfloat16)
    out_b[...] = total[TABLE_B * ROWS : TABLE_C * ROWS, :].astype(jnp.bfloat16)
    out_c[...] = total[TABLE_C * ROWS :, :].astype(jnp.bfloat16)


def query_grad_kernel(place, slots, live, first, rest, theirs, out):
    me = place[0]
    parity = lax.rem(me, 2)
    is_odd = parity == 1
    middle_even, far_middle = fold_flags(2 * (me - parity), slots, live)
    own_row = pl.multiple_of(parity * ROWS, ROWS)
    other_row = pl.multiple_of((1 - parity) * ROWS, ROWS)
    moved = jnp.logical_and(far_middle, is_odd)

    @pl.when(moved)
    def _():
        out[pl.ds(own_row, ROWS), :] = theirs[1]

    @pl.when(jnp.logical_not(moved))
    def _():
        out[pl.ds(own_row, ROWS), :] = first[...]

    @pl.when(middle_even)
    def _():
        out[pl.ds(other_row, ROWS), :] = rest[0]

    @pl.when(jnp.logical_not(middle_even))
    def _():
        out[pl.ds(other_row, ROWS), :] = theirs[0]


def sum_kernel(place, own, sib, back_a, back_b, back_c, key_out, value_out, acc):
    parity = lax.rem(place[0], 2)
    acc[...] = (
        own[...]
        + sib[...].astype(jnp.float32)
        + back_a[...].astype(jnp.float32)
        + back_b[...].astype(jnp.float32)
    )
    at = pl.ds(pl.multiple_of((1 - parity) * ROWS, ROWS), ROWS)
    acc[at, :] += back_c[...].astype(jnp.float32)
    key_out[...] = acc[:, :KV].astype(jnp.bfloat16)
    value_out[...] = acc[:, KV:].astype(jnp.bfloat16)


def vmem(count):
    return [pl.BlockSpec(memory_space=pltpu.VMEM)] * count


def smem(count):
    return [pl.BlockSpec(memory_space=pltpu.SMEM)] * count


def shards(
    queries,
    key_rows_slotted,
    value_rows_slotted,
    output_gradient,
    slot_to_block,
    doc_starts,
    block_live,
):
    me = lax.axis_index("ctx")
    parity = me % 2
    place = me.astype(jnp.int32).reshape(1)
    live = block_live.reshape(-1)
    params = pltpu.CompilerParams(vmem_limit_bytes=VMEM_LIMIT)

    kv = jnp.concatenate([key_rows_slotted, value_rows_slotted], axis=1)
    kv_far = lax.dynamic_slice_in_dim(kv, (1 - parity) * ROWS, ROWS, 0)
    kv_c = send(kv_far, -3, 3)
    kv_a = send(kv, 2, -2)
    kv_b = send(kv, -1, 1)
    kv_sib = send(kv, 1, -1)
    q_sib = send(queries, 1, -1)
    g_sib = send(output_gradient, 1, -1)

    ids = lax.dynamic_slice_in_dim(slot_to_block, 2 * (me - parity), 4, 0)
    positions = ids[:, None] * ROWS + lax.iota(jnp.int32, ROWS)[None, :]
    starts = jnp.max(
        jnp.where(
            doc_starts[None, None, :] <= positions[:, :, None],
            doc_starts[None, None, :],
            0,
        ),
        axis=2,
    )
    row_start = jnp.tile(starts, (1, GROUP))

    bf16 = functools.partial(jax.ShapeDtypeStruct, dtype=jnp.bfloat16)
    dq_first, dq_rest, own, sib, out_a, out_b, out_c = pl.pallas_call(
        attention_kernel,
        out_shape=(
            bf16((ROWS, WIDE)),
            bf16((2, ROWS, WIDE)),
            jax.ShapeDtypeStruct((2 * ROWS, 2 * KV), jnp.float32),
            bf16((2 * ROWS, 2 * KV)),
            bf16((2 * ROWS, 2 * KV)),
            bf16((2 * ROWS, 2 * KV)),
            bf16((ROWS, 2 * KV)),
        ),
        in_specs=smem(3) + vmem(10),
        out_specs=tuple(vmem(7)),
        scratch_shapes=[
            pltpu.VMEM((ENTRIES * ROWS, 2 * KV), jnp.bfloat16),
            pltpu.VMEM((ENTRIES * ROWS, 2 * KV), jnp.float32),
            pltpu.VMEM((3, ROWS, WIDE), jnp.bfloat16),
            pltpu.VMEM((3, ROWS, WIDE), jnp.bfloat16),
            pltpu.VMEM((3, ROWS, WIDE), jnp.bfloat16),
            pltpu.VMEM((SPAN, GROUP * ROWS), jnp.float32),
        ],
        compiler_params=params,
        name="attention_items",
    )(
        place,
        slot_to_block,
        live,
        row_start,
        queries,
        q_sib,
        output_gradient,
        g_sib,
        kv,
        kv_sib,
        kv_a,
        kv_b,
        kv_c,
    )

    back_c = send(out_c, -3, 3)
    back_a = send(out_a, -2, 2)
    back_b = send(out_b, -1, 1)
    back_sib = send(sib, 1, -1)
    dq_sib = send(dq_rest, 1, -1)

    query_grad = pl.pallas_call(
        query_grad_kernel,
        out_shape=bf16((2 * ROWS, WIDE)),
        in_specs=smem(3) + vmem(3),
        out_specs=vmem(1)[0],
        compiler_params=params,
        name="query_gradient_rows",
    )(place, slot_to_block, live, dq_first, dq_rest, dq_sib)

    key_gradient, value_gradient = pl.pallas_call(
        sum_kernel,
        out_shape=(bf16((2 * ROWS, KV)), bf16((2 * ROWS, KV))),
        in_specs=smem(1) + vmem(5),
        out_specs=tuple(vmem(2)),
        scratch_shapes=[pltpu.VMEM((2 * ROWS, 2 * KV), jnp.float32)],
        compiler_params=params,
        name="key_value_gradient_sum",
    )(place, own, back_sib, back_a, back_b, back_c)
    return query_grad, key_gradient, value_gradient


def solution(mesh):
    rows = P(("section", "ctx"), None)
    return jax.shard_map(
        shards,
        mesh=mesh,
        in_specs=(rows, rows, rows, rows, P("section"), P("section"), P("section", None)),
        out_specs=(rows, rows, rows),
        check_vma=False,
    )
```

```python
import functools
import math

import jax
import jax.numpy as jnp
from jax import lax
from jax.experimental import pallas as pl
from jax.experimental.pallas import tpu as pltpu
from jax.sharding import PartitionSpec as P

QUERY_HEADS = 16
KEY_VALUE_HEADS = 4
GROUP = QUERY_HEADS // KEY_VALUE_HEADS
HEAD_WIDTH = 128
ROWS = 64
KV = KEY_VALUE_HEADS * HEAD_WIDTH
WIDE = QUERY_HEADS * HEAD_WIDTH
REACH = 3
SPAN = (REACH + 1) * ROWS
SCALE = 1.0 / math.sqrt(HEAD_WIDTH)
EXP2_SCALE = SCALE * math.log2(math.e)
MASKED = -1e30
FAR = 1 << 30
ENTRIES = 9
VMEM_LIMIT = 24 * 1024 * 1024

TABLE_A, TABLE_B, TABLE_C = 4, 6, 8


def send(array, even_by, odd_by):
    count = lax.axis_size("ctx")
    pairs = [(i, (i + (odd_by if i % 2 else even_by)) % count) for i in range(count)]
    return lax.ppermute(array, "ctx", pairs)


def fold_flags(chip_base, slots, live):
    half = slots.shape[0] // 2
    middle_even = slots[chip_base] == half - 1
    middle_odd = slots[chip_base + 2] == half - 1
    far_middle = jnp.logical_and(middle_odd, live[half * (REACH + 1) + REACH] == 1)
    return middle_even, far_middle


def attention_kernel(
    place,
    slots,
    live,
    row_start,
    q_own,
    q_sib,
    g_own,
    g_sib,
    kv_own,
    kv_sib,
    kv_a,
    kv_b,
    kv_c,
    dq_first,
    dq_rest,
    out_own,
    out_sib,
    out_a,
    out_b,
    out_c,
    table,
    total,
    q_work,
    g_work,
    dq,
    bias,
):
    me = place[0]
    count = slots.shape[0] // 2
    parity = lax.rem(me, 2)
    is_odd = parity == 1
    chip_base = 2 * (me - parity)
    middle_even, far_middle = fold_flags(chip_base, slots, live)

    own_at = pl.multiple_of(parity * 128, 128)
    sib_at = pl.multiple_of((1 - parity) * 128, 128)
    table[pl.ds(own_at, 128), :] = kv_own[...]
    table[pl.ds(sib_at, 128), :] = kv_sib[...]
    table[TABLE_A * ROWS : TABLE_B * ROWS, :] = kv_a[...]
    table[TABLE_B * ROWS : TABLE_C * ROWS, :] = kv_b[...]
    table[TABLE_C * ROWS :, :] = kv_c[...]
    total[...] = jnp.zeros_like(total)

    toward = jnp.where(is_odd, 1, -1)
    near_a = lax.rem(me + 2 * toward + count, count)
    near_b = lax.rem(me + toward + count, count)
    far = lax.rem(me + 3 * toward + count, count)
    entry_ids = [slots[chip_base + e] for e in range(4)]
    entry_ids += [slots[2 * near_a], slots[2 * near_a + 1]]
    entry_ids += [slots[2 * near_b], slots[2 * near_b + 1]]
    entry_ids += [slots[2 * far + parity]]

    own_row = pl.multiple_of(parity * ROWS, ROWS)
    other_row = pl.multiple_of((1 - parity) * ROWS, ROWS)
    q_work[0] = q_own[pl.ds(own_row, ROWS), :]
    g_work[0] = g_own[pl.ds(own_row, ROWS), :]

    @pl.when(middle_even)
    def _():
        q_work[1] = q_own[pl.ds(other_row, ROWS), :]
        g_work[1] = g_own[pl.ds(other_row, ROWS), :]

    @pl.when(jnp.logical_not(middle_even))
    def _():
        q_work[1] = q_sib[pl.ds(own_row, ROWS), :]
        g_work[1] = g_sib[pl.ds(own_row, ROWS), :]

    @pl.when(far_middle)
    def _():
        q_work[2] = q_sib[ROWS:, :]
        g_work[2] = g_sib[ROWS:, :]

    first = jnp.where(jnp.logical_and(far_middle, is_odd), 1, 0)
    last = jnp.where(jnp.logical_and(far_middle, jnp.logical_not(is_odd)), 3, 2)

    own_entry = 3 * parity
    other_entry = jnp.where(middle_even, 1 + parity, jnp.where(is_odd, 1, 2))

    def work_item(item, carry):
        entry = jnp.where(item == 0, own_entry, jnp.where(item == 1, other_entry, 3))
        query_id = slots[chip_base + entry]
        indices = []
        key_base = []
        for distance in range(REACH + 1):
            key_id = query_id - distance
            is_live = jnp.logical_and(
                key_id >= 0, live[query_id * (REACH + 1) + distance] == 1
            )
            index = jnp.int32(0)
            found = jnp.bool_(False)
            for e in range(ENTRIES):
                match = entry_ids[e] == key_id
                index = jnp.where(match, e, index)
                found = jnp.logical_or(found, match)
            ok = jnp.logical_and(is_live, found)
            indices.append(pl.multiple_of(jnp.where(ok, index, 0) * ROWS, ROWS))
            key_base.append(jnp.where(ok, key_id * ROWS, FAR))
        lane = lax.broadcasted_iota(jnp.int32, (1, GROUP * ROWS), 1)
        query_pos = query_id * ROWS + lax.rem(lane, ROWS)
        query_start = row_start[pl.ds(entry, 1), :]
        sub = lax.broadcasted_iota(jnp.int32, (ROWS, GROUP * ROWS), 0)
        for distance in range(REACH + 1):
            key_pos = sub + key_base[distance]
            allowed = jnp.logical_and(key_pos <= query_pos, key_pos >= query_start)
            bias[distance * ROWS : (distance + 1) * ROWS, :] = jnp.where(
                allowed, 0.0, MASKED
            )
        for g in range(KEY_VALUE_HEADS):
            kcols = slice(g * HEAD_WIDTH, (g + 1) * HEAD_WIDTH)
            vcols = slice(KV + g * HEAD_WIDTH, KV + (g + 1) * HEAD_WIDTH)
            heads = [
                slice((GROUP * g + j) * HEAD_WIDTH, (GROUP * g + j + 1) * HEAD_WIDTH)
                for j in range(GROUP)
            ]
            keys = jnp.concatenate([table[pl.ds(i, ROWS), kcols] for i in indices], 0)
            values = jnp.concatenate([table[pl.ds(i, ROWS), vcols] for i in indices], 0)
            q = jnp.concatenate([q_work[item, :, h] for h in heads], 0)
            grad = jnp.concatenate([g_work[item, :, h] for h in heads], 0)
            nt = (((1,), (1,)), ((), ()))
            raw = lax.dot_general(keys, q, nt, preferred_element_type=jnp.float32)
            raw = raw + bias[...]
            top = jnp.max(raw, axis=0, keepdims=True)
            weights = jnp.exp2((raw - top) * EXP2_SCALE)
            probs = weights * (1.0 / jnp.sum(weights, axis=0, keepdims=True))
            grad_scores = lax.dot_general(
                values, grad, nt, preferred_element_type=jnp.float32
            )
            offset = jnp.sum(probs * grad_scores, axis=0, keepdims=True)
            score_low = (probs * (grad_scores - offset)).astype(jnp.bfloat16)
            value_add = jnp.dot(
                probs.astype(jnp.bfloat16), grad, preferred_element_type=jnp.float32
            )
            key_add = jnp.dot(score_low, q, preferred_element_type=jnp.float32)
            query_add = lax.dot_general(
                score_low,
                keys,
                (((0,), (0,)), ((), ())),
                preferred_element_type=jnp.float32,
            )
            query_add = (query_add * SCALE).astype(jnp.bfloat16)
            for j, h in enumerate(heads):
                dq[item, :, h] = query_add[j * ROWS : (j + 1) * ROWS]
            for distance in range(REACH + 1):
                part = slice(distance * ROWS, (distance + 1) * ROWS)
                at = pl.ds(indices[distance], ROWS)
                total[at, kcols] += key_add[part] * SCALE
                total[at, vcols] += value_add[part]
        return carry

    lax.fori_loop(first, last, work_item, 0)

    dq_first[...] = dq[0]
    dq_rest[...] = dq[1:]
    out_own[...] = total[pl.ds(own_at, 128), :]
    out_sib[...] = total[pl.ds(sib_at, 128), :].astype(jnp.bfloat16)
    out_a[...] = total[TABLE_A * ROWS : TABLE_B * ROWS, :].astype(jnp.bfloat16)
    out_b[...] = total[TABLE_B * ROWS : TABLE_C * ROWS, :].astype(jnp.bfloat16)
    out_c[...] = total[TABLE_C * ROWS :, :].astype(jnp.bfloat16)


def pack_kernel(place, keys, values, both, far, sems):
    at = pl.ds(pl.multiple_of((1 - lax.rem(place[0], 2)) * ROWS, ROWS), ROWS)
    copies = [
        pltpu.make_async_copy(source, target, sems.at[n])
        for n, (source, target) in enumerate(
            [
                (keys.at[at, :], far.at[:, pl.ds(0, KV)]),
                (values.at[at, :], far.at[:, pl.ds(KV, KV)]),
                (keys, both.at[:, pl.ds(0, KV)]),
                (values, both.at[:, pl.ds(KV, KV)]),
            ]
        )
    ]
    for copy in copies:
        copy.start()
    for copy in copies:
        copy.wait()


def prefetch_kernel(queries, grads, q_own, g_own, sems):
    copies = [
        pltpu.make_async_copy(queries, q_own, sems.at[0]),
        pltpu.make_async_copy(grads, g_own, sems.at[1]),
    ]
    for copy in copies:
        copy.start()
    for copy in copies:
        copy.wait()


def early_kernel(place, slots, live, first, rest, theirs, own, back_c, out, acc):
    me = place[0]
    parity = lax.rem(me, 2)
    is_odd = parity == 1
    middle_even, far_middle = fold_flags(2 * (me - parity), slots, live)
    own_row = pl.multiple_of(parity * ROWS, ROWS)
    other_row = pl.multiple_of((1 - parity) * ROWS, ROWS)
    moved = jnp.logical_and(far_middle, is_odd)

    @pl.when(moved)
    def _():
        out[pl.ds(own_row, ROWS), :] = theirs[1]

    @pl.when(jnp.logical_not(moved))
    def _():
        out[pl.ds(own_row, ROWS), :] = first[...]

    @pl.when(middle_even)
    def _():
        out[pl.ds(other_row, ROWS), :] = rest[0]

    @pl.when(jnp.logical_not(middle_even))
    def _():
        out[pl.ds(other_row, ROWS), :] = theirs[0]

    acc[pl.ds(own_row, ROWS), :] = own[pl.ds(own_row, ROWS), :]
    acc[pl.ds(other_row, ROWS), :] = own[pl.ds(other_row, ROWS), :] + back_c[
        ...
    ].astype(jnp.float32)


def sum_kernel(own, sib, back_a, back_b, key_out, value_out):
    def total(columns):
        return (
            own[:, columns]
            + sib[:, columns].astype(jnp.float32)
            + back_a[:, columns].astype(jnp.float32)
            + back_b[:, columns].astype(jnp.float32)
        ).astype(jnp.bfloat16)

    key_out[...] = total(slice(0, KV))
    value_out[...] = total(slice(KV, 2 * KV))


def vmem(count):
    return [pl.BlockSpec(memory_space=pltpu.VMEM)] * count


def in_hbm(array):
    return pltpu.with_memory_space_constraint(array, pltpu.HBM)


def hbm(count):
    return [pl.BlockSpec(memory_space=pltpu.HBM)] * count


def smem(count):
    return [pl.BlockSpec(memory_space=pltpu.SMEM)] * count


def shards(
    queries,
    key_rows_slotted,
    value_rows_slotted,
    output_gradient,
    slot_to_block,
    doc_starts,
    block_live,
):
    me = lax.axis_index("ctx")
    place = me.astype(jnp.int32).reshape(1)
    live = block_live.reshape(-1)
    params = pltpu.CompilerParams(vmem_limit_bytes=VMEM_LIMIT)

    bf16 = functools.partial(jax.ShapeDtypeStruct, dtype=jnp.bfloat16)
    kv, kv_far = pl.pallas_call(
        pack_kernel,
        out_shape=(bf16((2 * ROWS, 2 * KV)), bf16((ROWS, 2 * KV))),
        in_specs=smem(1) + hbm(2),
        out_specs=tuple(vmem(2)),
        scratch_shapes=[pltpu.SemaphoreType.DMA((4,))],
        compiler_params=params,
        name="key_value_pack",
    )(place, in_hbm(key_rows_slotted), in_hbm(value_rows_slotted))
    kv_c = send(kv_far, -3, 3)
    kv_a = send(kv, 2, -2)
    kv_b = send(kv, -1, 1)
    kv_sib = send(kv, 1, -1)
    q_sib = send(queries, 1, -1)
    g_sib = send(output_gradient, 1, -1)

    q_own, g_own = pl.pallas_call(
        prefetch_kernel,
        out_shape=(bf16((2 * ROWS, WIDE)), bf16((2 * ROWS, WIDE))),
        in_specs=hbm(2),
        out_specs=tuple(vmem(2)),
        scratch_shapes=[pltpu.SemaphoreType.DMA((2,))],
        compiler_params=params,
        cost_estimate=pl.CostEstimate(
            flops=0, bytes_accessed=1 << 21, transcendentals=0
        ),
        name="own_rows",
    )(in_hbm(queries), in_hbm(output_gradient))

    ids = lax.dynamic_slice_in_dim(slot_to_block, 2 * (me - me % 2), 4, 0)
    positions = ids[:, None] * ROWS + lax.iota(jnp.int32, ROWS)[None, :]
    starts = jnp.max(
        jnp.where(
            doc_starts[None, None, :] <= positions[:, :, None],
            doc_starts[None, None, :],
            0,
        ),
        axis=2,
    )
    row_start = jnp.tile(starts, (1, GROUP))

    dq_first, dq_rest, own, sib, out_a, out_b, out_c = pl.pallas_call(
        attention_kernel,
        out_shape=(
            bf16((ROWS, WIDE)),
            bf16((2, ROWS, WIDE)),
            jax.ShapeDtypeStruct((2 * ROWS, 2 * KV), jnp.float32),
            bf16((2 * ROWS, 2 * KV)),
            bf16((2 * ROWS, 2 * KV)),
            bf16((2 * ROWS, 2 * KV)),
            bf16((ROWS, 2 * KV)),
        ),
        in_specs=smem(3) + vmem(10),
        out_specs=tuple(vmem(7)),
        scratch_shapes=[
            pltpu.VMEM((ENTRIES * ROWS, 2 * KV), jnp.bfloat16),
            pltpu.VMEM((ENTRIES * ROWS, 2 * KV), jnp.float32),
            pltpu.VMEM((3, ROWS, WIDE), jnp.bfloat16),
            pltpu.VMEM((3, ROWS, WIDE), jnp.bfloat16),
            pltpu.VMEM((3, ROWS, WIDE), jnp.bfloat16),
            pltpu.VMEM((SPAN, GROUP * ROWS), jnp.float32),
        ],
        compiler_params=params,
        name="attention_items",
    )(
        place,
        slot_to_block,
        live,
        row_start,
        q_own,
        q_sib,
        g_own,
        g_sib,
        kv,
        kv_sib,
        kv_a,
        kv_b,
        kv_c,
    )

    back_c = send(out_c, -3, 3)
    back_a = send(out_a, -2, 2)
    back_b = send(out_b, -1, 1)
    back_sib = send(sib, 1, -1)
    dq_sib = send(dq_rest, 1, -1)

    query_grad, own = pl.pallas_call(
        early_kernel,
        out_shape=(
            bf16((2 * ROWS, WIDE)),
            jax.ShapeDtypeStruct((2 * ROWS, 2 * KV), jnp.float32),
        ),
        in_specs=smem(3) + vmem(5),
        out_specs=tuple(vmem(2)),
        compiler_params=params,
        cost_estimate=pl.CostEstimate(
            flops=1 << 36, bytes_accessed=1 << 22, transcendentals=0
        ),
        name="query_gradient_rows",
    )(place, slot_to_block, live, dq_first, dq_rest, dq_sib, own, back_c)

    key_gradient, value_gradient = pl.pallas_call(
        sum_kernel,
        out_shape=(bf16((2 * ROWS, KV)), bf16((2 * ROWS, KV))),
        in_specs=vmem(4),
        out_specs=tuple(vmem(2)),
        compiler_params=params,
        name="key_value_gradient_sum",
    )(own, back_sib, back_a, back_b)
    return query_grad, key_gradient, value_gradient


def solution(mesh):
    rows = P(("section", "ctx"), None)
    return jax.shard_map(
        shards,
        mesh=mesh,
        in_specs=(rows, rows, rows, rows, P("section"), P("section"), P("section", None)),
        out_specs=(rows, rows, rows),
        check_vma=False,
    )
```

```python
import functools
import math

import jax
import jax.numpy as jnp
from jax import lax
from jax.experimental import pallas as pl
from jax.experimental.pallas import tpu as pltpu
from jax.sharding import PartitionSpec as P

QUERY_HEADS = 16
KEY_VALUE_HEADS = 4
GROUP = QUERY_HEADS // KEY_VALUE_HEADS
HEAD_WIDTH = 128
ROWS = 64
KV = KEY_VALUE_HEADS * HEAD_WIDTH
WIDE = QUERY_HEADS * HEAD_WIDTH
REACH = 3
SPAN = (REACH + 1) * ROWS
SCALE = 1.0 / math.sqrt(HEAD_WIDTH)
EXP2_SCALE = SCALE * math.log2(math.e)
MASKED = -1e30
FAR = 1 << 30
ENTRIES = 9
VMEM_LIMIT = 24 * 1024 * 1024

TABLE_A, TABLE_B, TABLE_C = 4, 6, 8


def send(array, even_by, odd_by):
    count = lax.axis_size("ctx")
    pairs = [(i, (i + (odd_by if i % 2 else even_by)) % count) for i in range(count)]
    return lax.ppermute(array, "ctx", pairs)


def fold_flags(chip_base, slots, live):
    half = slots.shape[0] // 2
    middle_even = slots[chip_base] == half - 1
    middle_odd = slots[chip_base + 2] == half - 1
    far_middle = jnp.logical_and(middle_odd, live[REACH, half] == 1)
    return middle_even, far_middle


def attention_kernel(
    place,
    slots,
    live,
    row_start,
    q_own,
    q_sib,
    g_own,
    g_sib,
    kv_own,
    kv_sib,
    kv_b,
    kv_a,
    kv_c,
    dq_first,
    dq_rest,
    out_own,
    out_sib,
    out_a,
    out_b,
    out_c,
    table,
    total,
    q_work,
    g_work,
    dq,
    bias,
):
    me = place[0]
    count = slots.shape[0] // 2
    parity = lax.rem(me, 2)
    is_odd = parity == 1
    chip_base = 2 * (me - parity)
    middle_even, far_middle = fold_flags(chip_base, slots, live)

    own_at = pl.multiple_of(parity * 128, 128)
    sib_at = pl.multiple_of((1 - parity) * 128, 128)
    table[pl.ds(own_at, 128), :] = kv_own[...]
    table[pl.ds(sib_at, 128), :] = kv_sib[...]
    table[TABLE_A * ROWS : TABLE_B * ROWS, :] = kv_a[...]
    table[TABLE_B * ROWS : TABLE_C * ROWS, :] = kv_b[...]
    table[TABLE_C * ROWS :, :] = kv_c[...]
    total[...] = jnp.zeros_like(total)

    toward = jnp.where(is_odd, 1, -1)
    near_a = lax.rem(me + 2 * toward + count, count)
    near_b = lax.rem(me + toward + count, count)
    far = lax.rem(me + 3 * toward + count, count)
    entry_ids = [slots[chip_base + e] for e in range(4)]
    entry_ids += [slots[2 * near_a], slots[2 * near_a + 1]]
    entry_ids += [slots[2 * near_b], slots[2 * near_b + 1]]
    entry_ids += [slots[2 * far + parity]]

    own_row = pl.multiple_of(parity * ROWS, ROWS)
    other_row = pl.multiple_of((1 - parity) * ROWS, ROWS)
    q_work[0] = q_own[pl.ds(own_row, ROWS), :]
    g_work[0] = g_own[pl.ds(own_row, ROWS), :]

    @pl.when(middle_even)
    def _():
        q_work[1] = q_own[pl.ds(other_row, ROWS), :]
        g_work[1] = g_own[pl.ds(other_row, ROWS), :]

    @pl.when(jnp.logical_not(middle_even))
    def _():
        q_work[1] = q_sib[pl.ds(own_row, ROWS), :]
        g_work[1] = g_sib[pl.ds(own_row, ROWS), :]

    @pl.when(far_middle)
    def _():
        q_work[2] = q_sib[ROWS:, :]
        g_work[2] = g_sib[ROWS:, :]

    first = jnp.where(jnp.logical_and(far_middle, is_odd), 1, 0)
    last = jnp.where(jnp.logical_and(far_middle, jnp.logical_not(is_odd)), 3, 2)

    own_entry = 3 * parity
    other_entry = jnp.where(middle_even, 1 + parity, jnp.where(is_odd, 1, 2))

    def work_item(item, carry):
        entry = jnp.where(item == 0, own_entry, jnp.where(item == 1, other_entry, 3))
        query_id = slots[chip_base + entry]
        indices = []
        key_base = []
        for distance in range(REACH + 1):
            key_id = query_id - distance
            is_live = jnp.logical_and(
                key_id >= 0, live[distance, query_id] == 1
            )
            index = jnp.int32(0)
            found = jnp.bool_(False)
            for e in range(ENTRIES):
                match = entry_ids[e] == key_id
                index = jnp.where(match, e, index)
                found = jnp.logical_or(found, match)
            ok = jnp.logical_and(is_live, found)
            indices.append(pl.multiple_of(jnp.where(ok, index, 0) * ROWS, ROWS))
            key_base.append(jnp.where(ok, key_id * ROWS, FAR))
        lane = lax.broadcasted_iota(jnp.int32, (1, GROUP * ROWS), 1)
        query_pos = query_id * ROWS + lax.rem(lane, ROWS)
        query_start = row_start[pl.ds(entry, 1), :]
        sub = lax.broadcasted_iota(jnp.int32, (ROWS, GROUP * ROWS), 0)
        for distance in range(REACH + 1):
            key_pos = sub + key_base[distance]
            allowed = jnp.logical_and(key_pos <= query_pos, key_pos >= query_start)
            bias[distance * ROWS : (distance + 1) * ROWS, :] = jnp.where(
                allowed, 0.0, MASKED
            )
        for g in range(KEY_VALUE_HEADS):
            kcols = slice(g * HEAD_WIDTH, (g + 1) * HEAD_WIDTH)
            vcols = slice(KV + g * HEAD_WIDTH, KV + (g + 1) * HEAD_WIDTH)
            heads = [
                slice((GROUP * g + j) * HEAD_WIDTH, (GROUP * g + j + 1) * HEAD_WIDTH)
                for j in range(GROUP)
            ]
            keys = jnp.concatenate([table[pl.ds(i, ROWS), kcols] for i in indices], 0)
            values = jnp.concatenate([table[pl.ds(i, ROWS), vcols] for i in indices], 0)
            q = jnp.concatenate([q_work[item, :, h] for h in heads], 0)
            grad = jnp.concatenate([g_work[item, :, h] for h in heads], 0)
            nt = (((1,), (1,)), ((), ()))
            raw = lax.dot_general(keys, q, nt, preferred_element_type=jnp.float32)
            raw = raw + bias[...]
            top = jnp.max(raw, axis=0, keepdims=True)
            weights = jnp.exp2((raw - top) * EXP2_SCALE)
            probs = weights * (1.0 / jnp.sum(weights, axis=0, keepdims=True))
            grad_scores = lax.dot_general(
                values, grad, nt, preferred_element_type=jnp.float32
            )
            offset = jnp.sum(probs * grad_scores, axis=0, keepdims=True)
            score_low = (probs * (grad_scores - offset)).astype(jnp.bfloat16)
            value_add = jnp.dot(
                probs.astype(jnp.bfloat16), grad, preferred_element_type=jnp.float32
            )
            key_add = jnp.dot(score_low, q, preferred_element_type=jnp.float32)
            query_add = lax.dot_general(
                score_low,
                keys,
                (((0,), (0,)), ((), ())),
                preferred_element_type=jnp.float32,
            )
            query_add = (query_add * SCALE).astype(jnp.bfloat16)
            for j, h in enumerate(heads):
                dq[item, :, h] = query_add[j * ROWS : (j + 1) * ROWS]
            for distance in range(REACH + 1):
                part = slice(distance * ROWS, (distance + 1) * ROWS)
                at = pl.ds(indices[distance], ROWS)
                total[at, kcols] += key_add[part] * SCALE
                total[at, vcols] += value_add[part]
        return carry

    lax.fori_loop(first, last, work_item, 0)

    dq_first[...] = dq[0]
    dq_rest[...] = dq[1:]
    out_own[...] = total[pl.ds(own_at, 128), :]
    out_sib[...] = total[pl.ds(sib_at, 128), :].astype(jnp.bfloat16)
    out_a[...] = total[TABLE_A * ROWS : TABLE_B * ROWS, :].astype(jnp.bfloat16)
    out_b[...] = total[TABLE_B * ROWS : TABLE_C * ROWS, :].astype(jnp.bfloat16)
    out_c[...] = total[TABLE_C * ROWS :, :].astype(jnp.bfloat16)


def pack_kernel(
    place,
    slots_hbm,
    docs_hbm,
    keys,
    values,
    queries,
    grads,
    both,
    far,
    q_own,
    g_own,
    row_start,
    slots,
    docs,
    sems,
):
    parity = lax.rem(place[0], 2)
    at = pl.ds(pl.multiple_of((1 - parity) * ROWS, ROWS), ROWS)
    copies = [
        pltpu.make_async_copy(source, target, sems.at[n])
        for n, (source, target) in enumerate(
            [
                (slots_hbm, slots),
                (docs_hbm, docs),
                (keys.at[at, :], far.at[:, pl.ds(0, KV)]),
                (values.at[at, :], far.at[:, pl.ds(KV, KV)]),
                (keys, both.at[:, pl.ds(0, KV)]),
                (values, both.at[:, pl.ds(KV, KV)]),
                (queries, q_own),
                (grads, g_own),
            ]
        )
    ]
    for copy in copies:
        copy.start()
    copies[0].wait()
    copies[1].wait()
    count = docs.shape[0]
    lane = lax.rem(lax.broadcasted_iota(jnp.int32, (1, GROUP * ROWS), 1), ROWS)
    for entry in range(4):
        first = slots[2 * (place[0] - parity) + entry] * ROWS

        def halve(_, bounds):
            low, high = bounds
            middle = (low + high) // 2
            begun = docs[middle] <= first
            inside = low < high
            return (
                jnp.where(jnp.logical_and(inside, begun), middle + 1, low),
                jnp.where(jnp.logical_and(inside, jnp.logical_not(begun)), middle, high),
            )

        begun, _ = lax.fori_loop(
            0, count.bit_length(), halve, (jnp.int32(1), jnp.int32(count))
        )

        def more(state):
            index, _ = state
            start = docs[jnp.minimum(index, count - 1)]
            return jnp.logical_and(index < count, start < first + ROWS)

        def step(state):
            index, row = state
            start = docs[index]
            return index + 1, jnp.where(lane + first >= start, start, row)

        _, row = lax.while_loop(
            more, step, (begun, jnp.full((1, GROUP * ROWS), docs[begun - 1]))
        )
        row_start[pl.ds(entry, 1), :] = row
    for copy in copies[2:]:
        copy.wait()


def early_kernel(place, slots, live, first, rest, theirs, own, back_c, out, acc):
    me = place[0]
    parity = lax.rem(me, 2)
    is_odd = parity == 1
    middle_even, far_middle = fold_flags(2 * (me - parity), slots, live)
    own_row = pl.multiple_of(parity * ROWS, ROWS)
    other_row = pl.multiple_of((1 - parity) * ROWS, ROWS)
    moved = jnp.logical_and(far_middle, is_odd)

    @pl.when(moved)
    def _():
        out[pl.ds(own_row, ROWS), :] = theirs[1]

    @pl.when(jnp.logical_not(moved))
    def _():
        out[pl.ds(own_row, ROWS), :] = first[...]

    @pl.when(middle_even)
    def _():
        out[pl.ds(other_row, ROWS), :] = rest[0]

    @pl.when(jnp.logical_not(middle_even))
    def _():
        out[pl.ds(other_row, ROWS), :] = theirs[0]

    acc[pl.ds(own_row, ROWS), :] = own[pl.ds(own_row, ROWS), :]
    acc[pl.ds(other_row, ROWS), :] = own[pl.ds(other_row, ROWS), :] + back_c[
        ...
    ].astype(jnp.float32)


def sum_kernel(own, sib, back_a, back_b, key_out, value_out):
    def total(columns):
        return (
            own[:, columns]
            + sib[:, columns].astype(jnp.float32)
            + back_a[:, columns].astype(jnp.float32)
            + back_b[:, columns].astype(jnp.float32)
        ).astype(jnp.bfloat16)

    key_out[...] = total(slice(0, KV))
    value_out[...] = total(slice(KV, 2 * KV))


def vmem(count):
    return [pl.BlockSpec(memory_space=pltpu.VMEM)] * count


def in_hbm(array):
    return pltpu.with_memory_space_constraint(array, pltpu.HBM)


def hbm(count):
    return [pl.BlockSpec(memory_space=pltpu.HBM)] * count


def smem(count):
    return [pl.BlockSpec(memory_space=pltpu.SMEM)] * count


def shards(
    queries,
    key_rows_slotted,
    value_rows_slotted,
    output_gradient,
    slot_to_block,
    doc_starts,
    block_live,
):
    me = lax.axis_index("ctx")
    place = me.astype(jnp.int32).reshape(1)
    live = block_live.T
    params = pltpu.CompilerParams(vmem_limit_bytes=VMEM_LIMIT)

    bf16 = functools.partial(jax.ShapeDtypeStruct, dtype=jnp.bfloat16)
    kv, kv_far, q_own, g_own, row_start = pl.pallas_call(
        pack_kernel,
        out_shape=(
            bf16((2 * ROWS, 2 * KV)),
            bf16((ROWS, 2 * KV)),
            bf16((2 * ROWS, WIDE)),
            bf16((2 * ROWS, WIDE)),
            jax.ShapeDtypeStruct((4, GROUP * ROWS), jnp.int32),
        ),
        in_specs=smem(1) + hbm(6),
        out_specs=tuple(vmem(5)),
        scratch_shapes=[
            pltpu.SMEM(slot_to_block.shape, jnp.int32),
            pltpu.SMEM(doc_starts.shape, jnp.int32),
            pltpu.SemaphoreType.DMA((8,)),
        ],
        compiler_params=params,
        name="prepare",
    )(
        place,
        in_hbm(slot_to_block),
        in_hbm(doc_starts),
        in_hbm(key_rows_slotted),
        in_hbm(value_rows_slotted),
        in_hbm(queries),
        in_hbm(output_gradient),
    )
    kv_c = send(kv_far, -3, 3)
    kv_a = send(kv, 2, -2)
    kv_b = send(kv, -1, 1)
    kv_sib = send(kv, 1, -1)
    q_sib = send(queries, 1, -1)
    g_sib = send(output_gradient, 1, -1)

    dq_first, dq_rest, own, sib, out_a, out_b, out_c = pl.pallas_call(
        attention_kernel,
        out_shape=(
            bf16((ROWS, WIDE)),
            bf16((2, ROWS, WIDE)),
            jax.ShapeDtypeStruct((2 * ROWS, 2 * KV), jnp.float32),
            bf16((2 * ROWS, 2 * KV)),
            bf16((2 * ROWS, 2 * KV)),
            bf16((2 * ROWS, 2 * KV)),
            bf16((ROWS, 2 * KV)),
        ),
        in_specs=smem(3) + vmem(10),
        out_specs=tuple(vmem(7)),
        scratch_shapes=[
            pltpu.VMEM((ENTRIES * ROWS, 2 * KV), jnp.bfloat16),
            pltpu.VMEM((ENTRIES * ROWS, 2 * KV), jnp.float32),
            pltpu.VMEM((3, ROWS, WIDE), jnp.bfloat16),
            pltpu.VMEM((3, ROWS, WIDE), jnp.bfloat16),
            pltpu.VMEM((3, ROWS, WIDE), jnp.bfloat16),
            pltpu.VMEM((SPAN, GROUP * ROWS), jnp.float32),
        ],
        compiler_params=params,
        name="attention_items",
    )(
        place,
        in_hbm(slot_to_block),
        live,
        row_start,
        q_own,
        q_sib,
        g_own,
        g_sib,
        kv,
        kv_sib,
        kv_b,
        kv_a,
        kv_c,
    )

    back_c = send(out_c, -3, 3)
    back_a = send(out_a, -2, 2)
    back_b = send(out_b, -1, 1)
    back_sib = send(sib, 1, -1)
    dq_sib = send(dq_rest, 1, -1)

    query_grad, own = pl.pallas_call(
        early_kernel,
        out_shape=(
            bf16((2 * ROWS, WIDE)),
            jax.ShapeDtypeStruct((2 * ROWS, 2 * KV), jnp.float32),
        ),
        in_specs=smem(3) + vmem(5),
        out_specs=tuple(vmem(2)),
        compiler_params=params,
        cost_estimate=pl.CostEstimate(
            flops=1 << 36, bytes_accessed=1 << 22, transcendentals=0
        ),
        name="query_gradient_rows",
    )(
        place,
        in_hbm(slot_to_block),
        live,
        dq_first,
        dq_rest,
        dq_sib,
        own,
        back_c,
    )

    key_gradient, value_gradient = pl.pallas_call(
        sum_kernel,
        out_shape=(bf16((2 * ROWS, KV)), bf16((2 * ROWS, KV))),
        in_specs=vmem(4),
        out_specs=tuple(vmem(2)),
        compiler_params=params,
        name="key_value_gradient_sum",
    )(own, back_sib, back_a, back_b)
    return query_grad, key_gradient, value_gradient


def solution(mesh):
    rows = P(("section", "ctx"), None)
    return jax.shard_map(
        shards,
        mesh=mesh,
        in_specs=(rows, rows, rows, rows, P("section"), P("section"), P("section", None)),
        out_specs=(rows, rows, rows),
        check_vma=False,
    )
```

```python
import functools
import math

import jax
import jax.numpy as jnp
from jax import lax
from jax.experimental import pallas as pl
from jax.experimental.pallas import tpu as pltpu
from jax.sharding import PartitionSpec as P

QUERY_HEADS = 16
KEY_VALUE_HEADS = 4
GROUP = QUERY_HEADS // KEY_VALUE_HEADS
HEAD_WIDTH = 128
ROWS = 64
KV = KEY_VALUE_HEADS * HEAD_WIDTH
WIDE = QUERY_HEADS * HEAD_WIDTH
REACH = 3
SPAN = (REACH + 1) * ROWS
SCALE = 1.0 / math.sqrt(HEAD_WIDTH)
EXP2_SCALE = SCALE * math.log2(math.e)
MASKED = -1e30
FAR = 1 << 30
ENTRIES = 9
VMEM_LIMIT = 24 * 1024 * 1024

TABLE_A, TABLE_B, TABLE_C = 4, 6, 8


def send(array, even_by, odd_by):
    count = lax.axis_size("ctx")
    pairs = [(i, (i + (odd_by if i % 2 else even_by)) % count) for i in range(count)]
    return lax.ppermute(array, "ctx", pairs)


def fold_flags(chip_base, slots, live):
    half = slots.shape[0] // 2
    middle_even = slots[chip_base] == half - 1
    middle_odd = slots[chip_base + 2] == half - 1
    far_middle = jnp.logical_and(middle_odd, live[REACH, half] == 1)
    return middle_even, far_middle


def attention_kernel(
    place,
    slots,
    live,
    row_start,
    q_own,
    q_sib,
    g_own,
    g_sib,
    kv_own,
    kv_sib,
    kv_a,
    kv_b,
    kv_c,
    dq_first,
    dq_rest,
    out_own,
    out_sib,
    out_a,
    out_b,
    out_c,
    table,
    total,
    q_work,
    g_work,
    dq,
    bias,
):
    me = place[0]
    count = slots.shape[0] // 2
    parity = lax.rem(me, 2)
    is_odd = parity == 1
    chip_base = 2 * (me - parity)
    middle_even, far_middle = fold_flags(chip_base, slots, live)

    own_at = pl.multiple_of(parity * 128, 128)
    sib_at = pl.multiple_of((1 - parity) * 128, 128)
    table[pl.ds(own_at, 128), :] = kv_own[...]
    table[pl.ds(sib_at, 128), :] = kv_sib[...]
    table[TABLE_A * ROWS : TABLE_B * ROWS, :] = kv_a[...]
    table[TABLE_B * ROWS : TABLE_C * ROWS, :] = kv_b[...]
    table[TABLE_C * ROWS :, :] = kv_c[...]
    total[...] = jnp.zeros_like(total)

    toward = jnp.where(is_odd, 1, -1)
    near_a = lax.rem(me + 2 * toward + count, count)
    near_b = lax.rem(me + toward + count, count)
    far = lax.rem(me + 3 * toward + count, count)
    entry_ids = [slots[chip_base + e] for e in range(4)]
    entry_ids += [slots[2 * near_a], slots[2 * near_a + 1]]
    entry_ids += [slots[2 * near_b], slots[2 * near_b + 1]]
    entry_ids += [slots[2 * far + parity]]

    own_row = pl.multiple_of(parity * ROWS, ROWS)
    other_row = pl.multiple_of((1 - parity) * ROWS, ROWS)
    q_work[0] = q_own[pl.ds(own_row, ROWS), :]
    g_work[0] = g_own[pl.ds(own_row, ROWS), :]

    @pl.when(middle_even)
    def _():
        q_work[1] = q_own[pl.ds(other_row, ROWS), :]
        g_work[1] = g_own[pl.ds(other_row, ROWS), :]

    @pl.when(jnp.logical_not(middle_even))
    def _():
        q_work[1] = q_sib[pl.ds(own_row, ROWS), :]
        g_work[1] = g_sib[pl.ds(own_row, ROWS), :]

    @pl.when(far_middle)
    def _():
        q_work[2] = q_sib[ROWS:, :]
        g_work[2] = g_sib[ROWS:, :]

    first = jnp.where(jnp.logical_and(far_middle, is_odd), 1, 0)
    last = jnp.where(jnp.logical_and(far_middle, jnp.logical_not(is_odd)), 3, 2)

    own_entry = 3 * parity
    other_entry = jnp.where(middle_even, 1 + parity, jnp.where(is_odd, 1, 2))

    def work_item(item, carry):
        entry = jnp.where(item == 0, own_entry, jnp.where(item == 1, other_entry, 3))
        query_id = slots[chip_base + entry]
        indices = []
        key_base = []
        for distance in range(REACH + 1):
            key_id = query_id - distance
            is_live = jnp.logical_and(
                key_id >= 0, live[distance, query_id] == 1
            )
            index = jnp.int32(0)
            found = jnp.bool_(False)
            for e in range(ENTRIES):
                match = entry_ids[e] == key_id
                index = jnp.where(match, e, index)
                found = jnp.logical_or(found, match)
            ok = jnp.logical_and(is_live, found)
            indices.append(pl.multiple_of(jnp.where(ok, index, 0) * ROWS, ROWS))
            key_base.append(jnp.where(ok, key_id * ROWS, FAR))
        lane = lax.broadcasted_iota(jnp.int32, (1, GROUP * ROWS), 1)
        query_pos = query_id * ROWS + lax.rem(lane, ROWS)
        query_start = row_start[pl.ds(entry, 1), :]
        sub = lax.broadcasted_iota(jnp.int32, (ROWS, GROUP * ROWS), 0)
        for distance in range(REACH + 1):
            key_pos = sub + key_base[distance]
            allowed = jnp.logical_and(key_pos <= query_pos, key_pos >= query_start)
            bias[distance * ROWS : (distance + 1) * ROWS, :] = jnp.where(
                allowed, 0.0, MASKED
            )
        for g in range(KEY_VALUE_HEADS):
            kcols = slice(g * HEAD_WIDTH, (g + 1) * HEAD_WIDTH)
            vcols = slice(KV + g * HEAD_WIDTH, KV + (g + 1) * HEAD_WIDTH)
            heads = [
                slice((GROUP * g + j) * HEAD_WIDTH, (GROUP * g + j + 1) * HEAD_WIDTH)
                for j in range(GROUP)
            ]
            keys = jnp.concatenate([table[pl.ds(i, ROWS), kcols] for i in indices], 0)
            values = jnp.concatenate([table[pl.ds(i, ROWS), vcols] for i in indices], 0)
            q = jnp.concatenate([q_work[item, :, h] for h in heads], 0)
            grad = jnp.concatenate([g_work[item, :, h] for h in heads], 0)
            nt = (((1,), (1,)), ((), ()))
            raw = lax.dot_general(keys, q, nt, preferred_element_type=jnp.float32)
            raw = raw + bias[...]
            top = jnp.max(raw, axis=0, keepdims=True)
            weights = jnp.exp2((raw - top) * EXP2_SCALE)
            probs = weights * (1.0 / jnp.sum(weights, axis=0, keepdims=True))
            grad_scores = lax.dot_general(
                values, grad, nt, preferred_element_type=jnp.float32
            )
            offset = jnp.sum(probs * grad_scores, axis=0, keepdims=True)
            score_low = (probs * (grad_scores - offset)).astype(jnp.bfloat16)
            value_add = jnp.dot(
                probs.astype(jnp.bfloat16), grad, preferred_element_type=jnp.float32
            )
            key_add = jnp.dot(score_low, q, preferred_element_type=jnp.float32)
            query_add = lax.dot_general(
                score_low,
                keys,
                (((0,), (0,)), ((), ())),
                preferred_element_type=jnp.float32,
            )
            query_add = (query_add * SCALE).astype(jnp.bfloat16)
            for j, h in enumerate(heads):
                dq[item, :, h] = query_add[j * ROWS : (j + 1) * ROWS]
            for distance in range(REACH + 1):
                part = slice(distance * ROWS, (distance + 1) * ROWS)
                at = pl.ds(indices[distance], ROWS)
                total[at, kcols] += key_add[part] * SCALE
                total[at, vcols] += value_add[part]
        return carry

    lax.fori_loop(first, last, work_item, 0)

    dq_first[...] = dq[0]
    dq_rest[...] = dq[1:]
    out_own[...] = total[pl.ds(own_at, 128), :]
    out_sib[...] = total[pl.ds(sib_at, 128), :].astype(jnp.bfloat16)
    out_a[...] = total[TABLE_A * ROWS : TABLE_B * ROWS, :].astype(jnp.bfloat16)
    out_b[...] = total[TABLE_B * ROWS : TABLE_C * ROWS, :].astype(jnp.bfloat16)
    out_c[...] = total[TABLE_C * ROWS :, :].astype(jnp.bfloat16)


def pack_kernel(
    place,
    slots_hbm,
    docs_hbm,
    keys,
    values,
    queries,
    grads,
    both,
    far,
    q_own,
    g_own,
    row_start,
    slots,
    docs,
    sems,
):
    parity = lax.rem(place[0], 2)
    at = pl.ds(pl.multiple_of((1 - parity) * ROWS, ROWS), ROWS)
    copies = [
        pltpu.make_async_copy(source, target, sems.at[n])
        for n, (source, target) in enumerate(
            [
                (slots_hbm, slots),
                (docs_hbm, docs),
                (keys.at[at, :], far.at[:, pl.ds(0, KV)]),
                (values.at[at, :], far.at[:, pl.ds(KV, KV)]),
                (keys, both.at[:, pl.ds(0, KV)]),
                (values, both.at[:, pl.ds(KV, KV)]),
                (queries, q_own),
                (grads, g_own),
            ]
        )
    ]
    for copy in copies:
        copy.start()
    copies[0].wait()
    copies[1].wait()
    count = docs.shape[0]
    lane = lax.rem(lax.broadcasted_iota(jnp.int32, (1, GROUP * ROWS), 1), ROWS)
    for entry in range(4):
        first = slots[2 * (place[0] - parity) + entry] * ROWS

        def halve(_, bounds):
            low, high = bounds
            middle = (low + high) // 2
            begun = docs[middle] <= first
            inside = low < high
            return (
                jnp.where(jnp.logical_and(inside, begun), middle + 1, low),
                jnp.where(jnp.logical_and(inside, jnp.logical_not(begun)), middle, high),
            )

        begun, _ = lax.fori_loop(
            0, count.bit_length(), halve, (jnp.int32(1), jnp.int32(count))
        )

        def more(state):
            index, _ = state
            start = docs[jnp.minimum(index, count - 1)]
            return jnp.logical_and(index < count, start < first + ROWS)

        def step(state):
            index, row = state
            start = docs[index]
            return index + 1, jnp.where(lane + first >= start, start, row)

        _, row = lax.while_loop(
            more, step, (begun, jnp.full((1, GROUP * ROWS), docs[begun - 1]))
        )
        row_start[pl.ds(entry, 1), :] = row
    for copy in copies[2:]:
        copy.wait()


def early_kernel(place, slots, live, first, rest, theirs, own, back_c, out, acc):
    me = place[0]
    parity = lax.rem(me, 2)
    is_odd = parity == 1
    middle_even, far_middle = fold_flags(2 * (me - parity), slots, live)
    own_row = pl.multiple_of(parity * ROWS, ROWS)
    other_row = pl.multiple_of((1 - parity) * ROWS, ROWS)
    moved = jnp.logical_and(far_middle, is_odd)

    @pl.when(moved)
    def _():
        out[pl.ds(own_row, ROWS), :] = theirs[1]

    @pl.when(jnp.logical_not(moved))
    def _():
        out[pl.ds(own_row, ROWS), :] = first[...]

    @pl.when(middle_even)
    def _():
        out[pl.ds(other_row, ROWS), :] = rest[0]

    @pl.when(jnp.logical_not(middle_even))
    def _():
        out[pl.ds(other_row, ROWS), :] = theirs[0]

    acc[pl.ds(own_row, ROWS), :] = own[pl.ds(own_row, ROWS), :]
    acc[pl.ds(other_row, ROWS), :] = own[pl.ds(other_row, ROWS), :] + back_c[
        ...
    ].astype(jnp.float32)


def sum_kernel(own, sib, back_a, back_b, key_out, value_out):
    def total(columns):
        return (
            own[:, columns]
            + sib[:, columns].astype(jnp.float32)
            + back_a[:, columns].astype(jnp.float32)
            + back_b[:, columns].astype(jnp.float32)
        ).astype(jnp.bfloat16)

    key_out[...] = total(slice(0, KV))
    value_out[...] = total(slice(KV, 2 * KV))


def vmem(count):
    return [pl.BlockSpec(memory_space=pltpu.VMEM)] * count


def in_hbm(array):
    return pltpu.with_memory_space_constraint(array, pltpu.HBM)


def hbm(count):
    return [pl.BlockSpec(memory_space=pltpu.HBM)] * count


def smem(count):
    return [pl.BlockSpec(memory_space=pltpu.SMEM)] * count


def shards(
    queries,
    key_rows_slotted,
    value_rows_slotted,
    output_gradient,
    slot_to_block,
    doc_starts,
    block_live,
):
    me = lax.axis_index("ctx")
    place = me.astype(jnp.int32).reshape(1)
    live = block_live.T
    params = pltpu.CompilerParams(vmem_limit_bytes=VMEM_LIMIT)

    bf16 = functools.partial(jax.ShapeDtypeStruct, dtype=jnp.bfloat16)
    kv, kv_far, q_own, g_own, row_start = pl.pallas_call(
        pack_kernel,
        out_shape=(
            bf16((2 * ROWS, 2 * KV)),
            bf16((ROWS, 2 * KV)),
            bf16((2 * ROWS, WIDE)),
            bf16((2 * ROWS, WIDE)),
            jax.ShapeDtypeStruct((4, GROUP * ROWS), jnp.int32),
        ),
        in_specs=smem(1) + hbm(6),
        out_specs=tuple(vmem(5)),
        scratch_shapes=[
            pltpu.SMEM(slot_to_block.shape, jnp.int32),
            pltpu.SMEM(doc_starts.shape, jnp.int32),
            pltpu.SemaphoreType.DMA((8,)),
        ],
        compiler_params=params,
        name="prepare",
    )(
        place,
        in_hbm(slot_to_block),
        in_hbm(doc_starts),
        in_hbm(key_rows_slotted),
        in_hbm(value_rows_slotted),
        in_hbm(queries),
        in_hbm(output_gradient),
    )
    kv_c = send(kv_far, -3, 3)
    kv_a = send(kv, 2, -2)
    kv_b = send(kv, -1, 1)
    kv_sib = send(kv, 1, -1)
    q_sib = send(queries, 1, -1)
    g_sib = send(output_gradient, 1, -1)

    dq_first, dq_rest, own, sib, out_a, out_b, out_c = pl.pallas_call(
        attention_kernel,
        out_shape=(
            bf16((ROWS, WIDE)),
            bf16((2, ROWS, WIDE)),
            jax.ShapeDtypeStruct((2 * ROWS, 2 * KV), jnp.float32),
            bf16((2 * ROWS, 2 * KV)),
            bf16((2 * ROWS, 2 * KV)),
            bf16((2 * ROWS, 2 * KV)),
            bf16((ROWS, 2 * KV)),
        ),
        in_specs=smem(3) + vmem(10),
        out_specs=tuple(vmem(7)),
        scratch_shapes=[
            pltpu.VMEM((ENTRIES * ROWS, 2 * KV), jnp.bfloat16),
            pltpu.VMEM((ENTRIES * ROWS, 2 * KV), jnp.float32),
            pltpu.VMEM((3, ROWS, WIDE), jnp.bfloat16),
            pltpu.VMEM((3, ROWS, WIDE), jnp.bfloat16),
            pltpu.VMEM((3, ROWS, WIDE), jnp.bfloat16),
            pltpu.VMEM((SPAN, GROUP * ROWS), jnp.float32),
        ],
        compiler_params=params,
        name="attention_items",
    )(
        place,
        in_hbm(slot_to_block),
        live,
        row_start,
        q_own,
        q_sib,
        g_own,
        g_sib,
        kv,
        kv_sib,
        kv_a,
        kv_b,
        kv_c,
    )

    back_c = send(out_c, -3, 3)
    back_a = send(out_a, -2, 2)
    back_b = send(out_b, -1, 1)
    back_sib = send(sib, 1, -1)
    dq_sib = send(dq_rest, 1, -1)

    query_grad, own = pl.pallas_call(
        early_kernel,
        out_shape=(
            bf16((2 * ROWS, WIDE)),
            jax.ShapeDtypeStruct((2 * ROWS, 2 * KV), jnp.float32),
        ),
        in_specs=smem(3) + vmem(5),
        out_specs=tuple(vmem(2)),
        compiler_params=params,
        cost_estimate=pl.CostEstimate(
            flops=1 << 36, bytes_accessed=1 << 22, transcendentals=0
        ),
        name="query_gradient_rows",
    )(
        place,
        in_hbm(slot_to_block),
        live,
        dq_first,
        dq_rest,
        dq_sib,
        own,
        back_c,
    )

    key_gradient, value_gradient = pl.pallas_call(
        sum_kernel,
        out_shape=(bf16((2 * ROWS, KV)), bf16((2 * ROWS, KV))),
        in_specs=vmem(4),
        out_specs=tuple(vmem(2)),
        compiler_params=params,
        name="key_value_gradient_sum",
    )(own, back_sib, back_a, back_b)
    return query_grad, key_gradient, value_gradient


def solution(mesh):
    rows = P(("section", "ctx"), None)
    return jax.shard_map(
        shards,
        mesh=mesh,
        in_specs=(rows, rows, rows, rows, P("section"), P("section"), P("section", None)),
        out_specs=(rows, rows, rows),
        check_vma=False,
    )
```

```python
import functools
import math

import jax
import jax.numpy as jnp
from jax import lax
from jax.experimental import pallas as pl
from jax.experimental.pallas import tpu as pltpu
from jax.sharding import PartitionSpec as P

QUERY_HEADS = 16
KEY_VALUE_HEADS = 4
GROUP = QUERY_HEADS // KEY_VALUE_HEADS
HEAD_WIDTH = 128
ROWS = 64
KV = KEY_VALUE_HEADS * HEAD_WIDTH
WIDE = QUERY_HEADS * HEAD_WIDTH
REACH = 3
SPAN = (REACH + 1) * ROWS
SCALE = 1.0 / math.sqrt(HEAD_WIDTH)
EXP2_SCALE = SCALE * math.log2(math.e)
MASKED = -1e30
FAR = 1 << 30
ENTRIES = 7
VMEM_LIMIT = 24 * 1024 * 1024

TABLE_A, TABLE_B, TABLE_C = 4, 5, 6


def send(array, even_by, odd_by):
    count = lax.axis_size("ctx")
    pairs = [(i, (i + (odd_by if i % 2 else even_by)) % count) for i in range(count)]
    return lax.ppermute(array, "ctx", pairs)


def fold_flags(chip_base, slots, live):
    half = slots.shape[0] // 2
    middle_even = slots[chip_base] == half - 1
    middle_odd = slots[chip_base + 2] == half - 1
    far_middle = jnp.logical_and(middle_odd, live[REACH, half] == 1)
    return middle_even, far_middle


def attention_kernel(
    leading,
    place,
    slots,
    live,
    row_start,
    q_own,
    q_sib,
    g_own,
    g_sib,
    kv_own,
    kv_sib,
    kv_a,
    kv_b,
    *refs,
):
    if leading:
        dq_rest, total, table, q_work, g_work, bias = refs
        dq = dq_rest
    else:
        kv_c, total_in, dq_first, out_own, out_sib, out_a, out_b, out_c = refs[:8]
        total, table, q_work, g_work, bias = refs[8:]
        dq = dq_first
    me = place[0]
    count = slots.shape[0] // 2
    parity = lax.rem(me, 2)
    is_odd = parity == 1
    chip_base = 2 * (me - parity)
    middle_even, far_middle = fold_flags(chip_base, slots, live)

    own_at = pl.multiple_of(parity * 128, 128)
    sib_at = pl.multiple_of((1 - parity) * 128, 128)
    table[pl.ds(own_at, 128), :] = kv_own[...]
    table[pl.ds(sib_at, 128), :] = kv_sib[...]
    table[TABLE_A * ROWS : TABLE_B * ROWS, :] = kv_a[...]
    table[TABLE_B * ROWS : TABLE_C * ROWS, :] = kv_b[...]

    toward = jnp.where(is_odd, 1, -1)
    near_a = lax.rem(me + 2 * toward + count, count)
    near_b = lax.rem(me + toward + count, count)
    far = lax.rem(me + 3 * toward + count, count)
    passed_odd = jnp.logical_and(is_odd, slots[2 * near_a] == count - 1)
    passed_even = jnp.logical_and(is_odd, slots[2 * near_b] == count - 1)
    entry_ids = [slots[chip_base + e] for e in range(4)]
    entry_ids += [jnp.where(passed_even, count - 1, slots[2 * near_a + parity])]
    entry_ids += [slots[2 * near_b + parity]]
    if not leading:
        table[TABLE_C * ROWS :, :] = kv_c[...]
        entry_ids += [jnp.where(passed_odd, count - 1, slots[2 * far + parity])]

    own_row = pl.multiple_of(parity * ROWS, ROWS)
    other_row = pl.multiple_of((1 - parity) * ROWS, ROWS)
    if leading:
        total[...] = jnp.zeros_like(total)

        @pl.when(middle_even)
        def _():
            q_work[0] = q_own[pl.ds(other_row, ROWS), :]
            g_work[0] = g_own[pl.ds(other_row, ROWS), :]

        @pl.when(jnp.logical_not(middle_even))
        def _():
            q_work[0] = q_sib[pl.ds(own_row, ROWS), :]
            g_work[0] = g_sib[pl.ds(own_row, ROWS), :]

        @pl.when(far_middle)
        def _():
            q_work[1] = q_sib[ROWS:, :]
            g_work[1] = g_sib[ROWS:, :]

        first = 0
        last = jnp.where(jnp.logical_and(far_middle, jnp.logical_not(is_odd)), 2, 1)
        other_entry = jnp.where(middle_even, 1 + parity, jnp.where(is_odd, 1, 2))
    else:
        q_work[0] = q_own[pl.ds(own_row, ROWS), :]
        g_work[0] = g_own[pl.ds(own_row, ROWS), :]
        first = 0
        last = jnp.where(jnp.logical_and(far_middle, is_odd), 0, 1)

    def work_item(item, carry):
        entry = jnp.where(item == 0, other_entry, 3) if leading else 3 * parity
        query_id = slots[chip_base + entry]
        indices = []
        key_base = []
        for distance in range(REACH + 1):
            key_id = query_id - distance
            is_live = jnp.logical_and(key_id >= 0, live[distance, query_id] == 1)
            index = jnp.int32(0)
            found = jnp.bool_(False)
            for e in range(len(entry_ids)):
                match = entry_ids[e] == key_id
                index = jnp.where(match, e, index)
                found = jnp.logical_or(found, match)
            ok = jnp.logical_and(is_live, found)
            indices.append(pl.multiple_of(jnp.where(ok, index, 0) * ROWS, ROWS))
            key_base.append(jnp.where(ok, key_id * ROWS, FAR))
        lane = lax.broadcasted_iota(jnp.int32, (1, GROUP * ROWS), 1)
        query_pos = query_id * ROWS + lax.rem(lane, ROWS)
        query_start = row_start[pl.ds(entry, 1), :]
        sub = lax.broadcasted_iota(jnp.int32, (ROWS, GROUP * ROWS), 0)
        for distance in range(REACH + 1):
            key_pos = sub + key_base[distance]
            allowed = jnp.logical_and(key_pos <= query_pos, key_pos >= query_start)
            bias[distance * ROWS : (distance + 1) * ROWS, :] = jnp.where(
                allowed, 0.0, MASKED
            )
        for g in range(KEY_VALUE_HEADS):
            kcols = slice(g * HEAD_WIDTH, (g + 1) * HEAD_WIDTH)
            vcols = slice(KV + g * HEAD_WIDTH, KV + (g + 1) * HEAD_WIDTH)
            heads = [
                slice((GROUP * g + j) * HEAD_WIDTH, (GROUP * g + j + 1) * HEAD_WIDTH)
                for j in range(GROUP)
            ]
            keys = jnp.concatenate([table[pl.ds(i, ROWS), kcols] for i in indices], 0)
            values = jnp.concatenate([table[pl.ds(i, ROWS), vcols] for i in indices], 0)
            q = jnp.concatenate([q_work[item, :, h] for h in heads], 0)
            grad = jnp.concatenate([g_work[item, :, h] for h in heads], 0)
            nt = (((1,), (1,)), ((), ()))
            raw = lax.dot_general(keys, q, nt, preferred_element_type=jnp.float32)
            raw = raw + bias[...]
            top = jnp.max(raw, axis=0, keepdims=True)
            weights = jnp.exp2((raw - top) * EXP2_SCALE)
            probs = weights * (1.0 / jnp.sum(weights, axis=0, keepdims=True))
            grad_scores = lax.dot_general(
                values, grad, nt, preferred_element_type=jnp.float32
            )
            offset = jnp.sum(probs * grad_scores, axis=0, keepdims=True)
            score_low = (probs * (grad_scores - offset)).astype(jnp.bfloat16)
            value_add = jnp.dot(
                probs.astype(jnp.bfloat16), grad, preferred_element_type=jnp.float32
            )
            key_add = jnp.dot(score_low, q, preferred_element_type=jnp.float32)
            query_add = lax.dot_general(
                score_low,
                keys,
                (((0,), (0,)), ((), ())),
                preferred_element_type=jnp.float32,
            )
            query_add = (query_add * SCALE).astype(jnp.bfloat16)
            for j, h in enumerate(heads):
                dq[item, :, h] = query_add[j * ROWS : (j + 1) * ROWS]
            for distance in range(REACH + 1):
                part = slice(distance * ROWS, (distance + 1) * ROWS)
                at = pl.ds(indices[distance], ROWS)
                total[at, kcols] += key_add[part] * SCALE
                total[at, vcols] += value_add[part]
        return carry

    if not leading:
        total[...] = total_in[...]
    lax.fori_loop(first, last, work_item, 0)
    if leading:
        return
    low = jnp.bfloat16
    out_own[...] = total[pl.ds(own_at, 128), :]
    out_sib[...] = total[pl.ds(sib_at, 128), :].astype(low)
    nothing = jnp.zeros((ROWS, 2 * KV), low)
    passed = slice(TABLE_C * ROWS, ENTRIES * ROWS)
    out_a[pl.ds(own_row, ROWS), :] = total[TABLE_A * ROWS : TABLE_B * ROWS, :].astype(low)
    out_b[pl.ds(own_row, ROWS), :] = total[TABLE_B * ROWS : TABLE_C * ROWS, :].astype(low)
    out_a[pl.ds(other_row, ROWS), :] = nothing
    out_b[pl.ds(other_row, ROWS), :] = nothing
    out_c[...] = total[passed, :].astype(low)

    @pl.when(passed_odd)
    def _():
        out_a[pl.ds(other_row, ROWS), :] = total[passed, :].astype(low)
        out_c[...] = nothing

    @pl.when(passed_even)
    def _():
        out_b[pl.ds(other_row, ROWS), :] = out_a[pl.ds(own_row, ROWS), :]
        out_a[pl.ds(own_row, ROWS), :] = nothing


def pack_kernel(
    place,
    slots_hbm,
    docs_hbm,
    keys,
    values,
    queries,
    grads,
    both,
    chain,
    cross,
    q_own,
    g_own,
    row_start,
    slots,
    docs,
    sems,
):
    parity = lax.rem(place[0], 2)
    own_rows = pl.ds(pl.multiple_of(parity * ROWS, ROWS), ROWS)
    other_rows = pl.ds(pl.multiple_of((1 - parity) * ROWS, ROWS), ROWS)
    copies = [
        pltpu.make_async_copy(source, target, sems.at[n])
        for n, (source, target) in enumerate(
            [
                (slots_hbm, slots),
                (docs_hbm, docs),
                (keys.at[other_rows, :], cross.at[:, pl.ds(0, KV)]),
                (values.at[other_rows, :], cross.at[:, pl.ds(KV, KV)]),
                (keys.at[own_rows, :], chain.at[:, pl.ds(0, KV)]),
                (values.at[own_rows, :], chain.at[:, pl.ds(KV, KV)]),
                (keys, both.at[:, pl.ds(0, KV)]),
                (values, both.at[:, pl.ds(KV, KV)]),
                (queries, q_own),
                (grads, g_own),
            ]
        )
    ]
    for copy in copies:
        copy.start()
    copies[0].wait()
    copies[1].wait()
    count = docs.shape[0]
    lane = lax.rem(lax.broadcasted_iota(jnp.int32, (1, GROUP * ROWS), 1), ROWS)
    for entry in range(4):
        first = slots[2 * (place[0] - parity) + entry] * ROWS

        def halve(_, bounds):
            low, high = bounds
            middle = (low + high) // 2
            begun = docs[middle] <= first
            inside = low < high
            return (
                jnp.where(jnp.logical_and(inside, begun), middle + 1, low),
                jnp.where(jnp.logical_and(inside, jnp.logical_not(begun)), middle, high),
            )

        begun, _ = lax.fori_loop(
            0, count.bit_length(), halve, (jnp.int32(1), jnp.int32(count))
        )

        def more(state):
            index, _ = state
            start = docs[jnp.minimum(index, count - 1)]
            return jnp.logical_and(index < count, start < first + ROWS)

        def step(state):
            index, row = state
            start = docs[index]
            return index + 1, jnp.where(lane + first >= start, start, row)

        _, row = lax.while_loop(
            more, step, (begun, jnp.full((1, GROUP * ROWS), docs[begun - 1]))
        )
        row_start[pl.ds(entry, 1), :] = row
    for copy in copies[2:]:
        copy.wait()


def early_kernel(place, slots, live, first, rest, theirs, own, back_c, out, acc):
    me = place[0]
    parity = lax.rem(me, 2)
    is_odd = parity == 1
    middle_even, far_middle = fold_flags(2 * (me - parity), slots, live)
    own_row = pl.multiple_of(parity * ROWS, ROWS)
    other_row = pl.multiple_of((1 - parity) * ROWS, ROWS)
    moved = jnp.logical_and(far_middle, is_odd)

    @pl.when(moved)
    def _():
        out[pl.ds(own_row, ROWS), :] = theirs[1]

    @pl.when(jnp.logical_not(moved))
    def _():
        out[pl.ds(own_row, ROWS), :] = first[0]

    @pl.when(middle_even)
    def _():
        out[pl.ds(other_row, ROWS), :] = rest[0]

    @pl.when(jnp.logical_not(middle_even))
    def _():
        out[pl.ds(other_row, ROWS), :] = theirs[0]

    acc[pl.ds(own_row, ROWS), :] = own[pl.ds(own_row, ROWS), :]
    acc[pl.ds(other_row, ROWS), :] = own[pl.ds(other_row, ROWS), :] + back_c[
        ...
    ].astype(jnp.float32)


def sum_kernel(own, sib, back_a, back_b, key_out, value_out):
    def total(columns):
        return (
            own[:, columns]
            + sib[:, columns].astype(jnp.float32)
            + back_a[:, columns].astype(jnp.float32)
            + back_b[:, columns].astype(jnp.float32)
        ).astype(jnp.bfloat16)

    key_out[...] = total(slice(0, KV))
    value_out[...] = total(slice(KV, 2 * KV))


def vmem(count):
    return [pl.BlockSpec(memory_space=pltpu.VMEM)] * count


def in_hbm(array):
    return pltpu.with_memory_space_constraint(array, pltpu.HBM)


def hbm(count):
    return [pl.BlockSpec(memory_space=pltpu.HBM)] * count


def smem(count):
    return [pl.BlockSpec(memory_space=pltpu.SMEM)] * count


def shards(
    queries,
    key_rows_slotted,
    value_rows_slotted,
    output_gradient,
    slot_to_block,
    doc_starts,
    block_live,
):
    me = lax.axis_index("ctx")
    place = me.astype(jnp.int32).reshape(1)
    live = block_live.T
    params = pltpu.CompilerParams(vmem_limit_bytes=VMEM_LIMIT)

    bf16 = functools.partial(jax.ShapeDtypeStruct, dtype=jnp.bfloat16)
    kv, kv_chain, kv_cross, q_own, g_own, row_start = pl.pallas_call(
        pack_kernel,
        out_shape=(
            bf16((2 * ROWS, 2 * KV)),
            bf16((ROWS, 2 * KV)),
            bf16((ROWS, 2 * KV)),
            bf16((2 * ROWS, WIDE)),
            bf16((2 * ROWS, WIDE)),
            jax.ShapeDtypeStruct((4, GROUP * ROWS), jnp.int32),
        ),
        in_specs=smem(1) + hbm(6),
        out_specs=tuple(vmem(6)),
        scratch_shapes=[
            pltpu.SMEM(slot_to_block.shape, jnp.int32),
            pltpu.SMEM(doc_starts.shape, jnp.int32),
            pltpu.SemaphoreType.DMA((10,)),
        ],
        compiler_params=params,
        name="prepare",
    )(
        place,
        in_hbm(slot_to_block),
        in_hbm(doc_starts),
        in_hbm(key_rows_slotted),
        in_hbm(value_rows_slotted),
        in_hbm(queries),
        in_hbm(output_gradient),
    )
    kv_sib = send(kv, 1, -1)
    kv_b = send(kv_cross, -1, 1)
    q_sib = send(queries, 1, -1)
    g_sib = send(output_gradient, 1, -1)
    chip_ids = lax.dynamic_slice_in_dim(slot_to_block, 2 * (me - me % 2), 4, 0)
    middle = slot_to_block.shape[0] // 2 - 1
    is_odd = me % 2 == 1
    swapped = jnp.logical_and(is_odd, chip_ids[0] == middle)
    kv_a = send(jnp.where(swapped, kv_sib[:ROWS], kv_chain), 2, -2)
    holds = jnp.logical_and(is_odd, chip_ids[2] == middle)
    kv_c = send(jnp.where(holds, kv[:ROWS], kv_b), 2, -2)

    work = [
        pltpu.VMEM((ENTRIES * ROWS, 2 * KV), jnp.bfloat16),
        pltpu.VMEM((2, ROWS, WIDE), jnp.bfloat16),
        pltpu.VMEM((2, ROWS, WIDE), jnp.bfloat16),
        pltpu.VMEM((SPAN, GROUP * ROWS), jnp.float32),
    ]
    sums = jax.ShapeDtypeStruct((ENTRIES * ROWS, 2 * KV), jnp.float32)
    operands = (
        place,
        in_hbm(slot_to_block),
        live,
        row_start,
        q_own,
        q_sib,
        g_own,
        g_sib,
        kv,
        kv_sib,
        kv_a,
        kv_b,
    )
    dq_rest, total = pl.pallas_call(
        functools.partial(attention_kernel, True),
        out_shape=(bf16((2, ROWS, WIDE)), sums),
        in_specs=smem(3) + vmem(9),
        out_specs=tuple(vmem(2)),
        scratch_shapes=work,
        compiler_params=params,
        cost_estimate=pl.CostEstimate(
            flops=1 << 36, bytes_accessed=1 << 22, transcendentals=1 << 18
        ),
        name="attention_leading",
    )(*operands)
    dq_first, own, sib, out_a, out_b, out_c = pl.pallas_call(
        functools.partial(attention_kernel, False),
        out_shape=(
            bf16((1, ROWS, WIDE)),
            jax.ShapeDtypeStruct((2 * ROWS, 2 * KV), jnp.float32),
            bf16((2 * ROWS, 2 * KV)),
            bf16((2 * ROWS, 2 * KV)),
            bf16((2 * ROWS, 2 * KV)),
            bf16((ROWS, 2 * KV)),
        ),
        in_specs=smem(3) + vmem(11),
        out_specs=tuple(vmem(6)),
        scratch_shapes=[pltpu.VMEM(sums.shape, jnp.float32)] + work,
        compiler_params=params,
        name="attention_last",
    )(*operands, kv_c, total)

    back_c = send(out_c, -3, 3)
    back_a = send(out_a, -2, 2)
    back_b = send(out_b, -1, 1)
    back_sib = send(sib, 1, -1)
    dq_rest, _ = lax.optimization_barrier((dq_rest, out_c))
    dq_sib = send(dq_rest, 1, -1)

    query_grad, own = pl.pallas_call(
        early_kernel,
        out_shape=(
            bf16((2 * ROWS, WIDE)),
            jax.ShapeDtypeStruct((2 * ROWS, 2 * KV), jnp.float32),
        ),
        in_specs=smem(3) + vmem(5),
        out_specs=tuple(vmem(2)),
        compiler_params=params,
        cost_estimate=pl.CostEstimate(
            flops=1 << 36, bytes_accessed=1 << 22, transcendentals=0
        ),
        name="query_gradient_rows",
    )(
        place,
        in_hbm(slot_to_block),
        live,
        dq_first,
        dq_rest,
        dq_sib,
        own,
        back_c,
    )

    key_gradient, value_gradient = pl.pallas_call(
        sum_kernel,
        out_shape=(bf16((2 * ROWS, KV)), bf16((2 * ROWS, KV))),
        in_specs=vmem(4),
        out_specs=tuple(vmem(2)),
        compiler_params=params,
        name="key_value_gradient_sum",
    )(own, back_sib, back_a, back_b)
    return query_grad, key_gradient, value_gradient


def solution(mesh):
    rows = P(("section", "ctx"), None)
    return jax.shard_map(
        shards,
        mesh=mesh,
        in_specs=(rows, rows, rows, rows, P("section"), P("section"), P("section", None)),
        out_specs=(rows, rows, rows),
        check_vma=False,
    )
```

```python
import functools
import math

import jax
import jax.numpy as jnp
from jax import lax
from jax.experimental import pallas as pl
from jax.experimental.pallas import tpu as pltpu
from jax.sharding import PartitionSpec as P

QUERY_HEADS = 16
KEY_VALUE_HEADS = 4
GROUP = QUERY_HEADS // KEY_VALUE_HEADS
HEAD_WIDTH = 128
ROWS = 64
KV = KEY_VALUE_HEADS * HEAD_WIDTH
WIDE = QUERY_HEADS * HEAD_WIDTH
REACH = 3
SPAN = (REACH + 1) * ROWS
SCALE = 1.0 / math.sqrt(HEAD_WIDTH)
EXP2_SCALE = SCALE * math.log2(math.e)
MASKED = -1e30
FAR = 1 << 30
ENTRIES = 7
VMEM_LIMIT = 24 * 1024 * 1024

TABLE_A, TABLE_B, TABLE_C = 4, 5, 6


def send(array, even_by, odd_by):
    count = lax.axis_size("ctx")
    pairs = [(i, (i + (odd_by if i % 2 else even_by)) % count) for i in range(count)]
    return lax.ppermute(array, "ctx", pairs)


def fold_flags(chip_base, slots, live):
    half = slots.shape[0] // 2
    middle_even = slots[chip_base] == half - 1
    middle_odd = slots[chip_base + 2] == half - 1
    far_middle = jnp.logical_and(middle_odd, live[REACH, half] == 1)
    return middle_even, far_middle


def attention_kernel(
    leading,
    place,
    slots,
    live,
    row_start,
    q_own,
    q_sib,
    g_own,
    g_sib,
    kv_own,
    kv_sib,
    kv_a,
    kv_b,
    *refs,
):
    if leading:
        dq, total, table, q_work, g_work, bias = refs
    else:
        kv_c, dq_in, total_in, dq_first, dq_rest, out_own, out_sib, out_a, out_b, out_c = (
            refs[:10]
        )
        dq, total, table, q_work, g_work, bias = refs[10:]
    me = place[0]
    count = slots.shape[0] // 2
    parity = lax.rem(me, 2)
    is_odd = parity == 1
    chip_base = 2 * (me - parity)
    middle_even, far_middle = fold_flags(chip_base, slots, live)

    own_at = pl.multiple_of(parity * 128, 128)
    sib_at = pl.multiple_of((1 - parity) * 128, 128)
    table[pl.ds(own_at, 128), :] = kv_own[...]
    table[pl.ds(sib_at, 128), :] = kv_sib[...]
    table[TABLE_A * ROWS : TABLE_B * ROWS, :] = kv_a[...]
    table[TABLE_B * ROWS : TABLE_C * ROWS, :] = kv_b[...]

    toward = jnp.where(is_odd, 1, -1)
    near_a = lax.rem(me + 2 * toward + count, count)
    near_b = lax.rem(me + toward + count, count)
    far = lax.rem(me + 3 * toward + count, count)
    passed_odd = jnp.logical_and(is_odd, slots[2 * near_a] == count - 1)
    passed_even = jnp.logical_and(is_odd, slots[2 * near_b] == count - 1)
    entry_ids = [slots[chip_base + e] for e in range(4)]
    entry_ids += [slots[2 * near_a + parity], slots[2 * near_b + parity]]
    if not leading:
        table[TABLE_C * ROWS :, :] = kv_c[...]
        passed_middle = jnp.logical_or(passed_odd, passed_even)
        entry_ids += [jnp.where(passed_middle, count - 1, slots[2 * far + parity])]

    own_row = pl.multiple_of(parity * ROWS, ROWS)
    other_row = pl.multiple_of((1 - parity) * ROWS, ROWS)
    other_entry = jnp.where(middle_even, 1 + parity, jnp.where(is_odd, 1, 2))
    slot = 0 if leading else 1

    @pl.when(middle_even)
    def _():
        q_work[slot] = q_own[pl.ds(other_row, ROWS), :]
        g_work[slot] = g_own[pl.ds(other_row, ROWS), :]

    @pl.when(jnp.logical_not(middle_even))
    def _():
        q_work[slot] = q_sib[pl.ds(own_row, ROWS), :]
        g_work[slot] = g_sib[pl.ds(own_row, ROWS), :]

    if leading:
        total[...] = jnp.zeros_like(total)

        @pl.when(far_middle)
        def _():
            q_work[1] = q_sib[ROWS:, :]
            g_work[1] = g_sib[ROWS:, :]

        entries = (other_entry, 3)
        first = jnp.where(passed_even, 1, 0)
        last = jnp.where(jnp.logical_and(far_middle, jnp.logical_not(is_odd)), 2, 1)
    else:
        total[...] = total_in[...]
        q_work[0] = q_own[pl.ds(own_row, ROWS), :]
        g_work[0] = g_own[pl.ds(own_row, ROWS), :]
        entries = (3 * parity, other_entry)
        first = jnp.where(jnp.logical_and(far_middle, is_odd), 1, 0)
        last = jnp.where(passed_even, 2, 1)

    def work_item(item, carry):
        entry = jnp.where(item == 0, *entries)
        query_id = slots[chip_base + entry]
        indices = []
        key_base = []
        for distance in range(REACH + 1):
            key_id = query_id - distance
            is_live = jnp.logical_and(key_id >= 0, live[distance, query_id] == 1)
            index = jnp.int32(0)
            found = jnp.bool_(False)
            for e in range(len(entry_ids)):
                match = entry_ids[e] == key_id
                index = jnp.where(match, e, index)
                found = jnp.logical_or(found, match)
            ok = jnp.logical_and(is_live, found)
            indices.append(pl.multiple_of(jnp.where(ok, index, 0) * ROWS, ROWS))
            key_base.append(jnp.where(ok, key_id * ROWS, FAR))
        lane = lax.broadcasted_iota(jnp.int32, (1, GROUP * ROWS), 1)
        query_pos = query_id * ROWS + lax.rem(lane, ROWS)
        query_start = row_start[pl.ds(entry, 1), :]
        sub = lax.broadcasted_iota(jnp.int32, (ROWS, GROUP * ROWS), 0)
        for distance in range(REACH + 1):
            key_pos = sub + key_base[distance]
            allowed = jnp.logical_and(key_pos <= query_pos, key_pos >= query_start)
            bias[distance * ROWS : (distance + 1) * ROWS, :] = jnp.where(
                allowed, 0.0, MASKED
            )
        for g in range(KEY_VALUE_HEADS):
            kcols = slice(g * HEAD_WIDTH, (g + 1) * HEAD_WIDTH)
            vcols = slice(KV + g * HEAD_WIDTH, KV + (g + 1) * HEAD_WIDTH)
            heads = [
                slice((GROUP * g + j) * HEAD_WIDTH, (GROUP * g + j + 1) * HEAD_WIDTH)
                for j in range(GROUP)
            ]
            keys = jnp.concatenate([table[pl.ds(i, ROWS), kcols] for i in indices], 0)
            values = jnp.concatenate([table[pl.ds(i, ROWS), vcols] for i in indices], 0)
            q = jnp.concatenate([q_work[item, :, h] for h in heads], 0)
            grad = jnp.concatenate([g_work[item, :, h] for h in heads], 0)
            nt = (((1,), (1,)), ((), ()))
            raw = lax.dot_general(keys, q, nt, preferred_element_type=jnp.float32)
            raw = raw + bias[...]
            top = jnp.max(raw, axis=0, keepdims=True)
            weights = jnp.exp2((raw - top) * EXP2_SCALE)
            probs = weights * (1.0 / jnp.sum(weights, axis=0, keepdims=True))
            grad_scores = lax.dot_general(
                values, grad, nt, preferred_element_type=jnp.float32
            )
            offset = jnp.sum(probs * grad_scores, axis=0, keepdims=True)
            score_low = (probs * (grad_scores - offset)).astype(jnp.bfloat16)
            value_add = jnp.dot(
                probs.astype(jnp.bfloat16), grad, preferred_element_type=jnp.float32
            )
            key_add = jnp.dot(score_low, q, preferred_element_type=jnp.float32)
            query_add = lax.dot_general(
                score_low,
                keys,
                (((0,), (0,)), ((), ())),
                preferred_element_type=jnp.float32,
            )
            query_add = (query_add * SCALE).astype(jnp.bfloat16)
            for j, h in enumerate(heads):
                dq[item, :, h] = query_add[j * ROWS : (j + 1) * ROWS]
            for distance in range(REACH + 1):
                part = slice(distance * ROWS, (distance + 1) * ROWS)
                at = pl.ds(indices[distance], ROWS)
                total[at, kcols] += key_add[part] * SCALE
                total[at, vcols] += value_add[part]
        return carry

    lax.fori_loop(first, last, work_item, 0)
    if leading:
        return
    low = jnp.bfloat16
    dq_first[...] = dq[0]
    dq_rest[...] = dq_in[...]

    @pl.when(passed_even)
    def _():
        dq_rest[0] = dq[1]

    out_own[...] = total[pl.ds(own_at, 128), :]
    out_sib[...] = total[pl.ds(sib_at, 128), :].astype(low)
    nothing = jnp.zeros((ROWS, 2 * KV), low)
    passed = slice(TABLE_C * ROWS, ENTRIES * ROWS)
    out_a[pl.ds(own_row, ROWS), :] = total[TABLE_A * ROWS : TABLE_B * ROWS, :].astype(low)
    out_b[pl.ds(own_row, ROWS), :] = total[TABLE_B * ROWS : TABLE_C * ROWS, :].astype(low)
    out_a[pl.ds(other_row, ROWS), :] = nothing
    out_b[pl.ds(other_row, ROWS), :] = nothing
    out_c[...] = total[passed, :].astype(low)

    @pl.when(passed_odd)
    def _():
        out_a[pl.ds(other_row, ROWS), :] = total[passed, :].astype(low)
        out_c[...] = nothing

    @pl.when(passed_even)
    def _():
        out_b[pl.ds(other_row, ROWS), :] = total[passed, :].astype(low)
        out_c[...] = nothing


def pack_kernel(
    place,
    slots_hbm,
    docs_hbm,
    keys,
    values,
    queries,
    grads,
    both,
    chain,
    cross,
    q_own,
    g_own,
    row_start,
    fold,
    slots,
    docs,
    sems,
):
    parity = lax.rem(place[0], 2)
    own_rows = pl.ds(pl.multiple_of(parity * ROWS, ROWS), ROWS)
    other_rows = pl.ds(pl.multiple_of((1 - parity) * ROWS, ROWS), ROWS)
    copies = [
        pltpu.make_async_copy(source, target, sems.at[n])
        for n, (source, target) in enumerate(
            [
                (slots_hbm, slots),
                (docs_hbm, docs),
                (keys.at[other_rows, :], cross.at[:, pl.ds(0, KV)]),
                (values.at[other_rows, :], cross.at[:, pl.ds(KV, KV)]),
                (keys.at[own_rows, :], chain.at[:, pl.ds(0, KV)]),
                (values.at[own_rows, :], chain.at[:, pl.ds(KV, KV)]),
                (keys, both.at[:, pl.ds(0, KV)]),
                (values, both.at[:, pl.ds(KV, KV)]),
                (queries, q_own),
                (grads, g_own),
            ]
        )
    ]
    for copy in copies:
        copy.start()
    copies[0].wait()
    copies[1].wait()
    middle = slots.shape[0] // 2 - 1
    chip_base = 2 * (place[0] - parity)
    holder = jnp.where(
        slots[chip_base + 2] == middle, 1, jnp.where(slots[chip_base] == middle, 2, 0)
    )
    fold[...] = jnp.full(fold.shape, jnp.where(parity == 1, holder, 0))
    count = docs.shape[0]
    lane = lax.rem(lax.broadcasted_iota(jnp.int32, (1, GROUP * ROWS), 1), ROWS)
    for entry in range(4):
        first = slots[chip_base + entry] * ROWS

        def halve(_, bounds):
            low, high = bounds
            middle = (low + high) // 2
            begun = docs[middle] <= first
            inside = low < high
            return (
                jnp.where(jnp.logical_and(inside, begun), middle + 1, low),
                jnp.where(jnp.logical_and(inside, jnp.logical_not(begun)), middle, high),
            )

        begun, _ = lax.fori_loop(
            0, count.bit_length(), halve, (jnp.int32(1), jnp.int32(count))
        )

        def more(state):
            index, _ = state
            start = docs[jnp.minimum(index, count - 1)]
            return jnp.logical_and(index < count, start < first + ROWS)

        def step(state):
            index, row = state
            start = docs[index]
            return index + 1, jnp.where(lane + first >= start, start, row)

        _, row = lax.while_loop(
            more, step, (begun, jnp.full((1, GROUP * ROWS), docs[begun - 1]))
        )
        row_start[pl.ds(entry, 1), :] = row
    for copy in copies[2:]:
        copy.wait()


def early_kernel(place, slots, live, first, rest, theirs, own, back_c, out, acc):
    me = place[0]
    parity = lax.rem(me, 2)
    is_odd = parity == 1
    middle_even, far_middle = fold_flags(2 * (me - parity), slots, live)
    own_row = pl.multiple_of(parity * ROWS, ROWS)
    other_row = pl.multiple_of((1 - parity) * ROWS, ROWS)
    moved = jnp.logical_and(far_middle, is_odd)

    @pl.when(moved)
    def _():
        out[pl.ds(own_row, ROWS), :] = theirs[1]

    @pl.when(jnp.logical_not(moved))
    def _():
        out[pl.ds(own_row, ROWS), :] = first[...]

    @pl.when(middle_even)
    def _():
        out[pl.ds(other_row, ROWS), :] = rest[0]

    @pl.when(jnp.logical_not(middle_even))
    def _():
        out[pl.ds(other_row, ROWS), :] = theirs[0]

    acc[pl.ds(own_row, ROWS), :] = own[pl.ds(own_row, ROWS), :]
    acc[pl.ds(other_row, ROWS), :] = own[pl.ds(other_row, ROWS), :] + back_c[
        ...
    ].astype(jnp.float32)


def sum_kernel(own, sib, back_a, back_b, key_out, value_out):
    def total(columns):
        return (
            own[:, columns]
            + sib[:, columns].astype(jnp.float32)
            + back_a[:, columns].astype(jnp.float32)
            + back_b[:, columns].astype(jnp.float32)
        ).astype(jnp.bfloat16)

    key_out[...] = total(slice(0, KV))
    value_out[...] = total(slice(KV, 2 * KV))


def vmem(count):
    return [pl.BlockSpec(memory_space=pltpu.VMEM)] * count


def in_hbm(array):
    return pltpu.with_memory_space_constraint(array, pltpu.HBM)


def hbm(count):
    return [pl.BlockSpec(memory_space=pltpu.HBM)] * count


def smem(count):
    return [pl.BlockSpec(memory_space=pltpu.SMEM)] * count


def shards(
    queries,
    key_rows_slotted,
    value_rows_slotted,
    output_gradient,
    slot_to_block,
    doc_starts,
    block_live,
):
    me = lax.axis_index("ctx")
    place = me.astype(jnp.int32).reshape(1)
    live = block_live.T
    params = pltpu.CompilerParams(vmem_limit_bytes=VMEM_LIMIT)

    bf16 = functools.partial(jax.ShapeDtypeStruct, dtype=jnp.bfloat16)
    kv, kv_chain, kv_cross, q_own, g_own, row_start, fold = pl.pallas_call(
        pack_kernel,
        out_shape=(
            bf16((2 * ROWS, 2 * KV)),
            bf16((ROWS, 2 * KV)),
            bf16((ROWS, 2 * KV)),
            bf16((2 * ROWS, WIDE)),
            bf16((2 * ROWS, WIDE)),
            jax.ShapeDtypeStruct((4, GROUP * ROWS), jnp.int32),
            jax.ShapeDtypeStruct((8, 128), jnp.int32),
        ),
        in_specs=smem(1) + hbm(6),
        out_specs=tuple(vmem(7)),
        scratch_shapes=[
            pltpu.SMEM(slot_to_block.shape, jnp.int32),
            pltpu.SMEM(doc_starts.shape, jnp.int32),
            pltpu.SemaphoreType.DMA((10,)),
        ],
        compiler_params=params,
        name="prepare",
    )(
        place,
        in_hbm(slot_to_block),
        in_hbm(doc_starts),
        in_hbm(key_rows_slotted),
        in_hbm(value_rows_slotted),
        in_hbm(queries),
        in_hbm(output_gradient),
    )
    kv_a = send(kv_chain, 2, -2)
    kv_b = send(kv_cross, -1, 1)
    kv_sib = send(kv, 1, -1)
    q_sib = send(queries, 1, -1)
    g_sib = send(output_gradient, 1, -1)
    which = fold[:1, :1]
    passed = jnp.where(which == 1, kv[:ROWS], jnp.where(which == 2, kv_sib[:ROWS], kv_b))
    kv_c = send(passed, 2, -2)

    work = [
        pltpu.VMEM((2, ROWS, WIDE), jnp.bfloat16),
        pltpu.VMEM((ENTRIES * ROWS, 2 * KV), jnp.bfloat16),
        pltpu.VMEM((2, ROWS, WIDE), jnp.bfloat16),
        pltpu.VMEM((2, ROWS, WIDE), jnp.bfloat16),
        pltpu.VMEM((SPAN, GROUP * ROWS), jnp.float32),
    ]
    sums = jax.ShapeDtypeStruct((ENTRIES * ROWS, 2 * KV), jnp.float32)
    operands = (
        place,
        in_hbm(slot_to_block),
        live,
        row_start,
        q_own,
        q_sib,
        g_own,
        g_sib,
        kv,
        kv_sib,
        kv_a,
        kv_b,
    )
    dq_leading, total = pl.pallas_call(
        functools.partial(attention_kernel, True),
        out_shape=(bf16((2, ROWS, WIDE)), sums),
        in_specs=smem(3) + vmem(9),
        out_specs=tuple(vmem(2)),
        scratch_shapes=work[1:],
        compiler_params=params,
        cost_estimate=pl.CostEstimate(
            flops=1 << 36, bytes_accessed=1 << 22, transcendentals=1 << 18
        ),
        name="attention_leading",
    )(*operands)
    dq_first, dq_rest, own, sib, out_a, out_b, out_c = pl.pallas_call(
        functools.partial(attention_kernel, False),
        out_shape=(
            bf16((ROWS, WIDE)),
            bf16((2, ROWS, WIDE)),
            jax.ShapeDtypeStruct((2 * ROWS, 2 * KV), jnp.float32),
            bf16((2 * ROWS, 2 * KV)),
            bf16((2 * ROWS, 2 * KV)),
            bf16((2 * ROWS, 2 * KV)),
            bf16((ROWS, 2 * KV)),
        ),
        in_specs=smem(3) + vmem(12),
        out_specs=tuple(vmem(7)),
        scratch_shapes=work[:1] + [pltpu.VMEM(sums.shape, jnp.float32)] + work[1:],
        compiler_params=params,
        name="attention_last",
    )(*operands, kv_c, dq_leading, total)

    back_c = send(out_c, -3, 3)
    back_a = send(out_a, -2, 2)
    back_b = send(out_b, -1, 1)
    back_sib = send(sib, 1, -1)
    dq_sib = send(dq_rest, 1, -1)

    query_grad, own = pl.pallas_call(
        early_kernel,
        out_shape=(
            bf16((2 * ROWS, WIDE)),
            jax.ShapeDtypeStruct((2 * ROWS, 2 * KV), jnp.float32),
        ),
        in_specs=smem(3) + vmem(5),
        out_specs=tuple(vmem(2)),
        compiler_params=params,
        cost_estimate=pl.CostEstimate(
            flops=1 << 36, bytes_accessed=1 << 22, transcendentals=0
        ),
        name="query_gradient_rows",
    )(
        place,
        in_hbm(slot_to_block),
        live,
        dq_first,
        dq_rest,
        dq_sib,
        own,
        back_c,
    )

    key_gradient, value_gradient = pl.pallas_call(
        sum_kernel,
        out_shape=(bf16((2 * ROWS, KV)), bf16((2 * ROWS, KV))),
        in_specs=vmem(4),
        out_specs=tuple(vmem(2)),
        compiler_params=params,
        name="key_value_gradient_sum",
    )(own, back_sib, back_a, back_b)
    return query_grad, key_gradient, value_gradient


def solution(mesh):
    rows = P(("section", "ctx"), None)
    return jax.shard_map(
        shards,
        mesh=mesh,
        in_specs=(rows, rows, rows, rows, P("section"), P("section"), P("section", None)),
        out_specs=(rows, rows, rows),
        check_vma=False,
    )
```

```python
import functools
import math

import jax
import jax.numpy as jnp
from jax import lax
from jax.experimental import pallas as pl
from jax.experimental.pallas import tpu as pltpu
from jax.sharding import PartitionSpec as P

QUERY_HEADS = 16
KEY_VALUE_HEADS = 4
GROUP = QUERY_HEADS // KEY_VALUE_HEADS
HEAD_WIDTH = 128
ROWS = 64
KV = KEY_VALUE_HEADS * HEAD_WIDTH
WIDE = QUERY_HEADS * HEAD_WIDTH
REACH = 3
SPAN = (REACH + 1) * ROWS
SCALE = 1.0 / math.sqrt(HEAD_WIDTH)
EXP2_SCALE = SCALE * math.log2(math.e)
MASKED = -1e30
FAR = 1 << 30
ENTRIES = 7
VMEM_LIMIT = 24 * 1024 * 1024

TABLE_A, TABLE_B, TABLE_C = 4, 5, 6


def send(array, even_by, odd_by):
    count = lax.axis_size("ctx")
    pairs = [(i, (i + (odd_by if i % 2 else even_by)) % count) for i in range(count)]
    return lax.ppermute(array, "ctx", pairs)


def fold_flags(chip_base, slots, live):
    half = slots.shape[0] // 2
    middle_even = slots[chip_base] == half - 1
    middle_odd = slots[chip_base + 2] == half - 1
    far_middle = jnp.logical_and(middle_odd, live[REACH, half] == 1)
    return middle_even, far_middle


def attention_kernel(
    leading,
    place,
    slots,
    live,
    row_start,
    q_own,
    q_sib,
    g_own,
    g_sib,
    kv_own,
    kv_sib,
    kv_a,
    kv_b,
    *refs,
):
    if leading:
        dq, total, table, q_work, g_work, bias = refs
    else:
        kv_c, dq_in, total_in, dq_first, dq_rest, out_own, out_sib, out_a, out_b, out_c = (
            refs[:10]
        )
        dq, total, table, q_work, g_work, bias = refs[10:]
    me = place[0]
    count = slots.shape[0] // 2
    parity = lax.rem(me, 2)
    is_odd = parity == 1
    chip_base = 2 * (me - parity)
    middle_even, far_middle = fold_flags(chip_base, slots, live)

    own_at = pl.multiple_of(parity * 128, 128)
    sib_at = pl.multiple_of((1 - parity) * 128, 128)
    table[pl.ds(own_at, 128), :] = kv_own[...]
    table[pl.ds(sib_at, 128), :] = kv_sib[...]
    table[TABLE_A * ROWS : TABLE_B * ROWS, :] = kv_a[...]
    table[TABLE_B * ROWS : TABLE_C * ROWS, :] = kv_b[...]

    toward = jnp.where(is_odd, 1, -1)
    near_a = lax.rem(me + 2 * toward + count, count)
    near_b = lax.rem(me + toward + count, count)
    far = lax.rem(me + 3 * toward + count, count)
    passed_odd = jnp.logical_and(is_odd, slots[2 * near_a] == count - 1)
    passed_even = jnp.logical_and(is_odd, slots[2 * near_b] == count - 1)
    entry_ids = [slots[chip_base + e] for e in range(4)]
    entry_ids += [slots[2 * near_a + parity], slots[2 * near_b + parity]]
    if not leading:
        table[TABLE_C * ROWS :, :] = kv_c[...]
        passed_middle = jnp.logical_or(passed_odd, passed_even)
        entry_ids += [jnp.where(passed_middle, count - 1, slots[2 * far + parity])]

    own_row = pl.multiple_of(parity * ROWS, ROWS)
    other_row = pl.multiple_of((1 - parity) * ROWS, ROWS)
    other_entry = jnp.where(middle_even, 1 + parity, jnp.where(is_odd, 1, 2))
    slot = 0 if leading else 1

    @pl.when(middle_even)
    def _():
        q_work[slot] = q_own[pl.ds(other_row, ROWS), :]
        g_work[slot] = g_own[pl.ds(other_row, ROWS), :]

    @pl.when(jnp.logical_not(middle_even))
    def _():
        q_work[slot] = q_sib[pl.ds(own_row, ROWS), :]
        g_work[slot] = g_sib[pl.ds(own_row, ROWS), :]

    if leading:
        total[...] = jnp.zeros_like(total)

        @pl.when(far_middle)
        def _():
            q_work[1] = q_sib[ROWS:, :]
            g_work[1] = g_sib[ROWS:, :]

        entries = (other_entry, 3)
        first = jnp.where(passed_even, 1, 0)
        last = jnp.where(jnp.logical_and(far_middle, jnp.logical_not(is_odd)), 2, 1)
    else:
        total[...] = total_in[...]
        q_work[0] = q_own[pl.ds(own_row, ROWS), :]
        g_work[0] = g_own[pl.ds(own_row, ROWS), :]
        entries = (3 * parity, other_entry)
        first = jnp.where(jnp.logical_and(far_middle, is_odd), 1, 0)
        last = jnp.where(passed_even, 2, 1)

    def work_item(item, carry):
        entry = jnp.where(item == 0, *entries)
        query_id = slots[chip_base + entry]
        indices = []
        key_base = []
        for distance in range(REACH + 1):
            key_id = query_id - distance
            is_live = jnp.logical_and(key_id >= 0, live[distance, query_id] == 1)
            index = jnp.int32(0)
            found = jnp.bool_(False)
            for e in range(len(entry_ids)):
                match = entry_ids[e] == key_id
                index = jnp.where(match, e, index)
                found = jnp.logical_or(found, match)
            ok = jnp.logical_and(is_live, found)
            indices.append(pl.multiple_of(jnp.where(ok, index, 0) * ROWS, ROWS))
            key_base.append(jnp.where(ok, key_id * ROWS, FAR))
        lane = lax.broadcasted_iota(jnp.int32, (1, GROUP * ROWS), 1)
        query_pos = query_id * ROWS + lax.rem(lane, ROWS)
        query_start = row_start[pl.ds(entry, 1), :]
        sub = lax.broadcasted_iota(jnp.int32, (ROWS, GROUP * ROWS), 0)
        for distance in range(REACH + 1):
            key_pos = sub + key_base[distance]
            allowed = jnp.logical_and(key_pos <= query_pos, key_pos >= query_start)
            bias[distance * ROWS : (distance + 1) * ROWS, :] = jnp.where(
                allowed, 0.0, MASKED
            )
        for g in range(KEY_VALUE_HEADS):
            kcols = slice(g * HEAD_WIDTH, (g + 1) * HEAD_WIDTH)
            vcols = slice(KV + g * HEAD_WIDTH, KV + (g + 1) * HEAD_WIDTH)
            heads = [
                slice((GROUP * g + j) * HEAD_WIDTH, (GROUP * g + j + 1) * HEAD_WIDTH)
                for j in range(GROUP)
            ]
            keys = jnp.concatenate([table[pl.ds(i, ROWS), kcols] for i in indices], 0)
            values = jnp.concatenate([table[pl.ds(i, ROWS), vcols] for i in indices], 0)
            q = jnp.concatenate([q_work[item, :, h] for h in heads], 0)
            grad = jnp.concatenate([g_work[item, :, h] for h in heads], 0)
            nt = (((1,), (1,)), ((), ()))
            raw = lax.dot_general(keys, q, nt, preferred_element_type=jnp.float32)
            raw = raw + bias[...]
            top = jnp.max(raw, axis=0, keepdims=True)
            weights = jnp.exp2((raw - top) * EXP2_SCALE)
            probs = weights * (1.0 / jnp.sum(weights, axis=0, keepdims=True))
            grad_scores = lax.dot_general(
                values, grad, nt, preferred_element_type=jnp.float32
            )
            offset = jnp.sum(probs * grad_scores, axis=0, keepdims=True)
            score_low = (probs * (grad_scores - offset)).astype(jnp.bfloat16)
            value_add = jnp.dot(
                probs.astype(jnp.bfloat16), grad, preferred_element_type=jnp.float32
            )
            key_add = jnp.dot(score_low, q, preferred_element_type=jnp.float32)
            query_add = lax.dot_general(
                score_low,
                keys,
                (((0,), (0,)), ((), ())),
                preferred_element_type=jnp.float32,
            )
            query_add = (query_add * SCALE).astype(jnp.bfloat16)
            for j, h in enumerate(heads):
                dq[item, :, h] = query_add[j * ROWS : (j + 1) * ROWS]
            for distance in range(REACH + 1):
                part = slice(distance * ROWS, (distance + 1) * ROWS)
                at = pl.ds(indices[distance], ROWS)
                total[at, kcols] += key_add[part] * SCALE
                total[at, vcols] += value_add[part]
        return carry

    lax.fori_loop(first, last, work_item, 0)
    if leading:
        return
    low = jnp.bfloat16
    dq_first[...] = dq[0]
    dq_rest[...] = dq_in[...]

    @pl.when(passed_even)
    def _():
        dq_rest[0] = dq[1]

    out_own[...] = total[pl.ds(own_at, 128), :]
    out_sib[...] = total[pl.ds(sib_at, 128), :]
    out_a[...] = total[TABLE_A * ROWS : TABLE_B * ROWS, :].astype(low)
    out_b[...] = total[TABLE_B * ROWS : TABLE_C * ROWS, :]
    out_c[...] = total[TABLE_C * ROWS :, :].astype(low)


def pack_kernel(
    place,
    slots_hbm,
    docs_hbm,
    keys,
    values,
    queries,
    grads,
    both,
    chain,
    cross,
    q_own,
    g_own,
    row_start,
    fold,
    slots,
    docs,
    sems,
):
    parity = lax.rem(place[0], 2)
    own_rows = pl.ds(pl.multiple_of(parity * ROWS, ROWS), ROWS)
    other_rows = pl.ds(pl.multiple_of((1 - parity) * ROWS, ROWS), ROWS)
    copies = [
        pltpu.make_async_copy(source, target, sems.at[n])
        for n, (source, target) in enumerate(
            [
                (slots_hbm, slots),
                (docs_hbm, docs),
                (keys.at[other_rows, :], cross.at[:, pl.ds(0, KV)]),
                (values.at[other_rows, :], cross.at[:, pl.ds(KV, KV)]),
                (keys.at[own_rows, :], chain.at[:, pl.ds(0, KV)]),
                (values.at[own_rows, :], chain.at[:, pl.ds(KV, KV)]),
                (keys, both.at[:, pl.ds(0, KV)]),
                (values, both.at[:, pl.ds(KV, KV)]),
                (queries, q_own),
                (grads, g_own),
            ]
        )
    ]
    for copy in copies:
        copy.start()
    copies[0].wait()
    copies[1].wait()
    middle = slots.shape[0] // 2 - 1
    chip_base = 2 * (place[0] - parity)
    holder = jnp.where(
        slots[chip_base + 2] == middle, 1, jnp.where(slots[chip_base] == middle, 2, 0)
    )
    fold[...] = jnp.full(fold.shape, jnp.where(parity == 1, holder, 0))
    count = docs.shape[0]
    lane = lax.rem(lax.broadcasted_iota(jnp.int32, (1, GROUP * ROWS), 1), ROWS)
    for entry in range(4):
        first = slots[chip_base + entry] * ROWS

        def halve(_, bounds):
            low, high = bounds
            middle = (low + high) // 2
            begun = docs[middle] <= first
            inside = low < high
            return (
                jnp.where(jnp.logical_and(inside, begun), middle + 1, low),
                jnp.where(jnp.logical_and(inside, jnp.logical_not(begun)), middle, high),
            )

        begun, _ = lax.fori_loop(
            0, count.bit_length(), halve, (jnp.int32(1), jnp.int32(count))
        )

        def more(state):
            index, _ = state
            start = docs[jnp.minimum(index, count - 1)]
            return jnp.logical_and(index < count, start < first + ROWS)

        def step(state):
            index, row = state
            start = docs[index]
            return index + 1, jnp.where(lane + first >= start, start, row)

        _, row = lax.while_loop(
            more, step, (begun, jnp.full((1, GROUP * ROWS), docs[begun - 1]))
        )
        row_start[pl.ds(entry, 1), :] = row
    for copy in copies[2:]:
        copy.wait()


def early_kernel(place, slots, live, first, rest, theirs, own, back_c, out, acc):
    me = place[0]
    parity = lax.rem(me, 2)
    is_odd = parity == 1
    chip_base = 2 * (me - parity)
    middle_even, far_middle = fold_flags(chip_base, slots, live)
    own_row = pl.multiple_of(parity * ROWS, ROWS)
    other_row = pl.multiple_of((1 - parity) * ROWS, ROWS)
    moved = jnp.logical_and(far_middle, is_odd)

    @pl.when(moved)
    def _():
        out[pl.ds(own_row, ROWS), :] = theirs[1]

    @pl.when(jnp.logical_not(moved))
    def _():
        out[pl.ds(own_row, ROWS), :] = first[...]

    @pl.when(middle_even)
    def _():
        out[pl.ds(other_row, ROWS), :] = rest[0]

    @pl.when(jnp.logical_not(middle_even))
    def _():
        out[pl.ds(other_row, ROWS), :] = theirs[0]

    acc[...] = own[...]

    @pl.when(jnp.logical_and(is_odd, slots[chip_base + 2] == slots.shape[0] // 2 - 1))
    def _():
        acc[:ROWS, :] += back_c[...].astype(jnp.float32)


def sum_kernel(place, own, sib, back_a, back_b, key_out, value_out):
    parity = lax.rem(place[0], 2)
    for at, back in ((parity, back_a), (1 - parity, back_b)):
        rows = pl.ds(pl.multiple_of(at * ROWS, ROWS), ROWS)
        for out, columns in ((key_out, slice(0, KV)), (value_out, slice(KV, 2 * KV))):
            out[rows, :] = (
                own[rows, columns]
                + sib[rows, columns].astype(jnp.float32)
                + back[:, columns].astype(jnp.float32)
            ).astype(jnp.bfloat16)


def vmem(count):
    return [pl.BlockSpec(memory_space=pltpu.VMEM)] * count


def in_hbm(array):
    return pltpu.with_memory_space_constraint(array, pltpu.HBM)


def hbm(count):
    return [pl.BlockSpec(memory_space=pltpu.HBM)] * count


def smem(count):
    return [pl.BlockSpec(memory_space=pltpu.SMEM)] * count


def shards(
    queries,
    key_rows_slotted,
    value_rows_slotted,
    output_gradient,
    slot_to_block,
    doc_starts,
    block_live,
):
    me = lax.axis_index("ctx")
    place = me.astype(jnp.int32).reshape(1)
    live = block_live.T
    params = pltpu.CompilerParams(vmem_limit_bytes=VMEM_LIMIT)

    bf16 = functools.partial(jax.ShapeDtypeStruct, dtype=jnp.bfloat16)
    kv, kv_chain, kv_cross, q_own, g_own, row_start, fold = pl.pallas_call(
        pack_kernel,
        out_shape=(
            bf16((2 * ROWS, 2 * KV)),
            bf16((ROWS, 2 * KV)),
            bf16((ROWS, 2 * KV)),
            bf16((2 * ROWS, WIDE)),
            bf16((2 * ROWS, WIDE)),
            jax.ShapeDtypeStruct((4, GROUP * ROWS), jnp.int32),
            jax.ShapeDtypeStruct((8, 128), jnp.int32),
        ),
        in_specs=smem(1) + hbm(6),
        out_specs=tuple(vmem(7)),
        scratch_shapes=[
            pltpu.SMEM(slot_to_block.shape, jnp.int32),
            pltpu.SMEM(doc_starts.shape, jnp.int32),
            pltpu.SemaphoreType.DMA((10,)),
        ],
        compiler_params=params,
        name="prepare",
    )(
        place,
        in_hbm(slot_to_block),
        in_hbm(doc_starts),
        in_hbm(key_rows_slotted),
        in_hbm(value_rows_slotted),
        in_hbm(queries),
        in_hbm(output_gradient),
    )
    kv_a = send(kv_chain, 2, -2)
    kv_b = send(kv_cross, -1, 1)
    kv_sib = send(kv, 1, -1)
    q_sib = send(queries, 1, -1)
    g_sib = send(output_gradient, 1, -1)
    which = fold[:1, :1]
    passed = jnp.where(which == 1, kv[:ROWS], jnp.where(which == 2, kv_sib[:ROWS], kv_b))
    kv_c = send(passed, 2, -2)

    work = [
        pltpu.VMEM((2, ROWS, WIDE), jnp.bfloat16),
        pltpu.VMEM((ENTRIES * ROWS, 2 * KV), jnp.bfloat16),
        pltpu.VMEM((2, ROWS, WIDE), jnp.bfloat16),
        pltpu.VMEM((2, ROWS, WIDE), jnp.bfloat16),
        pltpu.VMEM((SPAN, GROUP * ROWS), jnp.float32),
    ]
    sums = jax.ShapeDtypeStruct((ENTRIES * ROWS, 2 * KV), jnp.float32)
    operands = (
        place,
        in_hbm(slot_to_block),
        live,
        row_start,
        q_own,
        q_sib,
        g_own,
        g_sib,
        kv,
        kv_sib,
        kv_a,
        kv_b,
    )
    dq_leading, total = pl.pallas_call(
        functools.partial(attention_kernel, True),
        out_shape=(bf16((2, ROWS, WIDE)), sums),
        in_specs=smem(3) + vmem(9),
        out_specs=tuple(vmem(2)),
        scratch_shapes=work[1:],
        compiler_params=params,
        cost_estimate=pl.CostEstimate(
            flops=1 << 36, bytes_accessed=1 << 22, transcendentals=1 << 18
        ),
        name="attention_leading",
    )(*operands)
    dq_first, dq_rest, own, sib, out_a, out_b, out_c = pl.pallas_call(
        functools.partial(attention_kernel, False),
        out_shape=(
            bf16((ROWS, WIDE)),
            bf16((2, ROWS, WIDE)),
            jax.ShapeDtypeStruct((2 * ROWS, 2 * KV), jnp.float32),
            jax.ShapeDtypeStruct((2 * ROWS, 2 * KV), jnp.float32),
            bf16((ROWS, 2 * KV)),
            jax.ShapeDtypeStruct((ROWS, 2 * KV), jnp.float32),
            bf16((ROWS, 2 * KV)),
        ),
        in_specs=smem(3) + vmem(12),
        out_specs=tuple(vmem(7)),
        scratch_shapes=work[:1] + [pltpu.VMEM(sums.shape, jnp.float32)] + work[1:],
        compiler_params=params,
        name="attention_last",
    )(*operands, kv_c, dq_leading, total)

    back_c = send(out_c, -2, 2)
    back_a = send(out_a, -2, 2)
    passing = back_c.astype(jnp.float32)
    back_b = send((out_b + jnp.where(which == 0, passing, 0)).astype(jnp.bfloat16), -1, 1)
    middle_part = jnp.pad(jnp.where(which == 2, passing, 0), ((0, ROWS), (0, 0)))
    back_sib = send((sib + middle_part).astype(jnp.bfloat16), 1, -1)
    dq_sib = send(dq_rest, 1, -1)

    query_grad, own = pl.pallas_call(
        early_kernel,
        out_shape=(
            bf16((2 * ROWS, WIDE)),
            jax.ShapeDtypeStruct((2 * ROWS, 2 * KV), jnp.float32),
        ),
        in_specs=smem(3) + vmem(5),
        out_specs=tuple(vmem(2)),
        compiler_params=params,
        cost_estimate=pl.CostEstimate(
            flops=1 << 36, bytes_accessed=1 << 22, transcendentals=0
        ),
        name="query_gradient_rows",
    )(
        place,
        in_hbm(slot_to_block),
        live,
        dq_first,
        dq_rest,
        dq_sib,
        own,
        back_c,
    )

    key_gradient, value_gradient = pl.pallas_call(
        sum_kernel,
        out_shape=(bf16((2 * ROWS, KV)), bf16((2 * ROWS, KV))),
        in_specs=smem(1) + vmem(4),
        out_specs=tuple(vmem(2)),
        compiler_params=params,
        name="key_value_gradient_sum",
    )(place, own, back_sib, back_a, back_b)
    return query_grad, key_gradient, value_gradient


def solution(mesh):
    rows = P(("section", "ctx"), None)
    return jax.shard_map(
        shards,
        mesh=mesh,
        in_specs=(rows, rows, rows, rows, P("section"), P("section"), P("section", None)),
        out_specs=(rows, rows, rows),
        check_vma=False,
    )
```

```python
import functools
import math

import jax
import jax.numpy as jnp
from jax import lax
from jax.experimental import pallas as pl
from jax.experimental.pallas import tpu as pltpu
from jax.sharding import PartitionSpec as P

QUERY_HEADS = 16
KEY_VALUE_HEADS = 4
GROUP = QUERY_HEADS // KEY_VALUE_HEADS
HEAD_WIDTH = 128
ROWS = 64
KV = KEY_VALUE_HEADS * HEAD_WIDTH
WIDE = QUERY_HEADS * HEAD_WIDTH
REACH = 3
SPAN = (REACH + 1) * ROWS
SCALE = 1.0 / math.sqrt(HEAD_WIDTH)
EXP2_SCALE = SCALE * math.log2(math.e)
MASKED = -1e30
FAR = 1 << 30
ENTRIES = 7
VMEM_LIMIT = 24 * 1024 * 1024

TABLE_A, TABLE_B, TABLE_C = 4, 5, 6


def send(array, even_by, odd_by):
    count = lax.axis_size("ctx")
    pairs = [(i, (i + (odd_by if i % 2 else even_by)) % count) for i in range(count)]
    return lax.ppermute(array, "ctx", pairs)


def send_pairs(array, steps):
    count = lax.axis_size("ctx")
    pairs = [(i, (i + steps[i % 4]) % count) for i in range(count) if steps[i % 4]]
    return lax.ppermute(array, "ctx", pairs)


NEAR_EVEN, NEAR_ODD = (None, 1, -1, None), (-1, None, None, 1)
PASS_EVEN, PASS_ODD = (2, None, None, -2), (None, -2, 2, None)


def fold_flags(chip_base, slots, live):
    half = slots.shape[0] // 2
    middle_even = slots[chip_base] == half - 1
    middle_odd = slots[chip_base + 2] == half - 1
    far_middle = jnp.logical_and(middle_odd, live[REACH, half] == 1)
    return middle_even, far_middle


def attention_kernel(
    leading,
    place,
    slots,
    live,
    row_start,
    q_own,
    q_sib,
    g_own,
    g_sib,
    kv_own,
    kv_sib,
    kv_a,
    kv_b_even,
    kv_b_odd,
    *refs,
):
    if leading:
        dq, total, table, q_work, g_work, bias = refs
    else:
        kv_c_even, kv_c_odd, dq_in, total_in = refs[:4]
        dq_first, dq_rest, out_own, out_sib, out_a, out_b, out_c = refs[4:11]
        dq, total, table, q_work, g_work, bias = refs[11:]
    me = place[0]
    count = slots.shape[0] // 2
    parity = lax.rem(me, 2)
    is_odd = parity == 1
    chip_base = 2 * (me - parity)
    middle_even, far_middle = fold_flags(chip_base, slots, live)

    own_at = pl.multiple_of(parity * 128, 128)
    sib_at = pl.multiple_of((1 - parity) * 128, 128)
    table[pl.ds(own_at, 128), :] = kv_own[...]
    table[pl.ds(sib_at, 128), :] = kv_sib[...]
    table[TABLE_A * ROWS : TABLE_B * ROWS, :] = kv_a[...]
    inner = jnp.logical_or(lax.rem(me, 4) == 1, lax.rem(me, 4) == 2)

    @pl.when(inner)
    def _():
        table[TABLE_B * ROWS : TABLE_C * ROWS, :] = kv_b_even[...]
        if not leading:
            table[TABLE_C * ROWS :, :] = kv_c_even[...]

    @pl.when(jnp.logical_not(inner))
    def _():
        table[TABLE_B * ROWS : TABLE_C * ROWS, :] = kv_b_odd[...]
        if not leading:
            table[TABLE_C * ROWS :, :] = kv_c_odd[...]


    toward = jnp.where(is_odd, 1, -1)
    near_a = lax.rem(me + 2 * toward + count, count)
    near_b = lax.rem(me + toward + count, count)
    far = lax.rem(me + 3 * toward + count, count)
    passed_odd = jnp.logical_and(is_odd, slots[2 * near_a] == count - 1)
    passed_even = jnp.logical_and(is_odd, slots[2 * near_b] == count - 1)
    entry_ids = [slots[chip_base + e] for e in range(4)]
    entry_ids += [slots[2 * near_a + parity], slots[2 * near_b + parity]]
    if not leading:
        passed_middle = jnp.logical_or(passed_odd, passed_even)
        entry_ids += [jnp.where(passed_middle, count - 1, slots[2 * far + parity])]

    own_row = pl.multiple_of(parity * ROWS, ROWS)
    other_row = pl.multiple_of((1 - parity) * ROWS, ROWS)
    other_entry = jnp.where(middle_even, 1 + parity, jnp.where(is_odd, 1, 2))
    slot = 0 if leading else 1

    @pl.when(middle_even)
    def _():
        q_work[slot] = q_own[pl.ds(other_row, ROWS), :]
        g_work[slot] = g_own[pl.ds(other_row, ROWS), :]

    @pl.when(jnp.logical_not(middle_even))
    def _():
        q_work[slot] = q_sib[pl.ds(own_row, ROWS), :]
        g_work[slot] = g_sib[pl.ds(own_row, ROWS), :]

    if leading:
        total[...] = jnp.zeros_like(total)

        @pl.when(far_middle)
        def _():
            q_work[1] = q_sib[ROWS:, :]
            g_work[1] = g_sib[ROWS:, :]

        entries = (other_entry, 3)
        first = jnp.where(passed_even, 1, 0)
        last = jnp.where(jnp.logical_and(far_middle, jnp.logical_not(is_odd)), 2, 1)
    else:
        total[...] = total_in[...]
        q_work[0] = q_own[pl.ds(own_row, ROWS), :]
        g_work[0] = g_own[pl.ds(own_row, ROWS), :]
        entries = (3 * parity, other_entry)
        first = jnp.where(jnp.logical_and(far_middle, is_odd), 1, 0)
        last = jnp.where(passed_even, 2, 1)

    def work_item(item, carry):
        entry = jnp.where(item == 0, *entries)
        query_id = slots[chip_base + entry]
        indices = []
        key_base = []
        for distance in range(REACH + 1):
            key_id = query_id - distance
            is_live = jnp.logical_and(key_id >= 0, live[distance, query_id] == 1)
            index = jnp.int32(0)
            found = jnp.bool_(False)
            for e in range(len(entry_ids)):
                match = entry_ids[e] == key_id
                index = jnp.where(match, e, index)
                found = jnp.logical_or(found, match)
            ok = jnp.logical_and(is_live, found)
            indices.append(pl.multiple_of(jnp.where(ok, index, 0) * ROWS, ROWS))
            key_base.append(jnp.where(ok, key_id * ROWS, FAR))
        lane = lax.broadcasted_iota(jnp.int32, (1, GROUP * ROWS), 1)
        query_pos = query_id * ROWS + lax.rem(lane, ROWS)
        query_start = row_start[pl.ds(entry, 1), :]
        sub = lax.broadcasted_iota(jnp.int32, (ROWS, GROUP * ROWS), 0)
        for distance in range(REACH + 1):
            key_pos = sub + key_base[distance]
            allowed = jnp.logical_and(key_pos <= query_pos, key_pos >= query_start)
            bias[distance * ROWS : (distance + 1) * ROWS, :] = jnp.where(
                allowed, 0.0, MASKED
            )
        for g in range(KEY_VALUE_HEADS):
            kcols = slice(g * HEAD_WIDTH, (g + 1) * HEAD_WIDTH)
            vcols = slice(KV + g * HEAD_WIDTH, KV + (g + 1) * HEAD_WIDTH)
            heads = [
                slice((GROUP * g + j) * HEAD_WIDTH, (GROUP * g + j + 1) * HEAD_WIDTH)
                for j in range(GROUP)
            ]
            keys = jnp.concatenate([table[pl.ds(i, ROWS), kcols] for i in indices], 0)
            values = jnp.concatenate([table[pl.ds(i, ROWS), vcols] for i in indices], 0)
            q = jnp.concatenate([q_work[item, :, h] for h in heads], 0)
            grad = jnp.concatenate([g_work[item, :, h] for h in heads], 0)
            nt = (((1,), (1,)), ((), ()))
            raw = lax.dot_general(keys, q, nt, preferred_element_type=jnp.float32)
            raw = raw + bias[...]
            top = jnp.max(raw, axis=0, keepdims=True)
            weights = jnp.exp2((raw - top) * EXP2_SCALE)
            probs = weights * (1.0 / jnp.sum(weights, axis=0, keepdims=True))
            grad_scores = lax.dot_general(
                values, grad, nt, preferred_element_type=jnp.float32
            )
            offset = jnp.sum(probs * grad_scores, axis=0, keepdims=True)
            score_low = (probs * (grad_scores - offset)).astype(jnp.bfloat16)
            value_add = jnp.dot(
                probs.astype(jnp.bfloat16), grad, preferred_element_type=jnp.float32
            )
            key_add = jnp.dot(score_low, q, preferred_element_type=jnp.float32)
            query_add = lax.dot_general(
                score_low,
                keys,
                (((0,), (0,)), ((), ())),
                preferred_element_type=jnp.float32,
            )
            query_add = (query_add * SCALE).astype(jnp.bfloat16)
            for j, h in enumerate(heads):
                dq[item, :, h] = query_add[j * ROWS : (j + 1) * ROWS]
            for distance in range(REACH + 1):
                part = slice(distance * ROWS, (distance + 1) * ROWS)
                at = pl.ds(indices[distance], ROWS)
                total[at, kcols] += key_add[part] * SCALE
                total[at, vcols] += value_add[part]
        return carry

    lax.fori_loop(first, last, work_item, 0)
    if leading:
        return
    low = jnp.bfloat16
    dq_first[...] = dq[0]
    dq_rest[...] = dq_in[...]

    @pl.when(passed_even)
    def _():
        dq_rest[0] = dq[1]

    out_own[...] = total[pl.ds(own_at, 128), :]
    out_sib[...] = total[pl.ds(sib_at, 128), :]
    out_a[...] = total[TABLE_A * ROWS : TABLE_B * ROWS, :].astype(low)
    out_b[...] = total[TABLE_B * ROWS : TABLE_C * ROWS, :]
    out_c[...] = total[TABLE_C * ROWS :, :].astype(low)


def pack_kernel(
    place,
    slots_hbm,
    docs_hbm,
    keys,
    values,
    queries,
    grads,
    both,
    chain,
    cross,
    q_own,
    g_own,
    row_start,
    fold,
    slots,
    docs,
    sems,
):
    parity = lax.rem(place[0], 2)
    own_rows = pl.ds(pl.multiple_of(parity * ROWS, ROWS), ROWS)
    other_rows = pl.ds(pl.multiple_of((1 - parity) * ROWS, ROWS), ROWS)
    copies = [
        pltpu.make_async_copy(source, target, sems.at[n])
        for n, (source, target) in enumerate(
            [
                (slots_hbm, slots),
                (docs_hbm, docs),
                (keys.at[other_rows, :], cross.at[:, pl.ds(0, KV)]),
                (values.at[other_rows, :], cross.at[:, pl.ds(KV, KV)]),
                (keys.at[own_rows, :], chain.at[:, pl.ds(0, KV)]),
                (values.at[own_rows, :], chain.at[:, pl.ds(KV, KV)]),
                (keys, both.at[:, pl.ds(0, KV)]),
                (values, both.at[:, pl.ds(KV, KV)]),
                (queries, q_own),
                (grads, g_own),
            ]
        )
    ]
    for copy in copies:
        copy.start()
    copies[0].wait()
    copies[1].wait()
    middle = slots.shape[0] // 2 - 1
    chip_base = 2 * (place[0] - parity)
    holder = jnp.where(
        slots[chip_base + 2] == middle, 1, jnp.where(slots[chip_base] == middle, 2, 0)
    )
    fold[...] = jnp.full(fold.shape, jnp.where(parity == 1, holder, 0))
    count = docs.shape[0]
    lane = lax.rem(lax.broadcasted_iota(jnp.int32, (1, GROUP * ROWS), 1), ROWS)
    for entry in range(4):
        first = slots[chip_base + entry] * ROWS

        def halve(_, bounds):
            low, high = bounds
            middle = (low + high) // 2
            begun = docs[middle] <= first
            inside = low < high
            return (
                jnp.where(jnp.logical_and(inside, begun), middle + 1, low),
                jnp.where(jnp.logical_and(inside, jnp.logical_not(begun)), middle, high),
            )

        begun, _ = lax.fori_loop(
            0, count.bit_length(), halve, (jnp.int32(1), jnp.int32(count))
        )

        def more(state):
            index, _ = state
            start = docs[jnp.minimum(index, count - 1)]
            return jnp.logical_and(index < count, start < first + ROWS)

        def step(state):
            index, row = state
            start = docs[index]
            return index + 1, jnp.where(lane + first >= start, start, row)

        _, row = lax.while_loop(
            more, step, (begun, jnp.full((1, GROUP * ROWS), docs[begun - 1]))
        )
        row_start[pl.ds(entry, 1), :] = row
    for copy in copies[2:]:
        copy.wait()


def early_kernel(place, slots, live, first, rest, theirs, own, back_c, out, acc):
    me = place[0]
    parity = lax.rem(me, 2)
    is_odd = parity == 1
    chip_base = 2 * (me - parity)
    middle_even, far_middle = fold_flags(chip_base, slots, live)
    own_row = pl.multiple_of(parity * ROWS, ROWS)
    other_row = pl.multiple_of((1 - parity) * ROWS, ROWS)
    moved = jnp.logical_and(far_middle, is_odd)

    @pl.when(moved)
    def _():
        out[pl.ds(own_row, ROWS), :] = theirs[1]

    @pl.when(jnp.logical_not(moved))
    def _():
        out[pl.ds(own_row, ROWS), :] = first[...]

    @pl.when(middle_even)
    def _():
        out[pl.ds(other_row, ROWS), :] = rest[0]

    @pl.when(jnp.logical_not(middle_even))
    def _():
        out[pl.ds(other_row, ROWS), :] = theirs[0]

    acc[...] = own[...]

    @pl.when(jnp.logical_and(is_odd, slots[chip_base + 2] == slots.shape[0] // 2 - 1))
    def _():
        acc[:ROWS, :] += back_c[...].astype(jnp.float32)


def sum_kernel(place, own, sib, back_a, back_b, key_out, value_out):
    parity = lax.rem(place[0], 2)
    for at, back in ((parity, back_a), (1 - parity, back_b)):
        rows = pl.ds(pl.multiple_of(at * ROWS, ROWS), ROWS)
        for out, columns in ((key_out, slice(0, KV)), (value_out, slice(KV, 2 * KV))):
            out[rows, :] = (
                own[rows, columns]
                + sib[rows, columns].astype(jnp.float32)
                + back[:, columns].astype(jnp.float32)
            ).astype(jnp.bfloat16)


def vmem(count):
    return [pl.BlockSpec(memory_space=pltpu.VMEM)] * count


def in_hbm(array):
    return pltpu.with_memory_space_constraint(array, pltpu.HBM)


def hbm(count):
    return [pl.BlockSpec(memory_space=pltpu.HBM)] * count


def smem(count):
    return [pl.BlockSpec(memory_space=pltpu.SMEM)] * count


def shards(
    queries,
    key_rows_slotted,
    value_rows_slotted,
    output_gradient,
    slot_to_block,
    doc_starts,
    block_live,
):
    me = lax.axis_index("ctx")
    place = me.astype(jnp.int32).reshape(1)
    live = block_live.T
    params = pltpu.CompilerParams(vmem_limit_bytes=VMEM_LIMIT)

    bf16 = functools.partial(jax.ShapeDtypeStruct, dtype=jnp.bfloat16)
    kv, kv_chain, kv_cross, q_own, g_own, row_start, fold = pl.pallas_call(
        pack_kernel,
        out_shape=(
            bf16((2 * ROWS, 2 * KV)),
            bf16((ROWS, 2 * KV)),
            bf16((ROWS, 2 * KV)),
            bf16((2 * ROWS, WIDE)),
            bf16((2 * ROWS, WIDE)),
            jax.ShapeDtypeStruct((4, GROUP * ROWS), jnp.int32),
            jax.ShapeDtypeStruct((8, 128), jnp.int32),
        ),
        in_specs=smem(1) + hbm(6),
        out_specs=tuple(vmem(7)),
        scratch_shapes=[
            pltpu.SMEM(slot_to_block.shape, jnp.int32),
            pltpu.SMEM(doc_starts.shape, jnp.int32),
            pltpu.SemaphoreType.DMA((10,)),
        ],
        compiler_params=params,
        name="prepare",
    )(
        place,
        in_hbm(slot_to_block),
        in_hbm(doc_starts),
        in_hbm(key_rows_slotted),
        in_hbm(value_rows_slotted),
        in_hbm(queries),
        in_hbm(output_gradient),
    )
    kv_sib = send(kv, 1, -1)
    q_sib = send(queries, 1, -1)
    g_sib = send(output_gradient, 1, -1)
    kv_b_even = send_pairs(kv_cross, NEAR_EVEN)
    kv_a = send(kv_chain, 2, -2)
    which = fold[:1, :1]
    middle_block = jnp.where(which == 1, kv[:ROWS], kv_sib[:ROWS])
    passed, kv_cross = lax.optimization_barrier(
        (jnp.where(which > 0, middle_block, kv_b_even), kv_cross)
    )
    kv_c_odd = send_pairs(passed, PASS_ODD)
    kv_b_odd = send_pairs(kv_cross, NEAR_ODD)
    kv_c_odd, kv_b_odd, kv_a = lax.optimization_barrier((kv_c_odd, kv_b_odd, kv_a))
    kv_c_even = send_pairs(jnp.where(which > 0, middle_block, kv_b_odd), PASS_EVEN)

    work = [
        pltpu.VMEM((2, ROWS, WIDE), jnp.bfloat16),
        pltpu.VMEM((ENTRIES * ROWS, 2 * KV), jnp.bfloat16),
        pltpu.VMEM((2, ROWS, WIDE), jnp.bfloat16),
        pltpu.VMEM((2, ROWS, WIDE), jnp.bfloat16),
        pltpu.VMEM((SPAN, GROUP * ROWS), jnp.float32),
    ]
    sums = jax.ShapeDtypeStruct((ENTRIES * ROWS, 2 * KV), jnp.float32)
    operands = (
        place,
        in_hbm(slot_to_block),
        live,
        row_start,
        q_own,
        q_sib,
        g_own,
        g_sib,
        kv,
        kv_sib,
        kv_a,
        kv_b_even,
        kv_b_odd,
    )
    dq_leading, total = pl.pallas_call(
        functools.partial(attention_kernel, True),
        out_shape=(bf16((2, ROWS, WIDE)), sums),
        in_specs=smem(3) + vmem(10),
        out_specs=tuple(vmem(2)),
        scratch_shapes=work[1:],
        compiler_params=params,
        cost_estimate=pl.CostEstimate(
            flops=1 << 36, bytes_accessed=1 << 22, transcendentals=1 << 18
        ),
        name="attention_leading",
    )(*operands)
    dq_first, dq_rest, own, sib, out_a, out_b, out_c = pl.pallas_call(
        functools.partial(attention_kernel, False),
        out_shape=(
            bf16((ROWS, WIDE)),
            bf16((2, ROWS, WIDE)),
            jax.ShapeDtypeStruct((2 * ROWS, 2 * KV), jnp.float32),
            jax.ShapeDtypeStruct((2 * ROWS, 2 * KV), jnp.float32),
            bf16((ROWS, 2 * KV)),
            jax.ShapeDtypeStruct((ROWS, 2 * KV), jnp.float32),
            bf16((ROWS, 2 * KV)),
        ),
        in_specs=smem(3) + vmem(14),
        out_specs=tuple(vmem(7)),
        scratch_shapes=work[:1] + [pltpu.VMEM(sums.shape, jnp.float32)] + work[1:],
        compiler_params=params,
        name="attention_last",
    )(*operands, kv_c_even, kv_c_odd, dq_leading, total)

    back_c = send(out_c, -2, 2)
    back_a = send(out_a, -2, 2)
    passing = back_c.astype(jnp.float32)
    back_b = send((out_b + jnp.where(which == 0, passing, 0)).astype(jnp.bfloat16), -1, 1)
    middle_part = jnp.pad(jnp.where(which == 2, passing, 0), ((0, ROWS), (0, 0)))
    back_sib = send((sib + middle_part).astype(jnp.bfloat16), 1, -1)
    dq_sib = send(dq_rest, 1, -1)

    query_grad, own = pl.pallas_call(
        early_kernel,
        out_shape=(
            bf16((2 * ROWS, WIDE)),
            jax.ShapeDtypeStruct((2 * ROWS, 2 * KV), jnp.float32),
        ),
        in_specs=smem(3) + vmem(5),
        out_specs=tuple(vmem(2)),
        compiler_params=params,
        cost_estimate=pl.CostEstimate(
            flops=1 << 36, bytes_accessed=1 << 22, transcendentals=0
        ),
        name="query_gradient_rows",
    )(
        place,
        in_hbm(slot_to_block),
        live,
        dq_first,
        dq_rest,
        dq_sib,
        own,
        back_c,
    )

    key_gradient, value_gradient = pl.pallas_call(
        sum_kernel,
        out_shape=(bf16((2 * ROWS, KV)), bf16((2 * ROWS, KV))),
        in_specs=smem(1) + vmem(4),
        out_specs=tuple(vmem(2)),
        compiler_params=params,
        name="key_value_gradient_sum",
    )(place, own, back_sib, back_a, back_b)
    return query_grad, key_gradient, value_gradient


def solution(mesh):
    rows = P(("section", "ctx"), None)
    return jax.shard_map(
        shards,
        mesh=mesh,
        in_specs=(rows, rows, rows, rows, P("section"), P("section"), P("section", None)),
        out_specs=(rows, rows, rows),
        check_vma=False,
    )
```

```python
import functools
import math

import jax
import jax.numpy as jnp
from jax import lax
from jax.experimental import pallas as pl
from jax.experimental.pallas import tpu as pltpu
from jax.sharding import PartitionSpec as P

QUERY_HEADS = 16
KEY_VALUE_HEADS = 4
GROUP = QUERY_HEADS // KEY_VALUE_HEADS
HEAD_WIDTH = 128
ROWS = 64
KV = KEY_VALUE_HEADS * HEAD_WIDTH
WIDE = QUERY_HEADS * HEAD_WIDTH
REACH = 3
SPAN = (REACH + 1) * ROWS
SCALE = 1.0 / math.sqrt(HEAD_WIDTH)
EXP2_SCALE = SCALE * math.log2(math.e)
MASKED = -1e30
FAR = 1 << 30
ENTRIES = 8
VMEM_LIMIT = 24 * 1024 * 1024

TABLE_A, TABLE_B, TABLE_C, TABLE_X = 4, 5, 6, 7
PACK_KV = 4 * ROWS
PACK_ROWS = 5 * ROWS


def send(array, even_by, odd_by):
    count = lax.axis_size("ctx")
    steps = [odd_by if i % 2 else even_by for i in range(count)]
    pairs = [(i, (i + by) % count) for i, by in enumerate(steps) if by is not None]
    return lax.ppermute(array, "ctx", pairs)


def fold_flags(chip_base, slots, live):
    half = slots.shape[0] // 2
    middle_even = slots[chip_base] == half - 1
    middle_odd = slots[chip_base + 2] == half - 1
    far_middle = jnp.logical_and(middle_odd, live[REACH, half] == 1)
    return middle_even, far_middle


def attention_kernel(
    place,
    slots,
    live,
    row_start,
    pack_own,
    pack_sib,
    kv_x,
    kv_b,
    kv_c,
    kv_a,
    dq_own,
    out_own,
    out_sib,
    out_a,
    out_b,
    out_c,
    dq,
    total,
    table,
    q_work,
    g_work,
    bias,
):
    me = place[0]
    count = slots.shape[0] // 2
    parity = lax.rem(me, 2)
    is_odd = parity == 1
    chip_base = 2 * (me - parity)
    middle_even, far_middle = fold_flags(chip_base, slots, live)

    own_at = pl.multiple_of(parity * 128, 128)
    sib_at = pl.multiple_of((1 - parity) * 128, 128)
    for at, pack in ((own_at, pack_own), (sib_at, pack_sib)):
        table[pl.ds(at, ROWS), :] = pack[PACK_KV:, : 2 * KV]
        table[pl.ds(at + ROWS, ROWS), :] = pack[PACK_KV:, 2 * KV :]
    for entry, block in (
        (TABLE_A, kv_a),
        (TABLE_B, kv_b),
        (TABLE_C, kv_c),
        (TABLE_X, kv_x),
    ):
        table[entry * ROWS : (entry + 1) * ROWS, :] = block[...]
    total[...] = jnp.zeros_like(total)

    toward = jnp.where(is_odd, 1, -1)
    near_a = lax.rem(me + 2 * toward + count, count)
    near_b = lax.rem(me + toward + count, count)
    far = lax.rem(me + 3 * toward + count, count)
    before_middle = jnp.logical_and(
        is_odd,
        jnp.logical_or(slots[2 * near_a] == count - 1, slots[2 * near_b] == count - 1),
    )
    entry_ids = [slots[chip_base + e] for e in range(4)]
    entry_ids += [slots[2 * i + parity] for i in (near_a, near_b, far)]
    entry_ids += [jnp.where(before_middle, count - 1, -1)]

    own_row = pl.multiple_of(parity * ROWS, ROWS)
    other_row = pl.multiple_of((1 - parity) * ROWS, ROWS)
    grads_at = 2 * ROWS
    q_work[0] = pack_own[pl.ds(own_row, ROWS), :]
    g_work[0] = pack_own[pl.ds(grads_at + own_row, ROWS), :]

    @pl.when(middle_even)
    def _():
        q_work[1] = pack_own[pl.ds(other_row, ROWS), :]
        g_work[1] = pack_own[pl.ds(grads_at + other_row, ROWS), :]

    @pl.when(jnp.logical_not(middle_even))
    def _():
        q_work[1] = pack_sib[pl.ds(own_row, ROWS), :]
        g_work[1] = pack_sib[pl.ds(grads_at + own_row, ROWS), :]

    @pl.when(far_middle)
    def _():
        q_work[2] = pack_sib[ROWS : 2 * ROWS, :]
        g_work[2] = pack_sib[grads_at + ROWS : grads_at + 2 * ROWS, :]

    first = jnp.where(jnp.logical_and(far_middle, is_odd), 1, 0)
    last = jnp.where(jnp.logical_and(far_middle, jnp.logical_not(is_odd)), 3, 2)
    own_entry = 3 * parity
    other_entry = jnp.where(middle_even, 1 + parity, jnp.where(is_odd, 1, 2))

    def work_item(item, carry):
        entry = jnp.where(item == 0, own_entry, jnp.where(item == 1, other_entry, 3))
        query_id = slots[chip_base + entry]
        indices = []
        key_base = []
        for distance in range(REACH + 1):
            key_id = query_id - distance
            is_live = jnp.logical_and(key_id >= 0, live[distance, query_id] == 1)
            index = jnp.int32(0)
            found = jnp.bool_(False)
            for e in range(len(entry_ids)):
                match = entry_ids[e] == key_id
                index = jnp.where(match, e, index)
                found = jnp.logical_or(found, match)
            ok = jnp.logical_and(is_live, found)
            indices.append(pl.multiple_of(jnp.where(ok, index, 0) * ROWS, ROWS))
            key_base.append(jnp.where(ok, key_id * ROWS, FAR))
        lane = lax.broadcasted_iota(jnp.int32, (1, GROUP * ROWS), 1)
        query_pos = query_id * ROWS + lax.rem(lane, ROWS)
        query_start = row_start[pl.ds(entry, 1), :]
        sub = lax.broadcasted_iota(jnp.int32, (ROWS, GROUP * ROWS), 0)
        for distance in range(REACH + 1):
            key_pos = sub + key_base[distance]
            allowed = jnp.logical_and(key_pos <= query_pos, key_pos >= query_start)
            bias[distance * ROWS : (distance + 1) * ROWS, :] = jnp.where(
                allowed, 0.0, MASKED
            )
        for g in range(KEY_VALUE_HEADS):
            kcols = slice(g * HEAD_WIDTH, (g + 1) * HEAD_WIDTH)
            vcols = slice(KV + g * HEAD_WIDTH, KV + (g + 1) * HEAD_WIDTH)
            heads = [
                slice((GROUP * g + j) * HEAD_WIDTH, (GROUP * g + j + 1) * HEAD_WIDTH)
                for j in range(GROUP)
            ]
            keys = jnp.concatenate([table[pl.ds(i, ROWS), kcols] for i in indices], 0)
            values = jnp.concatenate([table[pl.ds(i, ROWS), vcols] for i in indices], 0)
            q = jnp.concatenate([q_work[item, :, h] for h in heads], 0)
            grad = jnp.concatenate([g_work[item, :, h] for h in heads], 0)
            nt = (((1,), (1,)), ((), ()))
            raw = lax.dot_general(keys, q, nt, preferred_element_type=jnp.float32)
            raw = raw + bias[...]
            top = jnp.max(raw, axis=0, keepdims=True)
            weights = jnp.exp2((raw - top) * EXP2_SCALE)
            probs = weights * (1.0 / jnp.sum(weights, axis=0, keepdims=True))
            grad_scores = lax.dot_general(
                values, grad, nt, preferred_element_type=jnp.float32
            )
            offset = jnp.sum(probs * grad_scores, axis=0, keepdims=True)
            score_low = (probs * (grad_scores - offset)).astype(jnp.bfloat16)
            value_add = jnp.dot(
                probs.astype(jnp.bfloat16), grad, preferred_element_type=jnp.float32
            )
            key_add = jnp.dot(score_low, q, preferred_element_type=jnp.float32)
            query_add = lax.dot_general(
                score_low,
                keys,
                (((0,), (0,)), ((), ())),
                preferred_element_type=jnp.float32,
            )
            query_add = (query_add * SCALE).astype(jnp.bfloat16)
            for j, h in enumerate(heads):
                dq[item, :, h] = query_add[j * ROWS : (j + 1) * ROWS]
            for distance in range(REACH + 1):
                part = slice(distance * ROWS, (distance + 1) * ROWS)
                at = pl.ds(indices[distance], ROWS)
                total[at, kcols] += key_add[part] * SCALE
                total[at, vcols] += value_add[part]
        return carry

    lax.fori_loop(first, last, work_item, 0)
    low = jnp.bfloat16
    dq_own[...] = dq[:2]
    out_own[...] = total[pl.ds(own_at, 128), :]
    out_sib[:ROWS, :] = dq[1]
    out_sib[ROWS : 2 * ROWS, :] = dq[2]
    out_sib[2 * ROWS :, : 2 * KV] = total[pl.ds(sib_at, ROWS), :].astype(low)
    out_sib[2 * ROWS :, 2 * KV :] = total[pl.ds(sib_at + ROWS, ROWS), :].astype(low)
    for entry, out in (
        (TABLE_A, out_a.at[:ROWS, :]),
        (TABLE_X, out_a.at[ROWS:, :]),
        (TABLE_B, out_b),
        (TABLE_C, out_c),
    ):
        out[...] = total[entry * ROWS : (entry + 1) * ROWS, :].astype(low)


def pack_kernel(
    place,
    slots_hbm,
    docs_hbm,
    keys,
    values,
    queries,
    grads,
    chain,
    cross,
    pack,
    row_start,
    fold,
    slots,
    docs,
    sems,
):
    parity = lax.rem(place[0], 2)
    own_rows = pl.ds(pl.multiple_of(parity * ROWS, ROWS), ROWS)
    other_rows = pl.ds(pl.multiple_of((1 - parity) * ROWS, ROWS), ROWS)
    copies = [
        pltpu.make_async_copy(source, target, sems.at[n])
        for n, (source, target) in enumerate(
            [
                (slots_hbm, slots),
                (docs_hbm, docs),
                (keys.at[other_rows, :], cross.at[:, pl.ds(0, KV)]),
                (values.at[other_rows, :], cross.at[:, pl.ds(KV, KV)]),
                (keys.at[own_rows, :], chain.at[:, pl.ds(0, KV)]),
                (values.at[own_rows, :], chain.at[:, pl.ds(KV, KV)]),
                (queries, pack.at[pl.ds(0, 2 * ROWS), :]),
                (grads, pack.at[pl.ds(2 * ROWS, 2 * ROWS), :]),
            ]
            + [
                (
                    source.at[pl.ds(block * ROWS, ROWS), :],
                    pack.at[pl.ds(PACK_KV, ROWS), pl.ds((2 * block + n) * KV, KV)],
                )
                for block in range(2)
                for n, source in enumerate((keys, values))
            ]
        )
    ]
    for copy in copies:
        copy.start()
    copies[0].wait()
    copies[1].wait()
    middle = slots.shape[0] // 2 - 1
    chip_base = 2 * (place[0] - parity)
    lends = jnp.logical_and(parity == 1, slots[chip_base] == middle)
    fold[...] = jnp.full(fold.shape, jnp.where(lends, 1.0, 0.0))
    count = docs.shape[0]
    lane = lax.rem(lax.broadcasted_iota(jnp.int32, (1, GROUP * ROWS), 1), ROWS)
    for entry in range(4):
        first = slots[chip_base + entry] * ROWS

        def halve(_, bounds):
            low, high = bounds
            middle = (low + high) // 2
            begun = docs[middle] <= first
            inside = low < high
            return (
                jnp.where(jnp.logical_and(inside, begun), middle + 1, low),
                jnp.where(jnp.logical_and(inside, jnp.logical_not(begun)), middle, high),
            )

        begun, _ = lax.fori_loop(
            0, count.bit_length(), halve, (jnp.int32(1), jnp.int32(count))
        )

        def more(state):
            index, _ = state
            start = docs[jnp.minimum(index, count - 1)]
            return jnp.logical_and(index < count, start < first + ROWS)

        def step(state):
            index, row = state
            start = docs[index]
            return index + 1, jnp.where(lane + first >= start, start, row)

        _, row = lax.while_loop(
            more, step, (begun, jnp.full((1, GROUP * ROWS), docs[begun - 1]))
        )
        row_start[pl.ds(entry, 1), :] = row
    for copy in copies[2:]:
        copy.wait()


def final_kernel(
    place, slots, live, mine, own, lent, back_a, back_c, back_b, theirs, *outs
):
    query_out, key_out, value_out = outs
    me = place[0]
    parity = lax.rem(me, 2)
    is_odd = parity == 1
    chip_base = 2 * (me - parity)
    middle_even, far_middle = fold_flags(chip_base, slots, live)
    own_rows = pl.ds(pl.multiple_of(parity * ROWS, ROWS), ROWS)
    other_rows = pl.ds(pl.multiple_of((1 - parity) * ROWS, ROWS), ROWS)
    moved = jnp.logical_and(far_middle, is_odd)

    @pl.when(moved)
    def _():
        query_out[own_rows, :] = theirs[ROWS : 2 * ROWS, :]

    @pl.when(jnp.logical_not(moved))
    def _():
        query_out[own_rows, :] = mine[0]

    @pl.when(middle_even)
    def _():
        query_out[other_rows, :] = mine[1]

    @pl.when(jnp.logical_not(middle_even))
    def _():
        query_out[other_rows, :] = theirs[:ROWS, :]

    keeps = jnp.logical_and(is_odd, slots[chip_base + 2] == slots.shape[0] // 2 - 1)
    kept = jnp.where(keeps, 1.0, 0.0)
    f32 = jnp.float32
    for out, first in ((key_out, 0), (value_out, KV)):
        columns = slice(first, first + KV)
        chain = back_a[:ROWS, columns].astype(f32)
        cross = back_b[:, columns].astype(f32) + back_c[:, columns].astype(f32)
        low = own[:ROWS, columns] + theirs[2 * ROWS :, columns].astype(f32)
        low = low + lent[:, columns].astype(f32) + kept * back_a[ROWS:, columns].astype(f32)
        high = own[ROWS:, columns] + theirs[2 * ROWS :, 2 * KV + first : 3 * KV + first].astype(f32)
        out[:ROWS, :] = (low + jnp.where(is_odd, cross, chain)).astype(out.dtype)
        out[ROWS:, :] = (high + jnp.where(is_odd, chain, cross)).astype(out.dtype)


def vmem(count):
    return [pl.BlockSpec(memory_space=pltpu.VMEM)] * count


def in_hbm(array):
    return pltpu.with_memory_space_constraint(array, pltpu.HBM)


def hbm(count):
    return [pl.BlockSpec(memory_space=pltpu.HBM)] * count


def smem(count):
    return [pl.BlockSpec(memory_space=pltpu.SMEM)] * count


def shards(
    queries,
    key_rows_slotted,
    value_rows_slotted,
    output_gradient,
    slot_to_block,
    doc_starts,
    block_live,
):
    me = lax.axis_index("ctx")
    place = me.astype(jnp.int32).reshape(1)
    live = block_live.T
    params = pltpu.CompilerParams(vmem_limit_bytes=VMEM_LIMIT)

    bf16 = functools.partial(jax.ShapeDtypeStruct, dtype=jnp.bfloat16)
    kv_chain, kv_cross, pack, row_start, fold = pl.pallas_call(
        pack_kernel,
        out_shape=(
            bf16((ROWS, 2 * KV)),
            bf16((ROWS, 2 * KV)),
            bf16((PACK_ROWS, WIDE)),
            jax.ShapeDtypeStruct((4, GROUP * ROWS), jnp.int32),
            jax.ShapeDtypeStruct((ROWS, 2 * KV), jnp.float32),
        ),
        in_specs=smem(1) + hbm(6),
        out_specs=tuple(vmem(5)),
        scratch_shapes=[
            pltpu.SMEM(slot_to_block.shape, jnp.int32),
            pltpu.SMEM(doc_starts.shape, jnp.int32),
            pltpu.SemaphoreType.DMA((12,)),
        ],
        compiler_params=params,
        name="prepare",
    )(
        place,
        in_hbm(slot_to_block),
        in_hbm(doc_starts),
        in_hbm(key_rows_slotted),
        in_hbm(value_rows_slotted),
        in_hbm(queries),
        in_hbm(output_gradient),
    )
    kv_a = send(kv_chain, 2, -2)
    kv_b = send(kv_cross, -1, 1)
    kv_c = send(kv_cross, -3, 3)
    pack_sib = send(pack, 1, -1)
    low_rows = (slice(PACK_KV, None), slice(0, 2 * KV))
    kv_x = send(jnp.where(fold > 0, pack_sib[low_rows], pack[low_rows]), None, -2)

    wide = jax.ShapeDtypeStruct((2 * ROWS, 2 * KV), jnp.float32)
    dq_own, own, out_sib, out_a, out_b, out_c = pl.pallas_call(
        attention_kernel,
        out_shape=(
            bf16((2, ROWS, WIDE)),
            wide,
            bf16((3 * ROWS, WIDE)),
            bf16((2 * ROWS, 2 * KV)),
            bf16((ROWS, 2 * KV)),
            bf16((ROWS, 2 * KV)),
        ),
        in_specs=smem(3) + vmem(7),
        out_specs=tuple(vmem(6)),
        scratch_shapes=[
            pltpu.VMEM((3, ROWS, WIDE), jnp.bfloat16),
            pltpu.VMEM((ENTRIES * ROWS, 2 * KV), jnp.float32),
            pltpu.VMEM((ENTRIES * ROWS, 2 * KV), jnp.bfloat16),
            pltpu.VMEM((3, ROWS, WIDE), jnp.bfloat16),
            pltpu.VMEM((3, ROWS, WIDE), jnp.bfloat16),
            pltpu.VMEM((SPAN, GROUP * ROWS), jnp.float32),
        ],
        compiler_params=params,
        name="attention_items",
    )(
        place,
        in_hbm(slot_to_block),
        live,
        row_start,
        pack,
        pack_sib,
        kv_x,
        kv_b,
        kv_c,
        kv_a,
    )

    back_a = send(out_a, -2, 2)
    back_c = send(out_c, -3, 3)
    back_b = send(out_b, -1, 1)
    back_sib = send(out_sib, 1, -1)
    lent = send(jnp.where(fold > 0, back_a[ROWS:], 0), None, -1)

    query_grad, key_gradient, value_gradient = pl.pallas_call(
        final_kernel,
        out_shape=(bf16((2 * ROWS, WIDE)), bf16((2 * ROWS, KV)), bf16((2 * ROWS, KV))),
        in_specs=smem(3) + vmem(7),
        out_specs=tuple(vmem(3)),
        scratch_shapes=[],
        compiler_params=params,
        name="gradients_out",
    )(
        place,
        in_hbm(slot_to_block),
        live,
        dq_own,
        own,
        lent,
        back_a,
        back_c,
        back_b,
        back_sib,
    )
    return query_grad, key_gradient, value_gradient


def solution(mesh):
    rows = P(("section", "ctx"), None)
    return jax.shard_map(
        shards,
        mesh=mesh,
        in_specs=(rows, rows, rows, rows, P("section"), P("section"), P("section", None)),
        out_specs=(rows, rows, rows),
        check_vma=False,
    )
```

```python
import functools
import math

import jax
import jax.numpy as jnp
from jax import lax
from jax.experimental import pallas as pl
from jax.experimental.pallas import tpu as pltpu
from jax.sharding import PartitionSpec as P

QUERY_HEADS = 16
KEY_VALUE_HEADS = 4
GROUP = QUERY_HEADS // KEY_VALUE_HEADS
HEAD_WIDTH = 128
ROWS = 64
KV = KEY_VALUE_HEADS * HEAD_WIDTH
WIDE = QUERY_HEADS * HEAD_WIDTH
REACH = 3
SPAN = (REACH + 1) * ROWS
SCALE = 1.0 / math.sqrt(HEAD_WIDTH)
EXP2_SCALE = SCALE * math.log2(math.e)
MASKED = -1e30
FAR = 1 << 30
ENTRIES = 8
VMEM_LIMIT = 24 * 1024 * 1024

NEAR_COST = 1 << 34
TABLE_A, TABLE_B, TABLE_C, TABLE_X = 4, 5, 6, 7
PACK_KV = 4 * ROWS
PACK_ROWS = 5 * ROWS


def send(array, even_by, odd_by):
    count = lax.axis_size("ctx")
    steps = [odd_by if i % 2 else even_by for i in range(count)]
    pairs = [(i, (i + by) % count) for i, by in enumerate(steps) if by is not None]
    return lax.ppermute(array, "ctx", pairs)


def fold_flags(chip_base, slots, live):
    half = slots.shape[0] // 2
    middle_even = slots[chip_base] == half - 1
    middle_odd = slots[chip_base + 2] == half - 1
    far_middle = jnp.logical_and(middle_odd, live[REACH, half] == 1)
    return middle_even, far_middle


def attention_kernel(
    place,
    slots,
    live,
    row_start,
    pack_own,
    pack_sib,
    kv_x,
    kv_b,
    kv_c,
    kv_a,
    dq_own,
    out_own,
    out_sib,
    out_a,
    out_b,
    out_c,
    dq,
    total,
    table,
    q_work,
    g_work,
    bias,
):
    me = place[0]
    count = slots.shape[0] // 2
    parity = lax.rem(me, 2)
    is_odd = parity == 1
    chip_base = 2 * (me - parity)
    middle_even, far_middle = fold_flags(chip_base, slots, live)

    own_at = pl.multiple_of(parity * 128, 128)
    sib_at = pl.multiple_of((1 - parity) * 128, 128)
    for at, pack in ((own_at, pack_own), (sib_at, pack_sib)):
        table[pl.ds(at, ROWS), :] = pack[PACK_KV:, : 2 * KV]
        table[pl.ds(at + ROWS, ROWS), :] = pack[PACK_KV:, 2 * KV :]
    for entry, block in (
        (TABLE_A, kv_a),
        (TABLE_B, kv_b),
        (TABLE_C, kv_c),
        (TABLE_X, kv_x),
    ):
        table[entry * ROWS : (entry + 1) * ROWS, :] = block[...]
    total[...] = jnp.zeros_like(total)

    toward = jnp.where(is_odd, 1, -1)
    near_a = lax.rem(me + 2 * toward + count, count)
    near_b = lax.rem(me + toward + count, count)
    far = lax.rem(me + 3 * toward + count, count)
    before_middle = jnp.logical_and(
        is_odd,
        jnp.logical_or(slots[2 * near_a] == count - 1, slots[2 * near_b] == count - 1),
    )
    entry_ids = [slots[chip_base + e] for e in range(4)]
    entry_ids += [slots[2 * i + parity] for i in (near_a, near_b, far)]
    entry_ids += [jnp.where(before_middle, count - 1, -1)]

    own_row = pl.multiple_of(parity * ROWS, ROWS)
    other_row = pl.multiple_of((1 - parity) * ROWS, ROWS)
    grads_at = 2 * ROWS
    q_work[0] = pack_own[pl.ds(own_row, ROWS), :]
    g_work[0] = pack_own[pl.ds(grads_at + own_row, ROWS), :]

    @pl.when(middle_even)
    def _():
        q_work[1] = pack_own[pl.ds(other_row, ROWS), :]
        g_work[1] = pack_own[pl.ds(grads_at + other_row, ROWS), :]

    @pl.when(jnp.logical_not(middle_even))
    def _():
        q_work[1] = pack_sib[pl.ds(own_row, ROWS), :]
        g_work[1] = pack_sib[pl.ds(grads_at + own_row, ROWS), :]

    @pl.when(far_middle)
    def _():
        q_work[2] = pack_sib[ROWS : 2 * ROWS, :]
        g_work[2] = pack_sib[grads_at + ROWS : grads_at + 2 * ROWS, :]

    first = jnp.where(jnp.logical_and(far_middle, is_odd), 1, 0)
    last = jnp.where(jnp.logical_and(far_middle, jnp.logical_not(is_odd)), 3, 2)
    own_entry = 3 * parity
    other_entry = jnp.where(middle_even, 1 + parity, jnp.where(is_odd, 1, 2))

    def work_item(item, carry):
        entry = jnp.where(item == 0, own_entry, jnp.where(item == 1, other_entry, 3))
        query_id = slots[chip_base + entry]
        indices = []
        key_base = []
        for distance in range(REACH + 1):
            key_id = query_id - distance
            is_live = jnp.logical_and(key_id >= 0, live[distance, query_id] == 1)
            index = jnp.int32(0)
            found = jnp.bool_(False)
            for e in range(len(entry_ids)):
                match = entry_ids[e] == key_id
                index = jnp.where(match, e, index)
                found = jnp.logical_or(found, match)
            ok = jnp.logical_and(is_live, found)
            indices.append(pl.multiple_of(jnp.where(ok, index, 0) * ROWS, ROWS))
            key_base.append(jnp.where(ok, key_id * ROWS, FAR))
        lane = lax.broadcasted_iota(jnp.int32, (1, GROUP * ROWS), 1)
        query_pos = query_id * ROWS + lax.rem(lane, ROWS)
        query_start = row_start[pl.ds(entry, 1), :]
        sub = lax.broadcasted_iota(jnp.int32, (ROWS, GROUP * ROWS), 0)
        for distance in range(REACH + 1):
            key_pos = sub + key_base[distance]
            allowed = jnp.logical_and(key_pos <= query_pos, key_pos >= query_start)
            bias[distance * ROWS : (distance + 1) * ROWS, :] = jnp.where(
                allowed, 0.0, MASKED
            )
        for g in range(KEY_VALUE_HEADS):
            kcols = slice(g * HEAD_WIDTH, (g + 1) * HEAD_WIDTH)
            vcols = slice(KV + g * HEAD_WIDTH, KV + (g + 1) * HEAD_WIDTH)
            heads = [
                slice((GROUP * g + j) * HEAD_WIDTH, (GROUP * g + j + 1) * HEAD_WIDTH)
                for j in range(GROUP)
            ]
            keys = jnp.concatenate([table[pl.ds(i, ROWS), kcols] for i in indices], 0)
            values = jnp.concatenate([table[pl.ds(i, ROWS), vcols] for i in indices], 0)
            q = jnp.concatenate([q_work[item, :, h] for h in heads], 0)
            grad = jnp.concatenate([g_work[item, :, h] for h in heads], 0)
            nt = (((1,), (1,)), ((), ()))
            raw = lax.dot_general(keys, q, nt, preferred_element_type=jnp.float32)
            raw = raw + bias[...]
            top = jnp.max(raw, axis=0, keepdims=True)
            weights = jnp.exp2((raw - top) * EXP2_SCALE)
            probs = weights * (1.0 / jnp.sum(weights, axis=0, keepdims=True))
            grad_scores = lax.dot_general(
                values, grad, nt, preferred_element_type=jnp.float32
            )
            offset = jnp.sum(probs * grad_scores, axis=0, keepdims=True)
            score_low = (probs * (grad_scores - offset)).astype(jnp.bfloat16)
            value_add = jnp.dot(
                probs.astype(jnp.bfloat16), grad, preferred_element_type=jnp.float32
            )
            key_add = jnp.dot(score_low, q, preferred_element_type=jnp.float32)
            query_add = lax.dot_general(
                score_low,
                keys,
                (((0,), (0,)), ((), ())),
                preferred_element_type=jnp.float32,
            )
            query_add = (query_add * SCALE).astype(jnp.bfloat16)
            for j, h in enumerate(heads):
                dq[item, :, h] = query_add[j * ROWS : (j + 1) * ROWS]
            for distance in range(REACH + 1):
                part = slice(distance * ROWS, (distance + 1) * ROWS)
                at = pl.ds(indices[distance], ROWS)
                total[at, kcols] += key_add[part] * SCALE
                total[at, vcols] += value_add[part]
        return carry

    lax.fori_loop(first, last, work_item, 0)
    low = jnp.bfloat16
    dq_own[...] = dq[:2]
    out_own[...] = total[pl.ds(own_at, 128), :]
    out_sib[:ROWS, :] = dq[1]
    out_sib[ROWS : 2 * ROWS, :] = dq[2]
    out_sib[2 * ROWS :, : 2 * KV] = total[pl.ds(sib_at, ROWS), :].astype(low)
    out_sib[2 * ROWS :, 2 * KV :] = total[pl.ds(sib_at + ROWS, ROWS), :].astype(low)
    for entry, out in (
        (TABLE_A, out_a.at[:ROWS, :]),
        (TABLE_X, out_a.at[ROWS:, :]),
        (TABLE_B, out_b),
        (TABLE_C, out_c),
    ):
        out[...] = total[entry * ROWS : (entry + 1) * ROWS, :].astype(low)


def pack_kernel(
    place,
    slots_hbm,
    docs_hbm,
    keys,
    values,
    queries,
    grads,
    chain,
    cross,
    pack,
    row_start,
    fold,
    slots,
    docs,
    sems,
):
    parity = lax.rem(place[0], 2)
    own_rows = pl.ds(pl.multiple_of(parity * ROWS, ROWS), ROWS)
    other_rows = pl.ds(pl.multiple_of((1 - parity) * ROWS, ROWS), ROWS)
    copies = [
        pltpu.make_async_copy(source, target, sems.at[n])
        for n, (source, target) in enumerate(
            [
                (slots_hbm, slots),
                (docs_hbm, docs),
                (keys.at[other_rows, :], cross.at[:, pl.ds(0, KV)]),
                (values.at[other_rows, :], cross.at[:, pl.ds(KV, KV)]),
                (keys.at[own_rows, :], chain.at[:, pl.ds(0, KV)]),
                (values.at[own_rows, :], chain.at[:, pl.ds(KV, KV)]),
                (queries, pack.at[pl.ds(0, 2 * ROWS), :]),
                (grads, pack.at[pl.ds(2 * ROWS, 2 * ROWS), :]),
            ]
            + [
                (
                    source.at[pl.ds(block * ROWS, ROWS), :],
                    pack.at[pl.ds(PACK_KV, ROWS), pl.ds((2 * block + n) * KV, KV)],
                )
                for block in range(2)
                for n, source in enumerate((keys, values))
            ]
        )
    ]
    for copy in copies:
        copy.start()
    copies[0].wait()
    copies[1].wait()
    middle = slots.shape[0] // 2 - 1
    chip_base = 2 * (place[0] - parity)
    lends = jnp.logical_and(parity == 1, slots[chip_base] == middle)
    fold[...] = jnp.full(fold.shape, jnp.where(lends, 1.0, 0.0))
    count = docs.shape[0]
    lane = lax.rem(lax.broadcasted_iota(jnp.int32, (1, GROUP * ROWS), 1), ROWS)
    for entry in range(4):
        first = slots[chip_base + entry] * ROWS

        def halve(_, bounds):
            low, high = bounds
            middle = (low + high) // 2
            begun = docs[middle] <= first
            inside = low < high
            return (
                jnp.where(jnp.logical_and(inside, begun), middle + 1, low),
                jnp.where(jnp.logical_and(inside, jnp.logical_not(begun)), middle, high),
            )

        begun, _ = lax.fori_loop(
            0, count.bit_length(), halve, (jnp.int32(1), jnp.int32(count))
        )

        def more(state):
            index, _ = state
            start = docs[jnp.minimum(index, count - 1)]
            return jnp.logical_and(index < count, start < first + ROWS)

        def step(state):
            index, row = state
            start = docs[index]
            return index + 1, jnp.where(lane + first >= start, start, row)

        _, row = lax.while_loop(
            more, step, (begun, jnp.full((1, GROUP * ROWS), docs[begun - 1]))
        )
        row_start[pl.ds(entry, 1), :] = row
    for copy in copies[2:]:
        copy.wait()


def near_kernel(place, slots, own, back_a, out):
    parity = lax.rem(place[0], 2)
    is_odd = parity == 1
    own_rows = pl.ds(pl.multiple_of(parity * ROWS, ROWS), ROWS)
    out[...] = own[...]
    out[own_rows, :] += back_a[:ROWS, :].astype(jnp.float32)
    holder = slots[2 * (place[0] - parity) + 2] == slots.shape[0] // 2 - 1

    @pl.when(jnp.logical_and(is_odd, holder))
    def _():
        out[:ROWS, :] += back_a[ROWS:, :].astype(jnp.float32)


def final_kernel(place, slots, live, mine, own, lent, back_c, back_b, theirs, *outs):
    query_out, key_out, value_out = outs
    me = place[0]
    parity = lax.rem(me, 2)
    is_odd = parity == 1
    chip_base = 2 * (me - parity)
    middle_even, far_middle = fold_flags(chip_base, slots, live)
    own_rows = pl.ds(pl.multiple_of(parity * ROWS, ROWS), ROWS)
    other_rows = pl.ds(pl.multiple_of((1 - parity) * ROWS, ROWS), ROWS)
    moved = jnp.logical_and(far_middle, is_odd)

    @pl.when(moved)
    def _():
        query_out[own_rows, :] = theirs[ROWS : 2 * ROWS, :]

    @pl.when(jnp.logical_not(moved))
    def _():
        query_out[own_rows, :] = mine[0]

    @pl.when(middle_even)
    def _():
        query_out[other_rows, :] = mine[1]

    @pl.when(jnp.logical_not(middle_even))
    def _():
        query_out[other_rows, :] = theirs[:ROWS, :]

    f32 = jnp.float32
    for out, first in ((key_out, 0), (value_out, KV)):
        columns = slice(first, first + KV)
        cross = back_b[:, columns].astype(f32) + back_c[:, columns].astype(f32)
        low = own[:ROWS, columns] + theirs[2 * ROWS :, columns].astype(f32)
        low = low + lent[:, columns].astype(f32) + jnp.where(is_odd, cross, 0.0)
        high = own[ROWS:, columns] + theirs[2 * ROWS :, 2 * KV + first : 3 * KV + first].astype(f32)
        out[:ROWS, :] = low.astype(out.dtype)
        out[ROWS:, :] = (high + jnp.where(is_odd, 0.0, cross)).astype(out.dtype)


def vmem(count):
    return [pl.BlockSpec(memory_space=pltpu.VMEM)] * count


def in_hbm(array):
    return pltpu.with_memory_space_constraint(array, pltpu.HBM)


def hbm(count):
    return [pl.BlockSpec(memory_space=pltpu.HBM)] * count


def smem(count):
    return [pl.BlockSpec(memory_space=pltpu.SMEM)] * count


def shards(
    queries,
    key_rows_slotted,
    value_rows_slotted,
    output_gradient,
    slot_to_block,
    doc_starts,
    block_live,
):
    me = lax.axis_index("ctx")
    place = me.astype(jnp.int32).reshape(1)
    live = block_live.T
    params = pltpu.CompilerParams(vmem_limit_bytes=VMEM_LIMIT)

    bf16 = functools.partial(jax.ShapeDtypeStruct, dtype=jnp.bfloat16)
    kv_chain, kv_cross, pack, row_start, fold = pl.pallas_call(
        pack_kernel,
        out_shape=(
            bf16((ROWS, 2 * KV)),
            bf16((ROWS, 2 * KV)),
            bf16((PACK_ROWS, WIDE)),
            jax.ShapeDtypeStruct((4, GROUP * ROWS), jnp.int32),
            jax.ShapeDtypeStruct((ROWS, 2 * KV), jnp.float32),
        ),
        in_specs=smem(1) + hbm(6),
        out_specs=tuple(vmem(5)),
        scratch_shapes=[
            pltpu.SMEM(slot_to_block.shape, jnp.int32),
            pltpu.SMEM(doc_starts.shape, jnp.int32),
            pltpu.SemaphoreType.DMA((12,)),
        ],
        compiler_params=params,
        name="prepare",
    )(
        place,
        in_hbm(slot_to_block),
        in_hbm(doc_starts),
        in_hbm(key_rows_slotted),
        in_hbm(value_rows_slotted),
        in_hbm(queries),
        in_hbm(output_gradient),
    )
    kv_a = send(kv_chain, 2, -2)
    pack_sib, kv_cross = lax.optimization_barrier((send(pack, 1, -1), kv_cross))
    kv_b = send(kv_cross, -1, 1)
    kv_c = send(kv_cross, -3, 3)
    low_rows = (slice(PACK_KV, None), slice(0, 2 * KV))
    kv_x = send(jnp.where(fold > 0, pack_sib[low_rows], pack[low_rows]), None, -2)

    wide = jax.ShapeDtypeStruct((2 * ROWS, 2 * KV), jnp.float32)
    dq_own, own, out_sib, out_a, out_b, out_c = pl.pallas_call(
        attention_kernel,
        out_shape=(
            bf16((2, ROWS, WIDE)),
            wide,
            bf16((3 * ROWS, WIDE)),
            bf16((2 * ROWS, 2 * KV)),
            bf16((ROWS, 2 * KV)),
            bf16((ROWS, 2 * KV)),
        ),
        in_specs=smem(3) + vmem(7),
        out_specs=tuple(vmem(6)),
        scratch_shapes=[
            pltpu.VMEM((3, ROWS, WIDE), jnp.bfloat16),
            pltpu.VMEM((ENTRIES * ROWS, 2 * KV), jnp.float32),
            pltpu.VMEM((ENTRIES * ROWS, 2 * KV), jnp.bfloat16),
            pltpu.VMEM((3, ROWS, WIDE), jnp.bfloat16),
            pltpu.VMEM((3, ROWS, WIDE), jnp.bfloat16),
            pltpu.VMEM((SPAN, GROUP * ROWS), jnp.float32),
        ],
        compiler_params=params,
        name="attention_items",
    )(
        place,
        in_hbm(slot_to_block),
        live,
        row_start,
        pack,
        pack_sib,
        kv_x,
        kv_b,
        kv_c,
        kv_a,
    )

    back_a = send(out_a, -2, 2)
    back_c = send(out_c, -3, 3)
    back_b = send(out_b, -1, 1)
    back_sib = send(out_sib, 1, -1)
    lent = send(jnp.where(fold > 0, back_a[ROWS:], 0), None, -1)

    own = pl.pallas_call(
        near_kernel,
        out_shape=wide,
        in_specs=smem(2) + vmem(2),
        out_specs=vmem(1)[0],
        compiler_params=params,
        cost_estimate=pl.CostEstimate(
            flops=NEAR_COST, bytes_accessed=1 << 20, transcendentals=0
        ),
        name="two_away_sum",
    )(place, in_hbm(slot_to_block), own, back_a)

    query_grad, key_gradient, value_gradient = pl.pallas_call(
        final_kernel,
        out_shape=(bf16((2 * ROWS, WIDE)), bf16((2 * ROWS, KV)), bf16((2 * ROWS, KV))),
        in_specs=smem(3) + vmem(6),
        out_specs=tuple(vmem(3)),
        scratch_shapes=[],
        compiler_params=params,
        name="gradients_out",
    )(
        place,
        in_hbm(slot_to_block),
        live,
        dq_own,
        own,
        lent,
        back_c,
        back_b,
        back_sib,
    )
    return query_grad, key_gradient, value_gradient


def solution(mesh):
    rows = P(("section", "ctx"), None)
    return jax.shard_map(
        shards,
        mesh=mesh,
        in_specs=(rows, rows, rows, rows, P("section"), P("section"), P("section", None)),
        out_specs=(rows, rows, rows),
        check_vma=False,
    )
```

```python
import functools
import math

import jax
import jax.numpy as jnp
from jax import lax
from jax.experimental import pallas as pl
from jax.experimental.pallas import tpu as pltpu
from jax.sharding import PartitionSpec as P

QUERY_HEADS = 16
KEY_VALUE_HEADS = 4
GROUP = QUERY_HEADS // KEY_VALUE_HEADS
HEAD_WIDTH = 128
ROWS = 64
KV = KEY_VALUE_HEADS * HEAD_WIDTH
WIDE = QUERY_HEADS * HEAD_WIDTH
REACH = 3
SPAN = (REACH + 1) * ROWS
SCALE = 1.0 / math.sqrt(HEAD_WIDTH)
EXP2_SCALE = SCALE * math.log2(math.e)
MASKED = -1e30
FAR = 1 << 30
ENTRIES = 7
VMEM_LIMIT = 24 * 1024 * 1024

TABLE_A, TABLE_B, TABLE_C = 4, 5, 6
NEAR_COST = 1 << 34


def send(array, even_by, odd_by):
    count = lax.axis_size("ctx")
    steps = [odd_by if i % 2 else even_by for i in range(count)]
    pairs = [(i, (i + by) % count) for i, by in enumerate(steps) if by is not None]
    return lax.ppermute(array, "ctx", pairs)


def fold_flags(chip_base, slots, live):
    half = slots.shape[0] // 2
    middle_even = slots[chip_base] == half - 1
    middle_odd = slots[chip_base + 2] == half - 1
    far_middle = jnp.logical_and(middle_odd, live[REACH, half] == 1)
    return middle_even, far_middle


def attention_kernel(
    leading,
    place,
    slots,
    live,
    row_start,
    q_own,
    q_sib,
    g_own,
    g_sib,
    kv_own,
    kv_sib,
    kv_a,
    kv_b,
    *refs,
):
    if leading:
        dq, total, table, q_work, g_work, bias = refs
    else:
        kv_c, dq_in, total_in = refs[:3]
        dq_own, out_own, out_sib, out_a, out_b, out_c = refs[3:9]
        dq, total, table, q_work, g_work, bias = refs[9:]
    me = place[0]
    count = slots.shape[0] // 2
    parity = lax.rem(me, 2)
    is_odd = parity == 1
    chip_base = 2 * (me - parity)
    middle_even, far_middle = fold_flags(chip_base, slots, live)

    own_at = pl.multiple_of(parity * 128, 128)
    sib_at = pl.multiple_of((1 - parity) * 128, 128)
    table[pl.ds(own_at, 128), :] = kv_own[...]
    table[pl.ds(sib_at, 128), :] = kv_sib[...]
    table[TABLE_A * ROWS : TABLE_B * ROWS, :] = kv_a[...]
    table[TABLE_B * ROWS : TABLE_C * ROWS, :] = kv_b[...]

    toward = jnp.where(is_odd, 1, -1)
    near_a = lax.rem(me + 2 * toward + count, count)
    near_b = lax.rem(me + toward + count, count)
    far = lax.rem(me + 3 * toward + count, count)
    passed_odd = jnp.logical_and(is_odd, slots[2 * near_a] == count - 1)
    passed_even = jnp.logical_and(is_odd, slots[2 * near_b] == count - 1)
    entry_ids = [slots[chip_base + e] for e in range(4)]
    entry_ids += [slots[2 * near_a + parity], slots[2 * near_b + parity]]
    if not leading:
        table[TABLE_C * ROWS :, :] = kv_c[...]
        passed_middle = jnp.logical_or(passed_odd, passed_even)
        entry_ids += [jnp.where(passed_middle, count - 1, slots[2 * far + parity])]

    own_row = pl.multiple_of(parity * ROWS, ROWS)
    other_row = pl.multiple_of((1 - parity) * ROWS, ROWS)
    other_entry = jnp.where(middle_even, 1 + parity, jnp.where(is_odd, 1, 2))
    slot = 0 if leading else 1

    @pl.when(middle_even)
    def _():
        q_work[slot] = q_own[pl.ds(other_row, ROWS), :]
        g_work[slot] = g_own[pl.ds(other_row, ROWS), :]

    @pl.when(jnp.logical_not(middle_even))
    def _():
        q_work[slot] = q_sib[pl.ds(own_row, ROWS), :]
        g_work[slot] = g_sib[pl.ds(own_row, ROWS), :]

    if leading:
        total[...] = jnp.zeros_like(total)

        @pl.when(far_middle)
        def _():
            q_work[1] = q_sib[ROWS:, :]
            g_work[1] = g_sib[ROWS:, :]

        entries = (other_entry, 3)
        first = jnp.where(passed_even, 1, 0)
        last = jnp.where(jnp.logical_and(far_middle, jnp.logical_not(is_odd)), 2, 1)
    else:
        total[...] = total_in[...]
        q_work[0] = q_own[pl.ds(own_row, ROWS), :]
        g_work[0] = g_own[pl.ds(own_row, ROWS), :]
        entries = (3 * parity, other_entry)
        first = jnp.where(jnp.logical_and(far_middle, is_odd), 1, 0)
        last = jnp.where(passed_even, 2, 1)

    def work_item(item, carry):
        entry = jnp.where(item == 0, *entries)
        query_id = slots[chip_base + entry]
        indices = []
        key_base = []
        for distance in range(REACH + 1):
            key_id = query_id - distance
            is_live = jnp.logical_and(key_id >= 0, live[distance, query_id] == 1)
            index = jnp.int32(0)
            found = jnp.bool_(False)
            for e in range(len(entry_ids)):
                match = entry_ids[e] == key_id
                index = jnp.where(match, e, index)
                found = jnp.logical_or(found, match)
            ok = jnp.logical_and(is_live, found)
            indices.append(pl.multiple_of(jnp.where(ok, index, 0) * ROWS, ROWS))
            key_base.append(jnp.where(ok, key_id * ROWS, FAR))
        lane = lax.broadcasted_iota(jnp.int32, (1, GROUP * ROWS), 1)
        query_pos = query_id * ROWS + lax.rem(lane, ROWS)
        query_start = row_start[pl.ds(entry, 1), :]
        sub = lax.broadcasted_iota(jnp.int32, (ROWS, GROUP * ROWS), 0)
        for distance in range(REACH + 1):
            key_pos = sub + key_base[distance]
            allowed = jnp.logical_and(key_pos <= query_pos, key_pos >= query_start)
            bias[distance * ROWS : (distance + 1) * ROWS, :] = jnp.where(
                allowed, 0.0, MASKED
            )
        for g in range(KEY_VALUE_HEADS):
            kcols = slice(g * HEAD_WIDTH, (g + 1) * HEAD_WIDTH)
            vcols = slice(KV + g * HEAD_WIDTH, KV + (g + 1) * HEAD_WIDTH)
            heads = [
                slice((GROUP * g + j) * HEAD_WIDTH, (GROUP * g + j + 1) * HEAD_WIDTH)
                for j in range(GROUP)
            ]
            keys = jnp.concatenate([table[pl.ds(i, ROWS), kcols] for i in indices], 0)
            values = jnp.concatenate([table[pl.ds(i, ROWS), vcols] for i in indices], 0)
            q = jnp.concatenate([q_work[item, :, h] for h in heads], 0)
            grad = jnp.concatenate([g_work[item, :, h] for h in heads], 0)
            nt = (((1,), (1,)), ((), ()))
            raw = lax.dot_general(keys, q, nt, preferred_element_type=jnp.float32)
            raw = raw + bias[...]
            top = jnp.max(raw, axis=0, keepdims=True)
            weights = jnp.exp2((raw - top) * EXP2_SCALE)
            probs = weights * (1.0 / jnp.sum(weights, axis=0, keepdims=True))
            grad_scores = lax.dot_general(
                values, grad, nt, preferred_element_type=jnp.float32
            )
            offset = jnp.sum(probs * grad_scores, axis=0, keepdims=True)
            score_low = (probs * (grad_scores - offset)).astype(jnp.bfloat16)
            value_add = jnp.dot(
                probs.astype(jnp.bfloat16), grad, preferred_element_type=jnp.float32
            )
            key_add = jnp.dot(score_low, q, preferred_element_type=jnp.float32)
            query_add = lax.dot_general(
                score_low,
                keys,
                (((0,), (0,)), ((), ())),
                preferred_element_type=jnp.float32,
            )
            query_add = (query_add * SCALE).astype(jnp.bfloat16)
            for j, h in enumerate(heads):
                dq[item, :, h] = query_add[j * ROWS : (j + 1) * ROWS]
            for distance in range(REACH + 1):
                part = slice(distance * ROWS, (distance + 1) * ROWS)
                at = pl.ds(indices[distance], ROWS)
                total[at, kcols] += key_add[part] * SCALE
                total[at, vcols] += value_add[part]
        return carry

    lax.fori_loop(first, last, work_item, 0)
    if leading:
        return
    low = jnp.bfloat16
    dq_own[0] = dq[0]
    dq_own[1] = dq_in[0]

    @pl.when(passed_even)
    def _():
        dq_own[1] = dq[1]

    out_sib[:ROWS, :] = dq_own[1]
    out_sib[ROWS : 2 * ROWS, :] = dq_in[1]
    out_sib[2 * ROWS :, : 2 * KV] = total[pl.ds(sib_at, ROWS), :].astype(low)
    out_sib[2 * ROWS :, 2 * KV :] = total[pl.ds(sib_at + ROWS, ROWS), :].astype(low)
    out_own[...] = total[pl.ds(own_at, 128), :]
    out_a[:ROWS, :] = total[TABLE_A * ROWS : TABLE_B * ROWS, :].astype(low)
    out_b[...] = total[TABLE_B * ROWS : TABLE_C * ROWS, :].astype(low)
    passed = total[TABLE_C * ROWS :, :].astype(low)
    out_a[ROWS:, :] = jnp.zeros_like(passed)
    out_c[...] = passed

    @pl.when(passed_middle)
    def _():
        out_a[ROWS:, :] = passed
        out_c[...] = jnp.zeros_like(passed)


def pack_kernel(
    place,
    slots_hbm,
    docs_hbm,
    keys,
    values,
    queries,
    grads,
    both,
    chain,
    cross,
    q_own,
    g_own,
    row_start,
    fold,
    slots,
    docs,
    sems,
):
    parity = lax.rem(place[0], 2)
    own_rows = pl.ds(pl.multiple_of(parity * ROWS, ROWS), ROWS)
    other_rows = pl.ds(pl.multiple_of((1 - parity) * ROWS, ROWS), ROWS)
    copies = [
        pltpu.make_async_copy(source, target, sems.at[n])
        for n, (source, target) in enumerate(
            [
                (slots_hbm, slots),
                (docs_hbm, docs),
                (keys.at[other_rows, :], cross.at[:, pl.ds(0, KV)]),
                (values.at[other_rows, :], cross.at[:, pl.ds(KV, KV)]),
                (keys.at[own_rows, :], chain.at[:, pl.ds(0, KV)]),
                (values.at[own_rows, :], chain.at[:, pl.ds(KV, KV)]),
                (keys, both.at[:, pl.ds(0, KV)]),
                (values, both.at[:, pl.ds(KV, KV)]),
                (queries, q_own),
                (grads, g_own),
            ]
        )
    ]
    for copy in copies:
        copy.start()
    copies[0].wait()
    copies[1].wait()
    middle = slots.shape[0] // 2 - 1
    chip_base = 2 * (place[0] - parity)
    holder = jnp.where(
        slots[chip_base + 2] == middle, 1, jnp.where(slots[chip_base] == middle, 2, 0)
    )
    fold[...] = jnp.full(fold.shape, jnp.where(parity == 1, holder, 0).astype(jnp.float32))
    count = docs.shape[0]
    lane = lax.rem(lax.broadcasted_iota(jnp.int32, (1, GROUP * ROWS), 1), ROWS)
    for entry in range(4):
        first = slots[chip_base + entry] * ROWS

        def halve(_, bounds):
            low, high = bounds
            middle = (low + high) // 2
            begun = docs[middle] <= first
            inside = low < high
            return (
                jnp.where(jnp.logical_and(inside, begun), middle + 1, low),
                jnp.where(jnp.logical_and(inside, jnp.logical_not(begun)), middle, high),
            )

        begun, _ = lax.fori_loop(
            0, count.bit_length(), halve, (jnp.int32(1), jnp.int32(count))
        )

        def more(state):
            index, _ = state
            start = docs[jnp.minimum(index, count - 1)]
            return jnp.logical_and(index < count, start < first + ROWS)

        def step(state):
            index, row = state
            start = docs[index]
            return index + 1, jnp.where(lane + first >= start, start, row)

        _, row = lax.while_loop(
            more, step, (begun, jnp.full((1, GROUP * ROWS), docs[begun - 1]))
        )
        row_start[pl.ds(entry, 1), :] = row
    for copy in copies[2:]:
        copy.wait()


def near_kernel(place, slots, own, back_a, out):
    parity = lax.rem(place[0], 2)
    is_odd = parity == 1
    own_rows = pl.ds(pl.multiple_of(parity * ROWS, ROWS), ROWS)
    out[...] = own[...]
    out[own_rows, :] += back_a[:ROWS, :].astype(jnp.float32)
    holder = slots[2 * (place[0] - parity) + 2] == slots.shape[0] // 2 - 1

    @pl.when(jnp.logical_and(is_odd, holder))
    def _():
        out[:ROWS, :] += back_a[ROWS:, :].astype(jnp.float32)


def final_kernel(place, slots, live, mine, own, lent, back_c, back_b, theirs, *outs):
    query_out, key_out, value_out = outs
    me = place[0]
    parity = lax.rem(me, 2)
    is_odd = parity == 1
    chip_base = 2 * (me - parity)
    middle_even, far_middle = fold_flags(chip_base, slots, live)
    own_rows = pl.ds(pl.multiple_of(parity * ROWS, ROWS), ROWS)
    other_rows = pl.ds(pl.multiple_of((1 - parity) * ROWS, ROWS), ROWS)
    moved = jnp.logical_and(far_middle, is_odd)

    @pl.when(moved)
    def _():
        query_out[own_rows, :] = theirs[ROWS : 2 * ROWS, :]

    @pl.when(jnp.logical_not(moved))
    def _():
        query_out[own_rows, :] = mine[0]

    @pl.when(middle_even)
    def _():
        query_out[other_rows, :] = mine[1]

    @pl.when(jnp.logical_not(middle_even))
    def _():
        query_out[other_rows, :] = theirs[:ROWS, :]

    f32 = jnp.float32
    for out, first in ((key_out, 0), (value_out, KV)):
        columns = slice(first, first + KV)
        cross = back_b[:, columns].astype(f32) + back_c[:, columns].astype(f32)
        low = own[:ROWS, columns] + theirs[2 * ROWS :, columns].astype(f32)
        low = low + lent[:, columns].astype(f32) + jnp.where(is_odd, cross, 0.0)
        high = own[ROWS:, columns] + theirs[2 * ROWS :, 2 * KV + first : 3 * KV + first].astype(f32)
        out[:ROWS, :] = low.astype(out.dtype)
        out[ROWS:, :] = (high + jnp.where(is_odd, 0.0, cross)).astype(out.dtype)


def vmem(count):
    return [pl.BlockSpec(memory_space=pltpu.VMEM)] * count


def in_hbm(array):
    return pltpu.with_memory_space_constraint(array, pltpu.HBM)


def hbm(count):
    return [pl.BlockSpec(memory_space=pltpu.HBM)] * count


def smem(count):
    return [pl.BlockSpec(memory_space=pltpu.SMEM)] * count


def shards(
    queries,
    key_rows_slotted,
    value_rows_slotted,
    output_gradient,
    slot_to_block,
    doc_starts,
    block_live,
):
    me = lax.axis_index("ctx")
    place = me.astype(jnp.int32).reshape(1)
    live = block_live.T
    params = pltpu.CompilerParams(vmem_limit_bytes=VMEM_LIMIT)

    bf16 = functools.partial(jax.ShapeDtypeStruct, dtype=jnp.bfloat16)
    kv, kv_chain, kv_cross, q_own, g_own, row_start, fold = pl.pallas_call(
        pack_kernel,
        out_shape=(
            bf16((2 * ROWS, 2 * KV)),
            bf16((ROWS, 2 * KV)),
            bf16((ROWS, 2 * KV)),
            bf16((2 * ROWS, WIDE)),
            bf16((2 * ROWS, WIDE)),
            jax.ShapeDtypeStruct((4, GROUP * ROWS), jnp.int32),
            jax.ShapeDtypeStruct((ROWS, 2 * KV), jnp.float32),
        ),
        in_specs=smem(1) + hbm(6),
        out_specs=tuple(vmem(7)),
        scratch_shapes=[
            pltpu.SMEM(slot_to_block.shape, jnp.int32),
            pltpu.SMEM(doc_starts.shape, jnp.int32),
            pltpu.SemaphoreType.DMA((10,)),
        ],
        compiler_params=params,
        name="prepare",
    )(
        place,
        in_hbm(slot_to_block),
        in_hbm(doc_starts),
        in_hbm(key_rows_slotted),
        in_hbm(value_rows_slotted),
        in_hbm(queries),
        in_hbm(output_gradient),
    )
    kv_a = send(kv_chain, 2, -2)
    kv_b = send(kv_cross, -1, 1)
    kv_sib = send(kv, 1, -1)
    q_sib = send(queries, 1, -1)
    g_sib = send(output_gradient, 1, -1)
    passed = jnp.where(fold == 1, kv[:ROWS], jnp.where(fold == 2, kv_sib[:ROWS], kv_b))
    kv_c = send(passed, 2, -2)

    work = [
        pltpu.VMEM((2, ROWS, WIDE), jnp.bfloat16),
        pltpu.VMEM((ENTRIES * ROWS, 2 * KV), jnp.bfloat16),
        pltpu.VMEM((2, ROWS, WIDE), jnp.bfloat16),
        pltpu.VMEM((2, ROWS, WIDE), jnp.bfloat16),
        pltpu.VMEM((SPAN, GROUP * ROWS), jnp.float32),
    ]
    sums = jax.ShapeDtypeStruct((ENTRIES * ROWS, 2 * KV), jnp.float32)
    operands = (
        place,
        in_hbm(slot_to_block),
        live,
        row_start,
        q_own,
        q_sib,
        g_own,
        g_sib,
        kv,
        kv_sib,
        kv_a,
        kv_b,
    )
    dq_leading, total = pl.pallas_call(
        functools.partial(attention_kernel, True),
        out_shape=(bf16((2, ROWS, WIDE)), sums),
        in_specs=smem(3) + vmem(9),
        out_specs=tuple(vmem(2)),
        scratch_shapes=work[1:],
        compiler_params=params,
        cost_estimate=pl.CostEstimate(
            flops=1 << 36, bytes_accessed=1 << 22, transcendentals=1 << 18
        ),
        name="attention_leading",
    )(*operands)
    wide = jax.ShapeDtypeStruct((2 * ROWS, 2 * KV), jnp.float32)
    dq_own, own, out_sib, out_a, out_b, out_c = pl.pallas_call(
        functools.partial(attention_kernel, False),
        out_shape=(
            bf16((2, ROWS, WIDE)),
            wide,
            bf16((3 * ROWS, WIDE)),
            bf16((2 * ROWS, 2 * KV)),
            bf16((ROWS, 2 * KV)),
            bf16((ROWS, 2 * KV)),
        ),
        in_specs=smem(3) + vmem(12),
        out_specs=tuple(vmem(6)),
        scratch_shapes=work[:1] + [pltpu.VMEM(sums.shape, jnp.float32)] + work[1:],
        compiler_params=params,
        name="attention_last",
    )(*operands, kv_c, dq_leading, total)

    back_a = send(out_a, -2, 2)
    back_c = send(out_c, -3, 3)
    back_b = send(out_b, -1, 1)
    back_sib = send(out_sib, 1, -1)
    lent = send(jnp.where(fold == 2, back_a[ROWS:], 0), None, -1)

    own = pl.pallas_call(
        near_kernel,
        out_shape=wide,
        in_specs=smem(2) + vmem(2),
        out_specs=vmem(1)[0],
        compiler_params=params,
        cost_estimate=pl.CostEstimate(
            flops=NEAR_COST, bytes_accessed=1 << 20, transcendentals=0
        ),
        name="two_away_sum",
    )(place, in_hbm(slot_to_block), own, back_a)

    query_grad, key_gradient, value_gradient = pl.pallas_call(
        final_kernel,
        out_shape=(bf16((2 * ROWS, WIDE)), bf16((2 * ROWS, KV)), bf16((2 * ROWS, KV))),
        in_specs=smem(3) + vmem(6),
        out_specs=tuple(vmem(3)),
        scratch_shapes=[],
        compiler_params=params,
        name="gradients_out",
    )(
        place,
        in_hbm(slot_to_block),
        live,
        dq_own,
        own,
        lent,
        back_c,
        back_b,
        back_sib,
    )
    return query_grad, key_gradient, value_gradient


def solution(mesh):
    rows = P(("section", "ctx"), None)
    return jax.shard_map(
        shards,
        mesh=mesh,
        in_specs=(rows, rows, rows, rows, P("section"), P("section"), P("section", None)),
        out_specs=(rows, rows, rows),
        check_vma=False,
    )
```

```python
import functools
import math

import jax
import jax.numpy as jnp
from jax import lax
from jax.experimental import pallas as pl
from jax.experimental.pallas import tpu as pltpu
from jax.sharding import PartitionSpec as P

QUERY_HEADS = 16
KEY_VALUE_HEADS = 4
GROUP = QUERY_HEADS // KEY_VALUE_HEADS
HEAD_WIDTH = 128
ROWS = 64
KV = KEY_VALUE_HEADS * HEAD_WIDTH
WIDE = QUERY_HEADS * HEAD_WIDTH
REACH = 3
SPAN = (REACH + 1) * ROWS
SCALE = 1.0 / math.sqrt(HEAD_WIDTH)
EXP2_SCALE = SCALE * math.log2(math.e)
MASKED = -1e30
FAR = 1 << 30
ENTRIES = 7
VMEM_LIMIT = 24 * 1024 * 1024

TABLE_A, TABLE_B, TABLE_C = 4, 5, 6
NEAR_COST = 1 << 34


def send(array, even_by, odd_by):
    count = lax.axis_size("ctx")
    steps = [odd_by if i % 2 else even_by for i in range(count)]
    pairs = [(i, (i + by) % count) for i, by in enumerate(steps) if by is not None]
    return lax.ppermute(array, "ctx", pairs)


def fold_flags(chip_base, slots, live):
    half = slots.shape[0] // 2
    middle_even = slots[chip_base] == half - 1
    middle_odd = slots[chip_base + 2] == half - 1
    far_middle = jnp.logical_and(middle_odd, live[REACH, half] == 1)
    return middle_even, far_middle


def attention_kernel(
    leading,
    place,
    slots,
    live,
    row_start,
    q_own,
    q_sib,
    g_own,
    g_sib,
    kv_own,
    kv_sib,
    kv_a,
    kv_b,
    *refs,
):
    if leading:
        dq, total, table, q_work, g_work, bias = refs
    else:
        kv_c, dq_in, total_in = refs[:3]
        dq_own, out_own, out_sib, out_a, out_b, out_c = refs[3:9]
        dq, total, table, q_work, g_work, bias = refs[9:]
    me = place[0]
    count = slots.shape[0] // 2
    parity = lax.rem(me, 2)
    is_odd = parity == 1
    chip_base = 2 * (me - parity)
    middle_even, far_middle = fold_flags(chip_base, slots, live)

    own_at = pl.multiple_of(parity * 128, 128)
    sib_at = pl.multiple_of((1 - parity) * 128, 128)
    table[pl.ds(own_at, 128), :] = kv_own[...]
    table[pl.ds(sib_at, 128), :] = kv_sib[...]
    table[TABLE_A * ROWS : TABLE_B * ROWS, :] = kv_a[...]
    table[TABLE_B * ROWS : TABLE_C * ROWS, :] = kv_b[...]

    toward = jnp.where(is_odd, 1, -1)
    near_a = lax.rem(me + 2 * toward + count, count)
    near_b = lax.rem(me + toward + count, count)
    far = lax.rem(me + 3 * toward + count, count)
    passed_odd = jnp.logical_and(is_odd, slots[2 * near_a] == count - 1)
    passed_even = jnp.logical_and(is_odd, slots[2 * near_b] == count - 1)
    entry_ids = [slots[chip_base + e] for e in range(4)]
    entry_ids += [slots[2 * near_a + parity], slots[2 * near_b + parity]]
    if not leading:
        table[TABLE_C * ROWS :, :] = kv_c[...]
        passed_middle = jnp.logical_or(passed_odd, passed_even)
        entry_ids += [jnp.where(passed_middle, count - 1, slots[2 * far + parity])]

    own_row = pl.multiple_of(parity * ROWS, ROWS)
    other_row = pl.multiple_of((1 - parity) * ROWS, ROWS)
    other_entry = jnp.where(middle_even, 1 + parity, jnp.where(is_odd, 1, 2))
    slot = 0 if leading else 1

    @pl.when(middle_even)
    def _():
        q_work[slot] = q_own[pl.ds(other_row, ROWS), :]
        g_work[slot] = g_own[pl.ds(other_row, ROWS), :]

    @pl.when(jnp.logical_not(middle_even))
    def _():
        q_work[slot] = q_sib[pl.ds(own_row, ROWS), :]
        g_work[slot] = g_sib[pl.ds(own_row, ROWS), :]

    if leading:
        total[...] = jnp.zeros_like(total)

        @pl.when(far_middle)
        def _():
            q_work[1] = q_sib[ROWS:, :]
            g_work[1] = g_sib[ROWS:, :]

        entries = (other_entry, 3)
        first = jnp.where(passed_even, 1, 0)
        last = jnp.where(jnp.logical_and(far_middle, jnp.logical_not(is_odd)), 2, 1)
    else:
        total[...] = total_in[...]
        q_work[0] = q_own[pl.ds(own_row, ROWS), :]
        g_work[0] = g_own[pl.ds(own_row, ROWS), :]
        entries = (3 * parity, other_entry)
        first = jnp.where(jnp.logical_and(far_middle, is_odd), 1, 0)
        last = jnp.where(passed_even, 2, 1)

    def work_item(item, carry):
        entry = jnp.where(item == 0, *entries)
        query_id = slots[chip_base + entry]
        indices = []
        key_base = []
        for distance in range(REACH + 1):
            key_id = query_id - distance
            is_live = jnp.logical_and(key_id >= 0, live[distance, query_id] == 1)
            index = jnp.int32(0)
            found = jnp.bool_(False)
            for e in range(len(entry_ids)):
                match = entry_ids[e] == key_id
                index = jnp.where(match, e, index)
                found = jnp.logical_or(found, match)
            ok = jnp.logical_and(is_live, found)
            indices.append(pl.multiple_of(jnp.where(ok, index, 0) * ROWS, ROWS))
            key_base.append(jnp.where(ok, key_id * ROWS, FAR))
        lane = lax.broadcasted_iota(jnp.int32, (1, GROUP * ROWS), 1)
        query_pos = query_id * ROWS + lax.rem(lane, ROWS)
        query_start = row_start[pl.ds(entry, 1), :]
        sub = lax.broadcasted_iota(jnp.int32, (ROWS, GROUP * ROWS), 0)
        for distance in range(REACH + 1):
            key_pos = sub + key_base[distance]
            allowed = jnp.logical_and(key_pos <= query_pos, key_pos >= query_start)
            bias[distance * ROWS : (distance + 1) * ROWS, :] = jnp.where(
                allowed, 0.0, MASKED
            )
        for g in range(KEY_VALUE_HEADS):
            kcols = slice(g * HEAD_WIDTH, (g + 1) * HEAD_WIDTH)
            vcols = slice(KV + g * HEAD_WIDTH, KV + (g + 1) * HEAD_WIDTH)
            heads = [
                slice((GROUP * g + j) * HEAD_WIDTH, (GROUP * g + j + 1) * HEAD_WIDTH)
                for j in range(GROUP)
            ]
            keys = jnp.concatenate([table[pl.ds(i, ROWS), kcols] for i in indices], 0)
            values = jnp.concatenate([table[pl.ds(i, ROWS), vcols] for i in indices], 0)
            q = jnp.concatenate([q_work[item, :, h] for h in heads], 0)
            grad = jnp.concatenate([g_work[item, :, h] for h in heads], 0)
            nt = (((1,), (1,)), ((), ()))
            raw = lax.dot_general(keys, q, nt, preferred_element_type=jnp.float32)
            raw = raw + bias[...]
            top = jnp.max(raw, axis=0, keepdims=True)
            weights = jnp.exp2((raw - top) * EXP2_SCALE)
            probs = weights * (1.0 / jnp.sum(weights, axis=0, keepdims=True))
            grad_scores = lax.dot_general(
                values, grad, nt, preferred_element_type=jnp.float32
            )
            offset = jnp.sum(probs * grad_scores, axis=0, keepdims=True)
            score_low = (probs * (grad_scores - offset)).astype(jnp.bfloat16)
            value_add = jnp.dot(
                probs.astype(jnp.bfloat16), grad, preferred_element_type=jnp.float32
            )
            key_add = jnp.dot(score_low, q, preferred_element_type=jnp.float32)
            query_add = lax.dot_general(
                score_low,
                keys,
                (((0,), (0,)), ((), ())),
                preferred_element_type=jnp.float32,
            )
            query_add = (query_add * SCALE).astype(jnp.bfloat16)
            for j, h in enumerate(heads):
                dq[item, :, h] = query_add[j * ROWS : (j + 1) * ROWS]
            for distance in range(REACH + 1):
                part = slice(distance * ROWS, (distance + 1) * ROWS)
                at = pl.ds(indices[distance], ROWS)
                total[at, kcols] += key_add[part] * SCALE
                total[at, vcols] += value_add[part]
        return carry

    lax.fori_loop(first, last, work_item, 0)
    if leading:
        return
    low = jnp.bfloat16
    dq_own[0] = dq[0]
    dq_own[1] = dq_in[0]

    @pl.when(passed_even)
    def _():
        dq_own[1] = dq[1]

    out_sib[:ROWS, :] = dq_own[1]
    out_sib[ROWS : 2 * ROWS, :] = dq_in[1]
    out_sib[2 * ROWS :, : 2 * KV] = total[pl.ds(sib_at, ROWS), :].astype(low)
    out_sib[2 * ROWS :, 2 * KV :] = total[pl.ds(sib_at + ROWS, ROWS), :].astype(low)
    out_own[...] = total[pl.ds(own_at, 128), :]
    out_a[:ROWS, :] = total[TABLE_A * ROWS : TABLE_B * ROWS, :].astype(low)
    out_b[...] = total[TABLE_B * ROWS : TABLE_C * ROWS, :].astype(low)
    passed = total[TABLE_C * ROWS :, :].astype(low)
    out_a[ROWS:, :] = jnp.zeros_like(passed)
    out_c[...] = passed

    @pl.when(passed_middle)
    def _():
        out_a[ROWS:, :] = passed
        out_c[...] = jnp.zeros_like(passed)


def pack_kernel(
    place,
    slots_hbm,
    docs_hbm,
    keys,
    values,
    queries,
    grads,
    both,
    chain,
    cross,
    q_own,
    g_own,
    row_start,
    fold,
    slots,
    docs,
    sems,
):
    parity = lax.rem(place[0], 2)
    own_rows = pl.ds(pl.multiple_of(parity * ROWS, ROWS), ROWS)
    other_rows = pl.ds(pl.multiple_of((1 - parity) * ROWS, ROWS), ROWS)
    copies = [
        pltpu.make_async_copy(source, target, sems.at[n])
        for n, (source, target) in enumerate(
            [
                (slots_hbm, slots),
                (docs_hbm, docs),
                (keys.at[other_rows, :], cross.at[:, pl.ds(0, KV)]),
                (values.at[other_rows, :], cross.at[:, pl.ds(KV, KV)]),
                (keys.at[own_rows, :], chain.at[:, pl.ds(0, KV)]),
                (values.at[own_rows, :], chain.at[:, pl.ds(KV, KV)]),
                (keys, both.at[:, pl.ds(0, KV)]),
                (values, both.at[:, pl.ds(KV, KV)]),
                (queries, q_own),
                (grads, g_own),
            ]
        )
    ]
    for copy in copies:
        copy.start()
    copies[0].wait()
    copies[1].wait()
    middle = slots.shape[0] // 2 - 1
    chip_base = 2 * (place[0] - parity)
    holder = jnp.where(
        slots[chip_base + 2] == middle, 1, jnp.where(slots[chip_base] == middle, 2, 0)
    )
    fold[...] = jnp.full(fold.shape, jnp.where(parity == 1, holder, 0).astype(jnp.float32))
    count = docs.shape[0]
    lane = lax.rem(lax.broadcasted_iota(jnp.int32, (1, GROUP * ROWS), 1), ROWS)
    for entry in range(4):
        first = slots[chip_base + entry] * ROWS

        def halve(_, bounds):
            low, high = bounds
            middle = (low + high) // 2
            begun = docs[middle] <= first
            inside = low < high
            return (
                jnp.where(jnp.logical_and(inside, begun), middle + 1, low),
                jnp.where(jnp.logical_and(inside, jnp.logical_not(begun)), middle, high),
            )

        begun, _ = lax.fori_loop(
            0, count.bit_length(), halve, (jnp.int32(1), jnp.int32(count))
        )

        def more(state):
            index, _ = state
            start = docs[jnp.minimum(index, count - 1)]
            return jnp.logical_and(index < count, start < first + ROWS)

        def step(state):
            index, row = state
            start = docs[index]
            return index + 1, jnp.where(lane + first >= start, start, row)

        _, row = lax.while_loop(
            more, step, (begun, jnp.full((1, GROUP * ROWS), docs[begun - 1]))
        )
        row_start[pl.ds(entry, 1), :] = row
    for copy in copies[2:]:
        copy.wait()


def near_kernel(place, slots, own, back_a, out):
    parity = lax.rem(place[0], 2)
    is_odd = parity == 1
    own_rows = pl.ds(pl.multiple_of(parity * ROWS, ROWS), ROWS)
    out[...] = own[...]
    out[own_rows, :] += back_a[:ROWS, :].astype(jnp.float32)
    holder = slots[2 * (place[0] - parity) + 2] == slots.shape[0] // 2 - 1

    @pl.when(jnp.logical_and(is_odd, holder))
    def _():
        out[:ROWS, :] += back_a[ROWS:, :].astype(jnp.float32)


def final_kernel(place, slots, live, mine, own, lent, back_b, back_c, theirs, *outs):
    query_out, key_out, value_out = outs
    me = place[0]
    parity = lax.rem(me, 2)
    is_odd = parity == 1
    chip_base = 2 * (me - parity)
    middle_even, far_middle = fold_flags(chip_base, slots, live)
    own_rows = pl.ds(pl.multiple_of(parity * ROWS, ROWS), ROWS)
    other_rows = pl.ds(pl.multiple_of((1 - parity) * ROWS, ROWS), ROWS)
    moved = jnp.logical_and(far_middle, is_odd)

    @pl.when(moved)
    def _():
        query_out[own_rows, :] = theirs[ROWS : 2 * ROWS, :]

    @pl.when(jnp.logical_not(moved))
    def _():
        query_out[own_rows, :] = mine[0]

    @pl.when(middle_even)
    def _():
        query_out[other_rows, :] = mine[1]

    @pl.when(jnp.logical_not(middle_even))
    def _():
        query_out[other_rows, :] = theirs[:ROWS, :]

    f32 = jnp.float32
    for out, first in ((key_out, 0), (value_out, KV)):
        columns = slice(first, first + KV)
        cross = back_b[:, columns].astype(f32) + back_c[:, columns].astype(f32)
        low = own[:ROWS, columns] + theirs[2 * ROWS :, columns].astype(f32)
        low = low + lent[:, columns].astype(f32) + jnp.where(is_odd, cross, 0.0)
        high = own[ROWS:, columns] + theirs[2 * ROWS :, 2 * KV + first : 3 * KV + first].astype(f32)
        out[:ROWS, :] = low.astype(out.dtype)
        out[ROWS:, :] = (high + jnp.where(is_odd, 0.0, cross)).astype(out.dtype)


def vmem(count):
    return [pl.BlockSpec(memory_space=pltpu.VMEM)] * count


def in_hbm(array):
    return pltpu.with_memory_space_constraint(array, pltpu.HBM)


def hbm(count):
    return [pl.BlockSpec(memory_space=pltpu.HBM)] * count


def smem(count):
    return [pl.BlockSpec(memory_space=pltpu.SMEM)] * count


def shards(
    queries,
    key_rows_slotted,
    value_rows_slotted,
    output_gradient,
    slot_to_block,
    doc_starts,
    block_live,
):
    me = lax.axis_index("ctx")
    place = me.astype(jnp.int32).reshape(1)
    live = block_live.T
    params = pltpu.CompilerParams(vmem_limit_bytes=VMEM_LIMIT)

    bf16 = functools.partial(jax.ShapeDtypeStruct, dtype=jnp.bfloat16)
    kv, kv_chain, kv_cross, q_own, g_own, row_start, fold = pl.pallas_call(
        pack_kernel,
        out_shape=(
            bf16((2 * ROWS, 2 * KV)),
            bf16((ROWS, 2 * KV)),
            bf16((ROWS, 2 * KV)),
            bf16((2 * ROWS, WIDE)),
            bf16((2 * ROWS, WIDE)),
            jax.ShapeDtypeStruct((4, GROUP * ROWS), jnp.int32),
            jax.ShapeDtypeStruct((ROWS, 2 * KV), jnp.float32),
        ),
        in_specs=smem(1) + hbm(6),
        out_specs=tuple(vmem(7)),
        scratch_shapes=[
            pltpu.SMEM(slot_to_block.shape, jnp.int32),
            pltpu.SMEM(doc_starts.shape, jnp.int32),
            pltpu.SemaphoreType.DMA((10,)),
        ],
        compiler_params=params,
        name="prepare",
    )(
        place,
        in_hbm(slot_to_block),
        in_hbm(doc_starts),
        in_hbm(key_rows_slotted),
        in_hbm(value_rows_slotted),
        in_hbm(queries),
        in_hbm(output_gradient),
    )
    kv_a = send(kv_chain, 2, -2)
    kv_b = send(kv_cross, -1, 1)
    kv_sib = send(kv, 1, -1)
    q_sib = send(queries, 1, -1)
    g_sib = send(output_gradient, 1, -1)
    passed = jnp.where(fold == 1, kv[:ROWS], jnp.where(fold == 2, kv_sib[:ROWS], kv_b))
    kv_c = send(passed, 2, -2)

    work = [
        pltpu.VMEM((2, ROWS, WIDE), jnp.bfloat16),
        pltpu.VMEM((ENTRIES * ROWS, 2 * KV), jnp.bfloat16),
        pltpu.VMEM((2, ROWS, WIDE), jnp.bfloat16),
        pltpu.VMEM((2, ROWS, WIDE), jnp.bfloat16),
        pltpu.VMEM((SPAN, GROUP * ROWS), jnp.float32),
    ]
    sums = jax.ShapeDtypeStruct((ENTRIES * ROWS, 2 * KV), jnp.float32)
    operands = (
        place,
        in_hbm(slot_to_block),
        live,
        row_start,
        q_own,
        q_sib,
        g_own,
        g_sib,
        kv,
        kv_sib,
        kv_a,
        kv_b,
    )
    dq_leading, total = pl.pallas_call(
        functools.partial(attention_kernel, True),
        out_shape=(bf16((2, ROWS, WIDE)), sums),
        in_specs=smem(3) + vmem(9),
        out_specs=tuple(vmem(2)),
        scratch_shapes=work[1:],
        compiler_params=params,
        cost_estimate=pl.CostEstimate(
            flops=1 << 36, bytes_accessed=1 << 22, transcendentals=1 << 18
        ),
        name="attention_leading",
    )(*operands)
    wide = jax.ShapeDtypeStruct((2 * ROWS, 2 * KV), jnp.float32)
    dq_own, own, out_sib, out_a, out_b, out_c = pl.pallas_call(
        functools.partial(attention_kernel, False),
        out_shape=(
            bf16((2, ROWS, WIDE)),
            wide,
            bf16((3 * ROWS, WIDE)),
            bf16((2 * ROWS, 2 * KV)),
            bf16((ROWS, 2 * KV)),
            bf16((ROWS, 2 * KV)),
        ),
        in_specs=smem(3) + vmem(12),
        out_specs=tuple(vmem(6)),
        scratch_shapes=work[:1] + [pltpu.VMEM(sums.shape, jnp.float32)] + work[1:],
        compiler_params=params,
        name="attention_last",
    )(*operands, kv_c, dq_leading, total)

    back_a = send(out_a, -2, 2)
    back_c = send(out_c, -3, 3)
    back_b = send(out_b, -1, 1)
    back_sib = send(out_sib, 1, -1)
    lent = send(jnp.where(fold == 2, back_a[ROWS:], 0), None, -1)

    own = pl.pallas_call(
        near_kernel,
        out_shape=wide,
        in_specs=smem(2) + vmem(2),
        out_specs=vmem(1)[0],
        compiler_params=params,
        cost_estimate=pl.CostEstimate(
            flops=NEAR_COST, bytes_accessed=1 << 20, transcendentals=0
        ),
        name="two_away_sum",
    )(place, in_hbm(slot_to_block), own, back_a)

    query_grad, key_gradient, value_gradient = pl.pallas_call(
        final_kernel,
        out_shape=(bf16((2 * ROWS, WIDE)), bf16((2 * ROWS, KV)), bf16((2 * ROWS, KV))),
        in_specs=smem(3) + vmem(6),
        out_specs=tuple(vmem(3)),
        scratch_shapes=[],
        compiler_params=params,
        name="gradients_out",
    )(
        place,
        in_hbm(slot_to_block),
        live,
        dq_own,
        own,
        lent,
        back_b,
        back_c,
        back_sib,
    )
    return query_grad, key_gradient, value_gradient


def solution(mesh):
    rows = P(("section", "ctx"), None)
    return jax.shard_map(
        shards,
        mesh=mesh,
        in_specs=(rows, rows, rows, rows, P("section"), P("section"), P("section", None)),
        out_specs=(rows, rows, rows),
        check_vma=False,
    )
```

```python
import functools
import math

import jax
import jax.numpy as jnp
from jax import lax
from jax.experimental import pallas as pl
from jax.experimental.pallas import tpu as pltpu
from jax.sharding import PartitionSpec as P

QUERY_HEADS = 16
KEY_VALUE_HEADS = 4
GROUP = QUERY_HEADS // KEY_VALUE_HEADS
HEAD_WIDTH = 128
ROWS = 64
KV = KEY_VALUE_HEADS * HEAD_WIDTH
WIDE = QUERY_HEADS * HEAD_WIDTH
REACH = 3
SPAN = (REACH + 1) * ROWS
SCALE = 1.0 / math.sqrt(HEAD_WIDTH)
EXP2_SCALE = SCALE * math.log2(math.e)
MASKED = -1e30
FAR = 1 << 30
ENTRIES = 7
VMEM_LIMIT = 24 * 1024 * 1024

TABLE_A, TABLE_B, TABLE_C = 4, 5, 6
NEAR_COST = 1 << 34


def send(array, even_by, odd_by):
    count = lax.axis_size("ctx")
    steps = [odd_by if i % 2 else even_by for i in range(count)]
    pairs = [(i, (i + by) % count) for i, by in enumerate(steps) if by is not None]
    return lax.ppermute(array, "ctx", pairs)


def fold_flags(chip_base, slots, live):
    half = slots.shape[0] // 2
    middle_even = slots[chip_base] == half - 1
    middle_odd = slots[chip_base + 2] == half - 1
    far_middle = jnp.logical_and(middle_odd, live[REACH, half] == 1)
    return middle_even, far_middle


def attention_kernel(
    leading,
    place,
    slots,
    live,
    row_start,
    q_own,
    q_sib,
    g_own,
    g_sib,
    kv_own,
    kv_sib,
    kv_a,
    kv_b,
    *refs,
):
    if leading:
        dq, total, table, q_work, g_work, bias = refs
    else:
        kv_c, dq_in, total_in = refs[:3]
        dq_own, out_own, out_sib, out_a, out_b, out_c = refs[3:9]
        dq, total, table, q_work, g_work, bias = refs[9:]
    me = place[0]
    count = slots.shape[0] // 2
    parity = lax.rem(me, 2)
    is_odd = parity == 1
    chip_base = 2 * (me - parity)
    middle_even, far_middle = fold_flags(chip_base, slots, live)

    own_at = pl.multiple_of(parity * 128, 128)
    sib_at = pl.multiple_of((1 - parity) * 128, 128)
    table[pl.ds(own_at, 128), :] = kv_own[...]
    table[pl.ds(sib_at, 128), :] = kv_sib[...]
    table[TABLE_A * ROWS : TABLE_B * ROWS, :] = kv_a[...]
    table[TABLE_B * ROWS : TABLE_C * ROWS, :] = kv_b[...]

    toward = jnp.where(is_odd, 1, -1)
    near_a = lax.rem(me + 2 * toward + count, count)
    near_b = lax.rem(me + toward + count, count)
    far = lax.rem(me + 3 * toward + count, count)
    passed_odd = jnp.logical_and(is_odd, slots[2 * near_a] == count - 1)
    passed_even = jnp.logical_and(is_odd, slots[2 * near_b] == count - 1)
    entry_ids = [slots[chip_base + e] for e in range(4)]
    entry_ids += [slots[2 * near_a + parity], slots[2 * near_b + parity]]
    if not leading:
        table[TABLE_C * ROWS :, :] = kv_c[...]
        passed_middle = jnp.logical_or(passed_odd, passed_even)
        entry_ids += [jnp.where(passed_middle, count - 1, slots[2 * far + parity])]

    own_row = pl.multiple_of(parity * ROWS, ROWS)
    other_row = pl.multiple_of((1 - parity) * ROWS, ROWS)
    other_entry = jnp.where(middle_even, 1 + parity, jnp.where(is_odd, 1, 2))
    slot = 0 if leading else 1

    @pl.when(middle_even)
    def _():
        q_work[slot] = q_own[pl.ds(other_row, ROWS), :]
        g_work[slot] = g_own[pl.ds(other_row, ROWS), :]

    @pl.when(jnp.logical_not(middle_even))
    def _():
        q_work[slot] = q_sib[pl.ds(own_row, ROWS), :]
        g_work[slot] = g_sib[pl.ds(own_row, ROWS), :]

    if leading:
        total[...] = jnp.zeros_like(total)

        @pl.when(far_middle)
        def _():
            q_work[1] = q_sib[ROWS:, :]
            g_work[1] = g_sib[ROWS:, :]

        entries = (other_entry, 3)
        first = jnp.where(passed_even, 1, 0)
        last = jnp.where(jnp.logical_and(far_middle, jnp.logical_not(is_odd)), 2, 1)
    else:
        total[...] = total_in[...]
        q_work[0] = q_own[pl.ds(own_row, ROWS), :]
        g_work[0] = g_own[pl.ds(own_row, ROWS), :]
        entries = (3 * parity, other_entry)
        first = jnp.where(jnp.logical_and(far_middle, is_odd), 1, 0)
        last = jnp.where(passed_even, 2, 1)

    def work_item(item, carry):
        entry = jnp.where(item == 0, *entries)
        query_id = slots[chip_base + entry]
        indices = []
        key_base = []
        for distance in range(REACH + 1):
            key_id = query_id - distance
            is_live = jnp.logical_and(key_id >= 0, live[distance, query_id] == 1)
            index = jnp.int32(0)
            found = jnp.bool_(False)
            for e in range(len(entry_ids)):
                match = entry_ids[e] == key_id
                index = jnp.where(match, e, index)
                found = jnp.logical_or(found, match)
            ok = jnp.logical_and(is_live, found)
            indices.append(pl.multiple_of(jnp.where(ok, index, 0) * ROWS, ROWS))
            key_base.append(jnp.where(ok, key_id * ROWS, FAR))
        lane = lax.broadcasted_iota(jnp.int32, (1, GROUP * ROWS), 1)
        query_pos = query_id * ROWS + lax.rem(lane, ROWS)
        query_start = row_start[pl.ds(entry, 1), :]
        sub = lax.broadcasted_iota(jnp.int32, (ROWS, GROUP * ROWS), 0)
        for distance in range(REACH + 1):
            key_pos = sub + key_base[distance]
            allowed = jnp.logical_and(key_pos <= query_pos, key_pos >= query_start)
            bias[distance * ROWS : (distance + 1) * ROWS, :] = jnp.where(
                allowed, 0.0, MASKED
            )
        for g in range(KEY_VALUE_HEADS):
            kcols = slice(g * HEAD_WIDTH, (g + 1) * HEAD_WIDTH)
            vcols = slice(KV + g * HEAD_WIDTH, KV + (g + 1) * HEAD_WIDTH)
            heads = [
                slice((GROUP * g + j) * HEAD_WIDTH, (GROUP * g + j + 1) * HEAD_WIDTH)
                for j in range(GROUP)
            ]
            keys = jnp.concatenate([table[pl.ds(i, ROWS), kcols] for i in indices], 0)
            values = jnp.concatenate([table[pl.ds(i, ROWS), vcols] for i in indices], 0)
            q = jnp.concatenate([q_work[item, :, h] for h in heads], 0)
            grad = jnp.concatenate([g_work[item, :, h] for h in heads], 0)
            nt = (((1,), (1,)), ((), ()))
            raw = lax.dot_general(keys, q, nt, preferred_element_type=jnp.float32)
            raw = raw + bias[...]
            top = jnp.max(raw, axis=0, keepdims=True)
            weights = jnp.exp2((raw - top) * EXP2_SCALE)
            probs = weights * (1.0 / jnp.sum(weights, axis=0, keepdims=True))
            grad_scores = lax.dot_general(
                values, grad, nt, preferred_element_type=jnp.float32
            )
            offset = jnp.sum(probs * grad_scores, axis=0, keepdims=True)
            score_low = (probs * (grad_scores - offset)).astype(jnp.bfloat16)
            value_add = jnp.dot(
                probs.astype(jnp.bfloat16), grad, preferred_element_type=jnp.float32
            )
            key_add = jnp.dot(score_low, q, preferred_element_type=jnp.float32)
            query_add = lax.dot_general(
                score_low,
                keys,
                (((0,), (0,)), ((), ())),
                preferred_element_type=jnp.float32,
            )
            query_add = (query_add * SCALE).astype(jnp.bfloat16)
            for j, h in enumerate(heads):
                dq[item, :, h] = query_add[j * ROWS : (j + 1) * ROWS]
            for distance in range(REACH + 1):
                part = slice(distance * ROWS, (distance + 1) * ROWS)
                at = pl.ds(indices[distance], ROWS)
                total[at, kcols] += key_add[part] * SCALE
                total[at, vcols] += value_add[part]
        return carry

    lax.fori_loop(first, last, work_item, 0)
    if leading:
        return
    low = jnp.bfloat16
    dq_own[0] = dq[0]
    dq_own[1] = dq_in[0]

    @pl.when(passed_even)
    def _():
        dq_own[1] = dq[1]

    out_sib[:ROWS, :] = dq_own[1]
    out_sib[ROWS : 2 * ROWS, :] = dq_in[1]
    out_sib[2 * ROWS :, : 2 * KV] = total[pl.ds(sib_at, ROWS), :].astype(low)
    out_sib[2 * ROWS :, 2 * KV :] = total[pl.ds(sib_at + ROWS, ROWS), :].astype(low)
    out_own[...] = total[pl.ds(own_at, 128), :]
    out_a[:ROWS, :] = total[TABLE_A * ROWS : TABLE_B * ROWS, :].astype(low)
    out_b[...] = total[TABLE_B * ROWS : TABLE_C * ROWS, :].astype(low)
    passed = total[TABLE_C * ROWS :, :].astype(low)
    out_a[ROWS:, :] = jnp.zeros_like(passed)
    out_c[...] = passed

    @pl.when(passed_middle)
    def _():
        out_a[ROWS:, :] = passed
        out_c[...] = jnp.zeros_like(passed)


def pack_kernel(
    place,
    slots_hbm,
    docs_hbm,
    keys,
    values,
    queries,
    grads,
    both,
    chain,
    cross,
    q_own,
    g_own,
    row_start,
    fold,
    slots,
    docs,
    sems,
):
    parity = lax.rem(place[0], 2)
    own_rows = pl.ds(pl.multiple_of(parity * ROWS, ROWS), ROWS)
    other_rows = pl.ds(pl.multiple_of((1 - parity) * ROWS, ROWS), ROWS)
    copies = [
        pltpu.make_async_copy(source, target, sems.at[n])
        for n, (source, target) in enumerate(
            [
                (slots_hbm, slots),
                (docs_hbm, docs),
                (keys.at[other_rows, :], cross.at[:, pl.ds(0, KV)]),
                (values.at[other_rows, :], cross.at[:, pl.ds(KV, KV)]),
                (keys.at[own_rows, :], chain.at[:, pl.ds(0, KV)]),
                (values.at[own_rows, :], chain.at[:, pl.ds(KV, KV)]),
                (keys, both.at[:, pl.ds(0, KV)]),
                (values, both.at[:, pl.ds(KV, KV)]),
                (queries, q_own),
                (grads, g_own),
            ]
        )
    ]
    for copy in copies:
        copy.start()
    copies[0].wait()
    copies[1].wait()
    middle = slots.shape[0] // 2 - 1
    chip_base = 2 * (place[0] - parity)
    holder = jnp.where(
        slots[chip_base + 2] == middle, 1, jnp.where(slots[chip_base] == middle, 2, 0)
    )
    fold[...] = jnp.full(fold.shape, jnp.where(parity == 1, holder, 0).astype(jnp.float32))
    count = docs.shape[0]
    lane = lax.rem(lax.broadcasted_iota(jnp.int32, (1, GROUP * ROWS), 1), ROWS)
    for entry in range(4):
        first = slots[chip_base + entry] * ROWS

        def halve(_, bounds):
            low, high = bounds
            middle = (low + high) // 2
            begun = docs[middle] <= first
            inside = low < high
            return (
                jnp.where(jnp.logical_and(inside, begun), middle + 1, low),
                jnp.where(jnp.logical_and(inside, jnp.logical_not(begun)), middle, high),
            )

        begun, _ = lax.fori_loop(
            0, count.bit_length(), halve, (jnp.int32(1), jnp.int32(count))
        )

        def more(state):
            index, _ = state
            start = docs[jnp.minimum(index, count - 1)]
            return jnp.logical_and(index < count, start < first + ROWS)

        def step(state):
            index, row = state
            start = docs[index]
            return index + 1, jnp.where(lane + first >= start, start, row)

        _, row = lax.while_loop(
            more, step, (begun, jnp.full((1, GROUP * ROWS), docs[begun - 1]))
        )
        row_start[pl.ds(entry, 1), :] = row
    for copy in copies[2:]:
        copy.wait()


def far_kernel(place, own, back_c, out):
    parity = lax.rem(place[0], 2)
    out[...] = own[...]
    out[pl.ds(pl.multiple_of((1 - parity) * ROWS, ROWS), ROWS), :] += back_c[...].astype(
        jnp.float32
    )


def final_kernel(place, slots, live, mine, own, lent, back_b, back_a, theirs, *outs):
    query_out, key_out, value_out = outs
    me = place[0]
    parity = lax.rem(me, 2)
    is_odd = parity == 1
    chip_base = 2 * (me - parity)
    middle_even, far_middle = fold_flags(chip_base, slots, live)
    own_rows = pl.ds(pl.multiple_of(parity * ROWS, ROWS), ROWS)
    other_rows = pl.ds(pl.multiple_of((1 - parity) * ROWS, ROWS), ROWS)
    moved = jnp.logical_and(far_middle, is_odd)

    @pl.when(moved)
    def _():
        query_out[own_rows, :] = theirs[ROWS : 2 * ROWS, :]

    @pl.when(jnp.logical_not(moved))
    def _():
        query_out[own_rows, :] = mine[0]

    @pl.when(middle_even)
    def _():
        query_out[other_rows, :] = mine[1]

    @pl.when(jnp.logical_not(middle_even))
    def _():
        query_out[other_rows, :] = theirs[:ROWS, :]

    keeps = jnp.logical_and(is_odd, slots[chip_base + 2] == slots.shape[0] // 2 - 1)
    kept = jnp.where(keeps, 1.0, 0.0)
    f32 = jnp.float32
    for out, first in ((key_out, 0), (value_out, KV)):
        columns = slice(first, first + KV)
        chain = back_a[:ROWS, columns].astype(f32)
        cross = back_b[:, columns].astype(f32)
        low = own[:ROWS, columns] + theirs[2 * ROWS :, columns].astype(f32)
        low = low + lent[:, columns].astype(f32) + kept * back_a[ROWS:, columns].astype(f32)
        high = own[ROWS:, columns] + theirs[2 * ROWS :, 2 * KV + first : 3 * KV + first].astype(f32)
        out[:ROWS, :] = (low + jnp.where(is_odd, cross, chain)).astype(out.dtype)
        out[ROWS:, :] = (high + jnp.where(is_odd, chain, cross)).astype(out.dtype)


def vmem(count):
    return [pl.BlockSpec(memory_space=pltpu.VMEM)] * count


def in_hbm(array):
    return pltpu.with_memory_space_constraint(array, pltpu.HBM)


def hbm(count):
    return [pl.BlockSpec(memory_space=pltpu.HBM)] * count


def smem(count):
    return [pl.BlockSpec(memory_space=pltpu.SMEM)] * count


def shards(
    queries,
    key_rows_slotted,
    value_rows_slotted,
    output_gradient,
    slot_to_block,
    doc_starts,
    block_live,
):
    me = lax.axis_index("ctx")
    place = me.astype(jnp.int32).reshape(1)
    live = block_live.T
    params = pltpu.CompilerParams(vmem_limit_bytes=VMEM_LIMIT)

    bf16 = functools.partial(jax.ShapeDtypeStruct, dtype=jnp.bfloat16)
    kv, kv_chain, kv_cross, q_own, g_own, row_start, fold = pl.pallas_call(
        pack_kernel,
        out_shape=(
            bf16((2 * ROWS, 2 * KV)),
            bf16((ROWS, 2 * KV)),
            bf16((ROWS, 2 * KV)),
            bf16((2 * ROWS, WIDE)),
            bf16((2 * ROWS, WIDE)),
            jax.ShapeDtypeStruct((4, GROUP * ROWS), jnp.int32),
            jax.ShapeDtypeStruct((ROWS, 2 * KV), jnp.float32),
        ),
        in_specs=smem(1) + hbm(6),
        out_specs=tuple(vmem(7)),
        scratch_shapes=[
            pltpu.SMEM(slot_to_block.shape, jnp.int32),
            pltpu.SMEM(doc_starts.shape, jnp.int32),
            pltpu.SemaphoreType.DMA((10,)),
        ],
        compiler_params=params,
        name="prepare",
    )(
        place,
        in_hbm(slot_to_block),
        in_hbm(doc_starts),
        in_hbm(key_rows_slotted),
        in_hbm(value_rows_slotted),
        in_hbm(queries),
        in_hbm(output_gradient),
    )
    kv_a = send(kv_chain, 2, -2)
    kv_b = send(kv_cross, -1, 1)
    kv_sib = send(kv, 1, -1)
    q_sib = send(queries, 1, -1)
    g_sib = send(output_gradient, 1, -1)
    passed = jnp.where(fold == 1, kv[:ROWS], jnp.where(fold == 2, kv_sib[:ROWS], kv_b))
    kv_c = send(passed, 2, -2)

    work = [
        pltpu.VMEM((2, ROWS, WIDE), jnp.bfloat16),
        pltpu.VMEM((ENTRIES * ROWS, 2 * KV), jnp.bfloat16),
        pltpu.VMEM((2, ROWS, WIDE), jnp.bfloat16),
        pltpu.VMEM((2, ROWS, WIDE), jnp.bfloat16),
        pltpu.VMEM((SPAN, GROUP * ROWS), jnp.float32),
    ]
    sums = jax.ShapeDtypeStruct((ENTRIES * ROWS, 2 * KV), jnp.float32)
    operands = (
        place,
        in_hbm(slot_to_block),
        live,
        row_start,
        q_own,
        q_sib,
        g_own,
        g_sib,
        kv,
        kv_sib,
        kv_a,
        kv_b,
    )
    dq_leading, total = pl.pallas_call(
        functools.partial(attention_kernel, True),
        out_shape=(bf16((2, ROWS, WIDE)), sums),
        in_specs=smem(3) + vmem(9),
        out_specs=tuple(vmem(2)),
        scratch_shapes=work[1:],
        compiler_params=params,
        cost_estimate=pl.CostEstimate(
            flops=1 << 36, bytes_accessed=1 << 22, transcendentals=1 << 18
        ),
        name="attention_leading",
    )(*operands)
    wide = jax.ShapeDtypeStruct((2 * ROWS, 2 * KV), jnp.float32)
    dq_own, own, out_sib, out_a, out_b, out_c = pl.pallas_call(
        functools.partial(attention_kernel, False),
        out_shape=(
            bf16((2, ROWS, WIDE)),
            wide,
            bf16((3 * ROWS, WIDE)),
            bf16((2 * ROWS, 2 * KV)),
            bf16((ROWS, 2 * KV)),
            bf16((ROWS, 2 * KV)),
        ),
        in_specs=smem(3) + vmem(12),
        out_specs=tuple(vmem(6)),
        scratch_shapes=work[:1] + [pltpu.VMEM(sums.shape, jnp.float32)] + work[1:],
        compiler_params=params,
        name="attention_last",
    )(*operands, kv_c, dq_leading, total)

    back_a = send(out_a, -2, 2)
    back_c = send(out_c, -3, 3)
    back_b = send(out_b, -1, 1)
    back_sib = send(out_sib, 1, -1)

    own = pl.pallas_call(
        far_kernel,
        out_shape=wide,
        in_specs=smem(1) + vmem(2),
        out_specs=vmem(1)[0],
        compiler_params=params,
        cost_estimate=pl.CostEstimate(
            flops=NEAR_COST, bytes_accessed=1 << 20, transcendentals=0
        ),
        name="three_away_sum",
    )(place, own, back_c)

    own, back_a = lax.optimization_barrier((own, back_a))
    lent = send(jnp.where(fold == 2, back_a[ROWS:], 0), None, -1)

    query_grad, key_gradient, value_gradient = pl.pallas_call(
        final_kernel,
        out_shape=(bf16((2 * ROWS, WIDE)), bf16((2 * ROWS, KV)), bf16((2 * ROWS, KV))),
        in_specs=smem(3) + vmem(6),
        out_specs=tuple(vmem(3)),
        scratch_shapes=[],
        compiler_params=params,
        name="gradients_out",
    )(
        place,
        in_hbm(slot_to_block),
        live,
        dq_own,
        own,
        lent,
        back_b,
        back_a,
        back_sib,
    )
    return query_grad, key_gradient, value_gradient


def solution(mesh):
    rows = P(("section", "ctx"), None)
    return jax.shard_map(
        shards,
        mesh=mesh,
        in_specs=(rows, rows, rows, rows, P("section"), P("section"), P("section", None)),
        out_specs=(rows, rows, rows),
        check_vma=False,
    )
```

```python
import functools
import math

import jax
import jax.numpy as jnp
from jax import lax
from jax.experimental import pallas as pl
from jax.experimental.pallas import tpu as pltpu
from jax.sharding import PartitionSpec as P

QUERY_HEADS = 16
KEY_VALUE_HEADS = 4
GROUP = QUERY_HEADS // KEY_VALUE_HEADS
HEAD_WIDTH = 128
ROWS = 64
KV = KEY_VALUE_HEADS * HEAD_WIDTH
WIDE = QUERY_HEADS * HEAD_WIDTH
REACH = 3
SPAN = (REACH + 1) * ROWS
SCALE = 1.0 / math.sqrt(HEAD_WIDTH)
EXP2_SCALE = SCALE * math.log2(math.e)
MASKED = -1e30
FAR = 1 << 30
ENTRIES = 7
VMEM_LIMIT = 24 * 1024 * 1024

ROWS_COST = 1 << 20
TABLE_A, TABLE_B, TABLE_C = 4, 5, 6


def send(array, even_by, odd_by):
    count = lax.axis_size("ctx")
    pairs = [(i, (i + (odd_by if i % 2 else even_by)) % count) for i in range(count)]
    return lax.ppermute(array, "ctx", pairs)


def fold_flags(chip_base, slots, live):
    half = slots.shape[0] // 2
    middle_even = slots[chip_base] == half - 1
    middle_odd = slots[chip_base + 2] == half - 1
    far_middle = jnp.logical_and(middle_odd, live[REACH, half] == 1)
    return middle_even, far_middle


def attention_kernel(
    leading,
    place,
    slots,
    live,
    row_start,
    q_own,
    q_sib,
    g_own,
    g_sib,
    kv_own,
    kv_sib,
    kv_a,
    kv_b,
    *refs,
):
    if leading:
        dq, total, table, q_work, g_work, bias = refs
    else:
        kv_c, dq_in, total_in, dq_first, dq_rest, out_own, out_sib, out_a, out_b, out_c = (
            refs[:10]
        )
        dq, total, table, q_work, g_work, bias = refs[10:]
    me = place[0]
    count = slots.shape[0] // 2
    parity = lax.rem(me, 2)
    is_odd = parity == 1
    chip_base = 2 * (me - parity)
    middle_even, far_middle = fold_flags(chip_base, slots, live)

    own_at = pl.multiple_of(parity * 128, 128)
    sib_at = pl.multiple_of((1 - parity) * 128, 128)
    table[pl.ds(own_at, 128), :] = kv_own[...]
    table[pl.ds(sib_at, 128), :] = kv_sib[...]
    table[TABLE_A * ROWS : TABLE_B * ROWS, :] = kv_a[...]
    table[TABLE_B * ROWS : TABLE_C * ROWS, :] = kv_b[...]

    toward = jnp.where(is_odd, 1, -1)
    near_a = lax.rem(me + 2 * toward + count, count)
    near_b = lax.rem(me + toward + count, count)
    far = lax.rem(me + 3 * toward + count, count)
    passed_odd = jnp.logical_and(is_odd, slots[2 * near_a] == count - 1)
    passed_even = jnp.logical_and(is_odd, slots[2 * near_b] == count - 1)
    entry_ids = [slots[chip_base + e] for e in range(4)]
    entry_ids += [slots[2 * near_a + parity], slots[2 * near_b + parity]]
    if not leading:
        table[TABLE_C * ROWS :, :] = kv_c[...]
        passed_middle = jnp.logical_or(passed_odd, passed_even)
        entry_ids += [jnp.where(passed_middle, count - 1, slots[2 * far + parity])]

    own_row = pl.multiple_of(parity * ROWS, ROWS)
    other_row = pl.multiple_of((1 - parity) * ROWS, ROWS)
    other_entry = jnp.where(middle_even, 1 + parity, jnp.where(is_odd, 1, 2))
    slot = 0 if leading else 1

    @pl.when(middle_even)
    def _():
        q_work[slot] = q_own[pl.ds(other_row, ROWS), :]
        g_work[slot] = g_own[pl.ds(other_row, ROWS), :]

    @pl.when(jnp.logical_not(middle_even))
    def _():
        q_work[slot] = q_sib[pl.ds(own_row, ROWS), :]
        g_work[slot] = g_sib[pl.ds(own_row, ROWS), :]

    if leading:
        total[...] = jnp.zeros_like(total)

        @pl.when(far_middle)
        def _():
            q_work[1] = q_sib[ROWS:, :]
            g_work[1] = g_sib[ROWS:, :]

        entries = (other_entry, 3)
        first = jnp.where(passed_even, 1, 0)
        last = jnp.where(jnp.logical_and(far_middle, jnp.logical_not(is_odd)), 2, 1)
    else:
        total[...] = total_in[...]
        q_work[0] = q_own[pl.ds(own_row, ROWS), :]
        g_work[0] = g_own[pl.ds(own_row, ROWS), :]
        entries = (3 * parity, other_entry)
        first = jnp.where(jnp.logical_and(far_middle, is_odd), 1, 0)
        last = jnp.where(passed_even, 2, 1)

    def work_item(item, carry):
        entry = jnp.where(item == 0, *entries)
        query_id = slots[chip_base + entry]
        indices = []
        key_base = []
        for distance in range(REACH + 1):
            key_id = query_id - distance
            is_live = jnp.logical_and(key_id >= 0, live[distance, query_id] == 1)
            index = jnp.int32(0)
            found = jnp.bool_(False)
            for e in range(len(entry_ids)):
                match = entry_ids[e] == key_id
                index = jnp.where(match, e, index)
                found = jnp.logical_or(found, match)
            ok = jnp.logical_and(is_live, found)
            indices.append(pl.multiple_of(jnp.where(ok, index, 0) * ROWS, ROWS))
            key_base.append(jnp.where(ok, key_id * ROWS, FAR))
        lane = lax.broadcasted_iota(jnp.int32, (1, GROUP * ROWS), 1)
        query_pos = query_id * ROWS + lax.rem(lane, ROWS)
        query_start = row_start[pl.ds(entry, 1), :]
        sub = lax.broadcasted_iota(jnp.int32, (ROWS, GROUP * ROWS), 0)
        for distance in range(REACH + 1):
            key_pos = sub + key_base[distance]
            allowed = jnp.logical_and(key_pos <= query_pos, key_pos >= query_start)
            bias[distance * ROWS : (distance + 1) * ROWS, :] = jnp.where(
                allowed, 0.0, MASKED
            )
        for g in range(KEY_VALUE_HEADS):
            kcols = slice(g * HEAD_WIDTH, (g + 1) * HEAD_WIDTH)
            vcols = slice(KV + g * HEAD_WIDTH, KV + (g + 1) * HEAD_WIDTH)
            heads = [
                slice((GROUP * g + j) * HEAD_WIDTH, (GROUP * g + j + 1) * HEAD_WIDTH)
                for j in range(GROUP)
            ]
            keys = jnp.concatenate([table[pl.ds(i, ROWS), kcols] for i in indices], 0)
            values = jnp.concatenate([table[pl.ds(i, ROWS), vcols] for i in indices], 0)
            q = jnp.concatenate([q_work[item, :, h] for h in heads], 0)
            grad = jnp.concatenate([g_work[item, :, h] for h in heads], 0)
            nt = (((1,), (1,)), ((), ()))
            raw = lax.dot_general(keys, q, nt, preferred_element_type=jnp.float32)
            raw = raw + bias[...]
            top = jnp.max(raw, axis=0, keepdims=True)
            weights = jnp.exp2((raw - top) * EXP2_SCALE)
            probs = weights * (1.0 / jnp.sum(weights, axis=0, keepdims=True))
            grad_scores = lax.dot_general(
                values, grad, nt, preferred_element_type=jnp.float32
            )
            offset = jnp.sum(probs * grad_scores, axis=0, keepdims=True)
            score_low = (probs * (grad_scores - offset)).astype(jnp.bfloat16)
            value_add = jnp.dot(
                probs.astype(jnp.bfloat16), grad, preferred_element_type=jnp.float32
            )
            key_add = jnp.dot(score_low, q, preferred_element_type=jnp.float32)
            query_add = lax.dot_general(
                score_low,
                keys,
                (((0,), (0,)), ((), ())),
                preferred_element_type=jnp.float32,
            )
            query_add = (query_add * SCALE).astype(jnp.bfloat16)
            for j, h in enumerate(heads):
                dq[item, :, h] = query_add[j * ROWS : (j + 1) * ROWS]
            for distance in range(REACH + 1):
                part = slice(distance * ROWS, (distance + 1) * ROWS)
                at = pl.ds(indices[distance], ROWS)
                total[at, kcols] += key_add[part] * SCALE
                total[at, vcols] += value_add[part]
        return carry

    lax.fori_loop(first, last, work_item, 0)
    if leading:
        return
    low = jnp.bfloat16
    dq_first[...] = dq[0]
    dq_rest[...] = dq_in[...]

    @pl.when(passed_even)
    def _():
        dq_rest[0] = dq[1]

    out_own[...] = total[pl.ds(own_at, 128), :]
    out_sib[...] = total[pl.ds(sib_at, 128), :]
    out_a[...] = total[TABLE_A * ROWS : TABLE_B * ROWS, :].astype(low)
    out_b[...] = total[TABLE_B * ROWS : TABLE_C * ROWS, :]
    out_c[...] = total[TABLE_C * ROWS :, :].astype(low)


def pack_kernel(
    place,
    slots_hbm,
    docs_hbm,
    keys,
    values,
    queries,
    grads,
    both,
    chain,
    cross,
    q_own,
    g_own,
    row_start,
    fold,
    slots,
    docs,
    sems,
):
    parity = lax.rem(place[0], 2)
    own_rows = pl.ds(pl.multiple_of(parity * ROWS, ROWS), ROWS)
    other_rows = pl.ds(pl.multiple_of((1 - parity) * ROWS, ROWS), ROWS)
    copies = [
        pltpu.make_async_copy(source, target, sems.at[n])
        for n, (source, target) in enumerate(
            [
                (slots_hbm, slots),
                (docs_hbm, docs),
                (keys.at[other_rows, :], cross.at[:, pl.ds(0, KV)]),
                (values.at[other_rows, :], cross.at[:, pl.ds(KV, KV)]),
                (keys.at[own_rows, :], chain.at[:, pl.ds(0, KV)]),
                (values.at[own_rows, :], chain.at[:, pl.ds(KV, KV)]),
                (keys, both.at[:, pl.ds(0, KV)]),
                (values, both.at[:, pl.ds(KV, KV)]),
                (queries, q_own),
                (grads, g_own),
            ]
        )
    ]
    for copy in copies:
        copy.start()
    copies[0].wait()
    copies[1].wait()
    middle = slots.shape[0] // 2 - 1
    chip_base = 2 * (place[0] - parity)
    holder = jnp.where(
        slots[chip_base + 2] == middle, 1, jnp.where(slots[chip_base] == middle, 2, 0)
    )
    fold[...] = jnp.full(fold.shape, jnp.where(parity == 1, holder, 0))
    count = docs.shape[0]
    lane = lax.rem(lax.broadcasted_iota(jnp.int32, (1, GROUP * ROWS), 1), ROWS)
    for entry in range(4):
        first = slots[chip_base + entry] * ROWS

        def halve(_, bounds):
            low, high = bounds
            middle = (low + high) // 2
            begun = docs[middle] <= first
            inside = low < high
            return (
                jnp.where(jnp.logical_and(inside, begun), middle + 1, low),
                jnp.where(jnp.logical_and(inside, jnp.logical_not(begun)), middle, high),
            )

        begun, _ = lax.fori_loop(
            0, count.bit_length(), halve, (jnp.int32(1), jnp.int32(count))
        )

        def more(state):
            index, _ = state
            start = docs[jnp.minimum(index, count - 1)]
            return jnp.logical_and(index < count, start < first + ROWS)

        def step(state):
            index, row = state
            start = docs[index]
            return index + 1, jnp.where(lane + first >= start, start, row)

        _, row = lax.while_loop(
            more, step, (begun, jnp.full((1, GROUP * ROWS), docs[begun - 1]))
        )
        row_start[pl.ds(entry, 1), :] = row
    for copy in copies[2:]:
        copy.wait()


def early_kernel(place, slots, live, first, rest, theirs, out):
    me = place[0]
    parity = lax.rem(me, 2)
    is_odd = parity == 1
    chip_base = 2 * (me - parity)
    middle_even, far_middle = fold_flags(chip_base, slots, live)
    own_row = pl.multiple_of(parity * ROWS, ROWS)
    other_row = pl.multiple_of((1 - parity) * ROWS, ROWS)
    moved = jnp.logical_and(far_middle, is_odd)

    @pl.when(moved)
    def _():
        out[pl.ds(own_row, ROWS), :] = theirs[1]

    @pl.when(jnp.logical_not(moved))
    def _():
        out[pl.ds(own_row, ROWS), :] = first[...]

    @pl.when(middle_even)
    def _():
        out[pl.ds(other_row, ROWS), :] = rest[0]

    @pl.when(jnp.logical_not(middle_even))
    def _():
        out[pl.ds(other_row, ROWS), :] = theirs[0]


def near_kernel(place, slots, own, back_a, back_c, out):
    parity = lax.rem(place[0], 2)
    is_odd = parity == 1
    own_rows = pl.ds(pl.multiple_of(parity * ROWS, ROWS), ROWS)
    out[...] = own[...]
    out[own_rows, :] += back_a[...].astype(jnp.float32)
    holder = slots[2 * (place[0] - parity) + 2] == slots.shape[0] // 2 - 1

    @pl.when(jnp.logical_and(is_odd, holder))
    def _():
        out[:ROWS, :] += back_c[...].astype(jnp.float32)


def sum_kernel(place, own, sib, back_b, key_out, value_out):
    parity = lax.rem(place[0], 2)
    own_rows = pl.ds(pl.multiple_of(parity * ROWS, ROWS), ROWS)
    other_rows = pl.ds(pl.multiple_of((1 - parity) * ROWS, ROWS), ROWS)
    for out, columns in ((key_out, slice(0, KV)), (value_out, slice(KV, 2 * KV))):
        both = own[:, columns] + sib[:, columns].astype(jnp.float32)
        out[...] = both.astype(jnp.bfloat16)
        out[other_rows, :] = (
            own[other_rows, columns]
            + sib[other_rows, columns].astype(jnp.float32)
            + back_b[:, columns].astype(jnp.float32)
        ).astype(jnp.bfloat16)


def vmem(count):
    return [pl.BlockSpec(memory_space=pltpu.VMEM)] * count


def in_hbm(array):
    return pltpu.with_memory_space_constraint(array, pltpu.HBM)


def hbm(count):
    return [pl.BlockSpec(memory_space=pltpu.HBM)] * count


def smem(count):
    return [pl.BlockSpec(memory_space=pltpu.SMEM)] * count


def shards(
    queries,
    key_rows_slotted,
    value_rows_slotted,
    output_gradient,
    slot_to_block,
    doc_starts,
    block_live,
):
    me = lax.axis_index("ctx")
    place = me.astype(jnp.int32).reshape(1)
    live = block_live.T
    params = pltpu.CompilerParams(vmem_limit_bytes=VMEM_LIMIT)

    bf16 = functools.partial(jax.ShapeDtypeStruct, dtype=jnp.bfloat16)
    kv, kv_chain, kv_cross, q_own, g_own, row_start, fold = pl.pallas_call(
        pack_kernel,
        out_shape=(
            bf16((2 * ROWS, 2 * KV)),
            bf16((ROWS, 2 * KV)),
            bf16((ROWS, 2 * KV)),
            bf16((2 * ROWS, WIDE)),
            bf16((2 * ROWS, WIDE)),
            jax.ShapeDtypeStruct((4, GROUP * ROWS), jnp.int32),
            jax.ShapeDtypeStruct((8, 128), jnp.int32),
        ),
        in_specs=smem(1) + hbm(6),
        out_specs=tuple(vmem(7)),
        scratch_shapes=[
            pltpu.SMEM(slot_to_block.shape, jnp.int32),
            pltpu.SMEM(doc_starts.shape, jnp.int32),
            pltpu.SemaphoreType.DMA((10,)),
        ],
        compiler_params=params,
        name="prepare",
    )(
        place,
        in_hbm(slot_to_block),
        in_hbm(doc_starts),
        in_hbm(key_rows_slotted),
        in_hbm(value_rows_slotted),
        in_hbm(queries),
        in_hbm(output_gradient),
    )
    kv_a = send(kv_chain, 2, -2)
    kv_b = send(kv_cross, -1, 1)
    kv_sib = send(kv, 1, -1)
    q_sib = send(queries, 1, -1)
    g_sib = send(output_gradient, 1, -1)
    which = fold[:1, :1]
    passed = jnp.where(which == 1, kv[:ROWS], jnp.where(which == 2, kv_sib[:ROWS], kv_b))
    kv_c = send(passed, 2, -2)

    work = [
        pltpu.VMEM((2, ROWS, WIDE), jnp.bfloat16),
        pltpu.VMEM((ENTRIES * ROWS, 2 * KV), jnp.bfloat16),
        pltpu.VMEM((2, ROWS, WIDE), jnp.bfloat16),
        pltpu.VMEM((2, ROWS, WIDE), jnp.bfloat16),
        pltpu.VMEM((SPAN, GROUP * ROWS), jnp.float32),
    ]
    sums = jax.ShapeDtypeStruct((ENTRIES * ROWS, 2 * KV), jnp.float32)
    operands = (
        place,
        in_hbm(slot_to_block),
        live,
        row_start,
        q_own,
        q_sib,
        g_own,
        g_sib,
        kv,
        kv_sib,
        kv_a,
        kv_b,
    )
    dq_leading, total = pl.pallas_call(
        functools.partial(attention_kernel, True),
        out_shape=(bf16((2, ROWS, WIDE)), sums),
        in_specs=smem(3) + vmem(9),
        out_specs=tuple(vmem(2)),
        scratch_shapes=work[1:],
        compiler_params=params,
        cost_estimate=pl.CostEstimate(
            flops=1 << 36, bytes_accessed=1 << 22, transcendentals=1 << 18
        ),
        name="attention_leading",
    )(*operands)
    dq_first, dq_rest, own, sib, out_a, out_b, out_c = pl.pallas_call(
        functools.partial(attention_kernel, False),
        out_shape=(
            bf16((ROWS, WIDE)),
            bf16((2, ROWS, WIDE)),
            jax.ShapeDtypeStruct((2 * ROWS, 2 * KV), jnp.float32),
            jax.ShapeDtypeStruct((2 * ROWS, 2 * KV), jnp.float32),
            bf16((ROWS, 2 * KV)),
            jax.ShapeDtypeStruct((ROWS, 2 * KV), jnp.float32),
            bf16((ROWS, 2 * KV)),
        ),
        in_specs=smem(3) + vmem(12),
        out_specs=tuple(vmem(7)),
        scratch_shapes=work[:1] + [pltpu.VMEM(sums.shape, jnp.float32)] + work[1:],
        compiler_params=params,
        name="attention_last",
    )(*operands, kv_c, dq_leading, total)

    back_c = send(out_c, -2, 2)
    back_a = send(out_a, -2, 2)
    passing = back_c.astype(jnp.float32)
    back_b = send((out_b + jnp.where(which == 0, passing, 0)).astype(jnp.bfloat16), -1, 1)
    middle_part = jnp.pad(jnp.where(which == 2, passing, 0), ((0, ROWS), (0, 0)))
    back_sib = send((sib + middle_part).astype(jnp.bfloat16), 1, -1)
    dq_sib = send(dq_rest, 1, -1)

    own = pl.pallas_call(
        near_kernel,
        out_shape=jax.ShapeDtypeStruct((2 * ROWS, 2 * KV), jnp.float32),
        in_specs=smem(2) + vmem(3),
        out_specs=vmem(1)[0],
        compiler_params=params,
        cost_estimate=pl.CostEstimate(
            flops=1 << 34, bytes_accessed=1 << 20, transcendentals=0
        ),
        name="two_away_sum",
    )(place, in_hbm(slot_to_block), own, back_a, back_c)
    own, dq_sib = lax.optimization_barrier((own, dq_sib))
    query_grad = pl.pallas_call(
        early_kernel,
        out_shape=bf16((2 * ROWS, WIDE)),
        in_specs=smem(3) + vmem(3),
        out_specs=vmem(1)[0],
        compiler_params=params,
        cost_estimate=pl.CostEstimate(
            flops=ROWS_COST, bytes_accessed=1 << 20, transcendentals=0
        ),
        name="query_gradient_rows",
    )(place, in_hbm(slot_to_block), live, dq_first, dq_rest, dq_sib)
    own, query_grad = lax.optimization_barrier((own, query_grad))

    key_gradient, value_gradient = pl.pallas_call(
        sum_kernel,
        out_shape=(bf16((2 * ROWS, KV)), bf16((2 * ROWS, KV))),
        in_specs=smem(1) + vmem(3),
        out_specs=tuple(vmem(2)),
        compiler_params=params,
        name="key_value_gradient_sum",
    )(place, own, back_sib, back_b)
    return query_grad, key_gradient, value_gradient


def solution(mesh):
    rows = P(("section", "ctx"), None)
    return jax.shard_map(
        shards,
        mesh=mesh,
        in_specs=(rows, rows, rows, rows, P("section"), P("section"), P("section", None)),
        out_specs=(rows, rows, rows),
        check_vma=False,
    )
```
